32 devices in a mesh: stn: 8 (over z, y), grid: 4 (over x, core).
Axes of the slice: x: 2, y: 2, z: 4, core: 2. Of those that a mesh axis runs over, the one named last changes fastest.
Arguments:
- voltages: bfloat16 [512, 2, 12288], P('stn', None, 'grid'), may hold values from -6 to 6
- pfb_coeffs: float32 [16, 48], replicated, may hold values from -1.5 to 1.5
- station_offsets: int32 [2, 512], replicated, may hold values from 0 to 4
- tile_cells: int32 [24, 2, 136], P('stn'), may hold values from 0 to 127, as said below
- kernel_table: float32 [8, 7], replicated, may hold values from 0.2 to 1
Outputs:
- uv_grid: float32 [128, 24, 256], P('grid', 'stn')
The draws below stay inside these ranges and needn't reach their ends.
Inputs may be any that keep to these rules, and one draw needn't show every extreme that they name: tile_cells[c, 0, k] lies in one of the strips of 32 rows; in every channel at most 68 baseline tiles have their base row in the same strip, and one strip holds exactly 68. A base row in the last strip and every base column are at most 112.
All inputs are finite; a program needn't handle non-finite values.
Results may differ from the reference program's by a relative error of at most 0.0065.
Values may be sent and summed in bfloat16 or wider, within the bound.
A program may use at most 128 MiB of HBM per device.

```python
import math
import jax
import jax.numpy as jnp
import numpy as np
from jax import lax

STATIONS = 512
POLS = 2
CHANNELS = 24
FRAME = 48
TAPS = 16
SPECTRA = 256
TILE = 32
NPAIR = 136
PATCH = 16
KERN = 7
OVER = 8
SPREAD = 5
UV = 128
N_GRID = 4


def draw_tile_cells(key, part):
    subkeys = jax.random.split(key, 5)
    strip_rows = UV // N_GRID
    hot_count = NPAIR // 2
    hot_strip = jax.random.randint(subkeys[0], (CHANNELS, 1), 0, N_GRID)
    scores = jax.random.randint(subkeys[1], (CHANNELS, NPAIR), 0, 1 << 20) * NPAIR + jnp.arange(NPAIR, dtype=jnp.int32)[None, :]
    pair_rank = jnp.argsort(jnp.argsort(scores, axis=1), axis=1)
    other_step = jax.random.randint(subkeys[2], (CHANNELS, NPAIR), 1, N_GRID)
    owner_strip = jnp.where(pair_rank < hot_count, hot_strip, (hot_strip + other_step) % N_GRID)
    within = jax.random.randint(subkeys[3], (CHANNELS, NPAIR), 0, strip_rows)
    within = jnp.where(owner_strip == N_GRID - 1, within % (strip_rows - PATCH + 1), within)
    base_rows = owner_strip * strip_rows + within
    base_cols = jax.random.randint(subkeys[4], (CHANNELS, NPAIR), 0, UV - PATCH + 1)
    return jnp.stack([base_rows, base_cols], axis=1).astype(jnp.int32)


def with_ends(drawn, key, least, high):
    shape = drawn.shape
    spot = [jax.random.randint(jax.random.fold_in(key, axis), (), 0, shape[axis]) for axis in range(len(shape))]
    drawn = drawn.at[tuple(spot)].set(least)
    longest = shape.index(max(shape))
    spot[longest] = (spot[longest] + 1) % shape[longest]
    return drawn.at[tuple(spot)].set(high)


def levels(rng, shape, shards, smallest, high):
    factor_of, own = 1.0, jax.random.fold_in(rng, 6)
    for dim, blocks in shards:
        steps = jnp.exp(jax.random.uniform(jax.random.fold_in(own, dim), (blocks,), jnp.float32, smallest / len(shards), high / len(shards)))
        factor_of = factor_of * jnp.repeat(steps, shape[dim] // blocks).reshape([-1 if axis == dim else 1 for axis in range(len(shape))])
    return factor_of


def normal_values(stream_key, extent, spread, limit, pieces=(), kind=jnp.bfloat16):
    level = levels(stream_key, extent, pieces, -0.22, 0.18) if pieces else 1.0
    drawn = jax.random.normal(stream_key, extent, jnp.float32) * spread * level
    return jnp.minimum(jnp.maximum(drawn, -limit), limit).astype(kind)


def setup_inputs(seed: int = 0) -> dict:
    keys = jax.random.split(jax.random.key(seed), 6)
    return {
        "voltages": normal_values(keys[0], (STATIONS, POLS, SPECTRA * FRAME), 1.0, 6.0, ((0, 8), (2, 4))),
        "pfb_coeffs": normal_values(keys[1], (TAPS, FRAME), TAPS ** -0.5, 1.5, (), jnp.float32),
        "station_offsets": with_ends(jax.random.randint(keys[2], (2, STATIONS), 0, SPREAD), jax.random.fold_in(keys[2], 1), 0, SPREAD - 1).astype(jnp.int32),
        "tile_cells": draw_tile_cells(jax.random.fold_in(keys[5], 71), 0),
        "kernel_table": jnp.clip(jax.random.uniform(keys[4], (OVER, KERN), jnp.float32, 0.2, 1.0), 0.2, 1.0),
    }


highest = lax.Precision.HIGHEST

def dft_table(frame_len):
    chan_count = frame_len // 2
    sample_line = jnp.arange(frame_len, dtype=jnp.int32)[:, None]
    chan_line = jnp.arange(chan_count, dtype=jnp.int32)[None, :]
    angles = (sample_line * chan_line % frame_len).astype(jnp.float32) * (2.0 * math.pi / frame_len)
    norm_factor = 1.0 / math.sqrt(frame_len)
    twiddle = jnp.stack([jnp.cos(angles) * norm_factor, -jnp.sin(angles) * norm_factor], axis=2)
    return twiddle.reshape(frame_len, 2 * chan_count).astype(jnp.bfloat16)

def filter_frames(frames, coeffs, spec_count):
    summed = jnp.zeros(frames.shape[:2] + (spec_count, frames.shape[3]), jnp.float32)
    for tap_index in range(coeffs.shape[0]):
        summed = summed + coeffs[tap_index] * frames[:, :, tap_index:tap_index + spec_count, :].astype(jnp.float32)
    return summed.astype(jnp.bfloat16)

def pair_tables(tile_count):
    pair_first, pair_second = np.triu_indices(tile_count)
    return (jnp.asarray(pair_first.astype(np.int32)), jnp.asarray(pair_second.astype(np.int32)))

def correlate(spectrum, norm_factor):
    real_part, imag_part = (spectrum[0], spectrum[1])
    stacked = jnp.concatenate([jnp.concatenate([real_part, imag_part], axis=1), jnp.concatenate([imag_part, -real_part], axis=1)], axis=0)
    partner = jnp.concatenate([real_part, imag_part], axis=1)
    product = lax.dot_general(stacked, partner, (((1,), (1,)), ((), ())), preferred_element_type=jnp.float32)
    stations = real_part.shape[0]
    return product.reshape(2, stations, stations) * norm_factor

def axis_weights(offsets, first_stn, second_stn, frequency, divisor, kernel_table):
    over_count = kernel_table.shape[0]
    separation = offsets[first_stn][:, :, None] - offsets[second_stn][:, None, :] + (SPREAD - 1)
    scaled = separation * frequency
    cell_index = scaled // divisor
    fine_index = scaled % divisor * over_count // divisor
    choose = (fine_index[..., None] == jnp.arange(over_count, dtype=jnp.int32)).astype(jnp.float32)
    tap_values = jnp.einsum('kpqo,ot->kpqt', choose, kernel_table, precision=highest)
    place_rel = jnp.arange(PATCH, dtype=jnp.int32) - cell_index[..., None]
    weights = jnp.zeros(place_rel.shape, jnp.float32)
    for tap_index in range(kernel_table.shape[1]):
        weights = weights + tap_values[..., tap_index:tap_index + 1] * (place_rel == tap_index).astype(jnp.float32)
    return weights.reshape(weights.shape[0], -1, PATCH)

def make_patches(vis_real, vis_imag, first_stn, second_stn, offsets, frequency, divisor, kernel_table):
    weight_u = axis_weights(offsets[0], first_stn, second_stn, frequency, divisor, kernel_table)
    weight_v = axis_weights(offsets[1], first_stn, second_stn, frequency, divisor, kernel_table)
    keep_mask = (first_stn[:, :, None] < second_stn[:, None, :]).astype(jnp.float32).reshape(first_stn.shape[0], -1)
    real_kept = vis_real.reshape(keep_mask.shape) * keep_mask
    imag_kept = vis_imag.reshape(keep_mask.shape) * keep_mask
    weighted = jnp.concatenate([weight_v * real_kept[..., None], weight_v * imag_kept[..., None]], axis=2)
    return jnp.einsum('kbr,kbs->krs', weight_u, weighted, precision=highest)

def place_patches(uv_plane, patches, base_rows, base_cols):
    patch_line = jnp.arange(PATCH, dtype=jnp.int32)
    row_index = base_rows[:, None] + patch_line[None, :]
    col_index = jnp.concatenate([base_cols[:, None] + patch_line[None, :], UV + base_cols[:, None] + patch_line[None, :]], axis=1)
    return uv_plane.at[row_index[:, :, None], col_index[:, None, :]].add(patches, mode='drop')

def grid_pairs(visibility, base_cells, frequency, offsets, kernel_table, divisor):
    stations = visibility.shape[1]
    tile_count = stations // TILE
    vis_tiles = visibility.reshape(2, tile_count, TILE, tile_count, TILE)
    pair_first, pair_second = pair_tables(tile_count)
    pair_block = tile_count + 1
    tile_line = jnp.arange(TILE, dtype=jnp.int32)

    def add_block(uv_plane, block_index):
        block_start = (block_index * pair_block).astype(jnp.int32)
        first_tile = lax.dynamic_slice_in_dim(pair_first, block_start, pair_block)
        second_tile = lax.dynamic_slice_in_dim(pair_second, block_start, pair_block)
        vis_real = vis_tiles[0][first_tile, :, second_tile, :]
        vis_imag = vis_tiles[1][first_tile, :, second_tile, :]
        first_stn = first_tile[:, None] * TILE + tile_line[None, :]
        second_stn = second_tile[:, None] * TILE + tile_line[None, :]
        patches = make_patches(vis_real, vis_imag, first_stn, second_stn, offsets, frequency, divisor, kernel_table)
        base_rows = lax.dynamic_slice_in_dim(base_cells[0], block_start, pair_block)
        base_cols = lax.dynamic_slice_in_dim(base_cells[1], block_start, pair_block)
        return (place_patches(uv_plane, patches, base_rows, base_cols), None)
    uv_plane, _ = lax.scan(add_block, jnp.zeros((UV, 2 * UV), jnp.float32), jnp.arange(pair_first.shape[0] // pair_block, dtype=jnp.int32))
    return uv_plane

def station_spectra(station_volts, pfb_coeffs, twiddle):
    frame_len = pfb_coeffs.shape[1]
    tap_count = pfb_coeffs.shape[0]
    spec_count = station_volts.shape[1] // frame_len
    frames = station_volts.reshape(1, station_volts.shape[0], spec_count, frame_len)
    padded = jnp.concatenate([jnp.zeros((1, station_volts.shape[0], tap_count - 1, frame_len), station_volts.dtype), frames], axis=2)
    filtered = filter_frames(padded, pfb_coeffs, spec_count).reshape(-1, frame_len)
    return lax.dot_general(twiddle, filtered, (((0,), (1,)), ((), ())), preferred_element_type=jnp.float32).astype(jnp.bfloat16)

def reference(voltages, pfb_coeffs, station_offsets, tile_cells, kernel_table):
    twiddle = dft_table(FRAME)
    spectra = lax.map(lambda station_volts: station_spectra(station_volts, pfb_coeffs, twiddle), voltages)
    spectra = jnp.transpose(spectra, (1, 0, 2)).reshape(CHANNELS, 2, STATIONS, -1)
    norm_factor = 1.0 / (POLS * SPECTRA)
    divisor = FRAME - 1

    def channel_plane(chan_index):
        visibility = correlate(spectra[chan_index], norm_factor)
        return grid_pairs(visibility, tile_cells[chan_index], CHANNELS + chan_index, station_offsets, kernel_table, divisor)
    planes = lax.map(channel_plane, jnp.arange(CHANNELS, dtype=jnp.int32))
    return jnp.transpose(planes, (1, 0, 2))
```

```python
import functools
import math

import jax
import jax.numpy as jnp
import numpy as np
from jax import lax
from jax.experimental import pallas as pl
from jax.experimental.pallas import tpu as pltpu
from jax.sharding import PartitionSpec as P

TILE = 32
PATCH = 16
SPREAD = 5
UV = 128


highest = lax.Precision.HIGHEST


def shifted(block, axis, distance):
    devices = range(lax.axis_size(axis))
    route = [(i - distance, i) for i in devices if i - distance in devices]
    return lax.ppermute(block, axis, route)


def dft_table(frame_len):
    chan_count = frame_len // 2
    sample_line = jnp.arange(frame_len, dtype=jnp.int32)[:, None]
    chan_line = jnp.arange(chan_count, dtype=jnp.int32)[None, :]
    angles = (sample_line * chan_line % frame_len).astype(jnp.float32) * (2.0 * math.pi / frame_len)
    norm_factor = 1.0 / math.sqrt(frame_len)
    twiddle = jnp.stack([jnp.cos(angles) * norm_factor, -jnp.sin(angles) * norm_factor], axis=2)
    return twiddle.reshape(frame_len, 2 * chan_count).astype(jnp.bfloat16)


CLASSES = SPREAD * SPREAD
high = lax.Precision.HIGH


def fused_filter(coeffs, twiddle, step):
    taps, frame_len = coeffs.shape
    flat = coeffs.reshape(-1)
    columns = [
        jnp.pad(flat, (frame_len * (f + 1), frame_len * (step - 1 - f))) for f in range(step)
    ]
    shifted_coeffs = jnp.stack(columns, axis=0)
    spread = np.kron(np.ones((1, frame_len), np.float32), np.eye(step, dtype=np.float32))
    wide = jnp.einsum("fm,fn->mn", shifted_coeffs, jnp.asarray(spread), precision=highest)
    tiled = jnp.tile(jnp.repeat(twiddle.astype(jnp.float32), step, axis=1), (step + taps, 1))
    return (wide * tiled).astype(jnp.bfloat16)

def separation_table(frequency, divisor, kernel_table):
    over_count = kernel_table.shape[0]
    separation = jnp.arange(2 * SPREAD - 1, dtype=jnp.int32)
    scaled = separation * frequency
    cell_index = scaled // divisor
    fine_index = scaled % divisor * over_count // divisor
    choose = (fine_index[:, None] == jnp.arange(over_count, dtype=jnp.int32)[None, :]).astype(
        jnp.float32
    )
    tap_values = jnp.dot(choose, kernel_table, precision=highest)
    place_rel = jnp.arange(PATCH, dtype=jnp.int32)[None, :] - cell_index[:, None]
    weights = jnp.zeros(place_rel.shape, jnp.float32)
    for tap_index in range(kernel_table.shape[1]):
        weights = weights + tap_values[:, tap_index : tap_index + 1] * (
            place_rel == tap_index
        ).astype(jnp.float32)
    return weights


def shifted_weights(weights, bases):
    place = jnp.arange(UV, dtype=jnp.int32)[None, :, None] - bases[:, None, :]
    taps = jnp.arange(PATCH, dtype=jnp.int32)[None, :, None, None]
    spots = place[:, None] == taps
    if weights.dtype == jnp.float32:
        return jnp.einsum("cdt,ctwp->cdwp", weights, spots.astype(jnp.float32), precision=highest)
    return jnp.einsum(
        "cdt,ctwp->cdwp", weights, spots.astype(jnp.bfloat16), preferred_element_type=jnp.float32
    ).astype(jnp.bfloat16)


def body(voltages, pfb_coeffs, station_offsets, tile_cells, kernel_table):
    stn_local, pol_count, samples = voltages.shape
    tap_count, frame_len = pfb_coeffs.shape
    spec_count = samples // frame_len
    step = 128 // math.gcd(128, frame_len)
    chunks = spec_count // step
    flat = jnp.transpose(voltages, (1, 0, 2))
    earlier = shifted(flat[:, :, samples - tap_count * frame_len :], "grid", 1)
    extended = jnp.concatenate([earlier, flat], axis=2)
    width = step * frame_len
    reach = (step + tap_count) * frame_len
    blocks = jnp.stack(
        [extended[:, :, c * width : c * width + reach] for c in range(chunks)], axis=1
    )
    matrix = fused_filter(pfb_coeffs, dft_table(frame_len), step)
    spectra = jnp.einsum(
        "pcsm,mn->npcs", blocks, matrix, preferred_element_type=jnp.float32
    ).astype(jnp.bfloat16)
    spectra = spectra.reshape(frame_len // 2, 2, step * pol_count * chunks, stn_local)
    spectra, tile_cells = lax.optimization_barrier((spectra, tile_cells))
    turned = lax.all_to_all(spectra, "stn", split_axis=0, concat_axis=3, tiled=True)
    turned = jnp.transpose(turned, (0, 1, 3, 2))
    ch_dev, _, stations, depth = turned.shape
    tiles = stations // TILE
    divisor = frame_len - 1
    first_chan = lax.axis_index("stn") * ch_dev + frame_len // 2
    norm_factor = 1.0 / (pol_count * spec_count * lax.axis_size("grid"))

    classes = (station_offsets[0] * SPREAD + station_offsets[1]).reshape(tiles, TILE)
    hot = classes[:, :, None] == jnp.arange(CLASSES, dtype=jnp.int32)
    hot_low = hot.astype(jnp.bfloat16)
    hot_full = hot.astype(jnp.float32)
    tiled = turned.reshape(ch_dev, 2, tiles, TILE, depth)
    summed = jnp.einsum(
        "aiq,ceaik->ceaqk", hot_low, tiled, preferred_element_type=jnp.float32
    ).astype(jnp.bfloat16)

    def stacked(z):
        real_part, imag_part = z[:, 0], z[:, 1]
        partner = jnp.concatenate([real_part, imag_part], axis=-1)
        turned_partner = jnp.concatenate([imag_part, -real_part], axis=-1)
        return jnp.stack([partner, turned_partner], axis=1), partner

    left, right = stacked(summed)
    shape = (SPREAD, SPREAD, 2 * depth)
    terms = []
    for i in range(ch_dev):
        taps = jnp.transpose(left[i].reshape((2 * tiles,) + shape), (1, 2, 3, 0))
        terms.append(
            lax.conv_general_dilated(
                right[i].reshape((tiles,) + shape),
                taps,
                (1, 1),
                [(SPREAD - 1, SPREAD - 1)] * 2,
                dimension_numbers=("NHWC", "HWIO", "HWNC"),
                preferred_element_type=jnp.float32,
            )
        )
    seps = 2 * SPREAD - 1
    cross = jnp.stack(terms).reshape(ch_dev, seps, seps, tiles, 2, tiles)
    cross = jnp.transpose(cross, (0, 4, 1, 2, 3, 5)).reshape(ch_dev, 2, seps, seps, tiles * tiles)
    own_left, own_right = stacked(tiled)
    own = jnp.einsum("ceaik,cajk->ceaij", own_left, own_right, preferred_element_type=jnp.float32)
    line = np.arange(TILE)
    own = jnp.where(jnp.asarray(line[:, None] < line[None, :]), own, 0.0)
    own = jnp.einsum("aiq,ceaij->ceaqj", hot_full, own, precision=high)
    own = jnp.einsum("ceaqj,ajs->ceasq", own, hot_full, precision=high)
    class_line = np.arange(CLASSES)
    back_u = class_line[:, None] // SPREAD - class_line[None, :] // SPREAD + SPREAD - 1
    back_v = class_line[:, None] % SPREAD - class_line[None, :] % SPREAD + SPREAD - 1
    pick = np.arange(seps * seps) == (back_u * seps + back_v).reshape(-1, 1)
    own = jnp.einsum(
        "ceam,mz->ceza",
        own.reshape(ch_dev, 2, tiles, CLASSES * CLASSES),
        jnp.asarray(pick.astype(np.float32)),
        precision=high,
    )
    diagonal = np.zeros((tiles, tiles * tiles), np.float32)
    diagonal[np.arange(tiles), np.arange(tiles) * (tiles + 1)] = 1.0
    own = jnp.einsum("ceza,ap->cezp", own, jnp.asarray(diagonal), precision=high)
    own = own.reshape(ch_dev, 2, seps, seps, tiles * tiles)
    same = jnp.asarray(diagonal.sum(axis=0) > 0)
    cross = jnp.where(same, own, cross)

    pair_first, pair_second = np.triu_indices(tiles)
    select = np.zeros((pair_first.size, tiles * tiles), np.float32)
    select[np.arange(pair_first.size), pair_second * tiles + pair_first] = 1.0
    missing = (1.0 - select.sum(axis=0)).astype(np.int32) * 4096
    cells = jnp.einsum(
        "cxk,kp->cxp", tile_cells.astype(jnp.float32), jnp.asarray(select), precision=highest
    )
    cells = jnp.round(cells).astype(jnp.int32) + jnp.asarray(missing)
    weights = jnp.stack(
        [separation_table(first_chan + i, divisor, kernel_table)[::-1] for i in range(ch_dev)]
    )
    scaled = weights * norm_factor
    coarse = lax.reduce_precision(scaled, 8, 7)
    rest = (scaled - coarse).astype(jnp.bfloat16)
    rows = [shifted_weights(part, cells[:, 0]) for part in (coarse.astype(jnp.bfloat16), rest)]
    place = jnp.arange(UV, dtype=jnp.int32)[None, :, None] - cells[:, 1][:, None, :]
    cols = []
    for v in range(seps):
        placed = jnp.zeros(place.shape, jnp.float32)
        for t in range(PATCH):
            placed = jnp.where(place == t, weights[:, v, t][:, None, None], placed)
        cols.append(placed)
    cols = lax.optimization_barrier(tuple(cols))
    spread_cols = sum(
        cross[:, :, :, v, None, :] * cols[v][:, None, None] for v in range(seps)
    )
    spread_cols = spread_cols.astype(jnp.bfloat16)
    planes = sum(
        jnp.einsum(
            "cdup,cedwp->ucew", part, spread_cols, preferred_element_type=jnp.float32
        )
        for part in rows
    )
    grid_count = lax.axis_size("grid")
    planes = planes.reshape(grid_count, UV // grid_count, ch_dev, 2 * UV).astype(jnp.bfloat16)
    parts = lax.all_to_all(planes, "grid", split_axis=0, concat_axis=0, tiled=True)
    return parts.astype(jnp.float32).sum(axis=0)


f32, bf16, i32 = jnp.float32, jnp.bfloat16, jnp.int32
MESH = pl.DeviceIdType.MESH
SEPS = 2 * SPREAD - 1
STEP = 16
ROWS = 112
LANES = 128
PAIR_ROWS = 256


def iota(shape, axis):
    return lax.broadcasted_iota(i32, shape, axis)


def ones_where(mask, kind=bf16):
    return jnp.where(mask, 1.0, 0.0).astype(kind)


def dot(a, b):
    return lax.dot_general(a, b, (((1,), (0,)), ((), ())), preferred_element_type=f32)


def dot_nt(a, b):
    return lax.dot_general(a, b, (((1,), (1,)), ((), ())), preferred_element_type=f32)


def split(x):
    top = x.astype(bf16)
    return top, (x - top.astype(f32)).astype(bf16)


def send_order(n):
    return sorted(range(1, n), key=lambda k: abs(2 * k - n))


def front_kernel(
    dims, v_ref, coef_ref, tw_ref, off_ref, off_smem, recv_ref, drecv_ref,
    vext, wide, spec, send, own, vis, left, picks, dsend,
    in_sem, halo_send, halo_recv, send_sem, recv_sem, dsend_sem, drecv_sem,
):
    n_stn, n_grid, chans, taps, frame_len, st = dims
    me, here = lax.axis_index("stn"), lax.axis_index("grid")
    reach = (STEP + taps) * frame_len
    halo = taps * frame_len
    samples = v_ref.shape[1]
    blocks = samples // (STEP * frame_len)
    order = send_order(n_stn)

    barrier = pltpu.get_barrier_semaphore()
    for k in range(1, n_stn):
        pl.semaphore_signal(
            barrier, inc=1, device_id=(lax.rem(me + k, n_stn), here), device_id_type=MESH
        )
    for k in range(1, n_grid):
        pl.semaphore_signal(
            barrier, inc=1, device_id=(me, lax.rem(here + k, n_grid)), device_id_type=MESH
        )
    load = pltpu.make_async_copy(v_ref, vext.at[:, pl.ds(halo, samples)], in_sem)
    load.start()

    coef = coef_ref[...]
    line = jnp.concatenate(
        [jnp.zeros((1, frame_len), f32)]
        + [coef[k : k + 1, :] for k in range(taps)]
        + [jnp.zeros((1, reach - (taps + 1) * frame_len), f32)],
        axis=1,
    )
    shifted_line = jnp.concatenate(
        [line if f == 0 else pltpu.roll(line, f * frame_len, 1) for f in range(STEP)], axis=0
    )
    for r in range(2 * n_stn * chans):
        wide[r * STEP : (r + 1) * STEP, :] = (tw_ref[r : r + 1, :] * shifted_line).astype(bf16)

    offs = off_ref[...].astype(f32)
    stations = offs.shape[1]
    cls = jnp.broadcast_to(SPREAD * offs[0:1] + offs[1:2], (16, stations)).astype(bf16)
    kap = jnp.broadcast_to(SEPS * offs[0:1] + offs[1:2], (LANES, stations)).astype(bf16)
    row_of = (stations, LANES)
    mine = ones_where(iota(row_of, 0) == me * st + iota(row_of, 1) // 2)
    cls_line = dot(cls, mine)[0:1]
    lane = iota((1, LANES), 1)
    code = ((lane % 2) * 2 + lane // 2 // TILE).astype(f32) * CLASSES + cls_line
    line_a = iota((ROWS, LANES), 0).astype(f32)
    sum_rows = ones_where(line_a == code)
    line_b = iota((LANES, LANES), 0)
    lane_b = iota((LANES, LANES), 1)
    own_rows = ones_where(line_b == (lane_b % 2) * st + lane_b // 2)
    gather_rows = jnp.concatenate([sum_rows, own_rows], axis=0)

    pl.semaphore_wait(barrier, n_stn + n_grid - 2)

    @pl.when(here < n_grid - 1)
    def _():
        pltpu.make_async_remote_copy(
            src_ref=v_ref.at[:, pl.ds(samples - halo, halo)],
            dst_ref=vext.at[:, pl.ds(0, halo)],
            send_sem=halo_send,
            recv_sem=halo_recv,
            device_id=(me, here + 1),
            device_id_type=MESH,
        ).start()

    load.wait()

    def filtered(c, t):
        rows = wide[c * 2 * n_stn * STEP : (c + 1) * 2 * n_stn * STEP, :]
        window = vext[:, t * STEP * frame_len : t * STEP * frame_len + reach]
        got = dot_nt(rows, window).astype(bf16)
        spec[c, :, :, t] = got.reshape(n_stn, 2, STEP, LANES)

    for t in range(1, blocks):
        filtered(0, t)

    halo_copy = pltpu.make_async_remote_copy(
        src_ref=v_ref.at[:, pl.ds(samples - halo, halo)],
        dst_ref=vext.at[:, pl.ds(0, halo)],
        send_sem=halo_send,
        recv_sem=halo_recv,
        device_id=(me, lax.rem(here + 1, n_grid)),
        device_id_type=MESH,
    )

    @pl.when(here > 0)
    def _():
        halo_copy.wait_recv()

    @pl.when(here == 0)
    def _():
        vext[:, 0:halo] = jnp.zeros((LANES, halo), bf16)

    copies = []
    for c in range(chans):
        for t in range(blocks) if c else (0,):
            filtered(c, t)
        for k in order + [0]:
            to = lax.rem(me + k, n_stn)
            got = dot_nt(gather_rows, spec[c, to].reshape(LANES, LANES))
            send[c, to] = got[:ROWS].astype(bf16)
            alone = got[ROWS:].astype(bf16)
            own[c, to] = jnp.concatenate([alone[:st], alone[st:]], axis=1)
            if k:
                copy = pltpu.make_async_remote_copy(
                    src_ref=send.at[c, to],
                    dst_ref=recv_ref.at[c, me],
                    send_sem=send_sem.at[c, k],
                    recv_sem=recv_sem.at[c, k],
                    device_id=(to, here),
                    device_id_type=MESH,
                )
                copy.start()
                copies.append(copy)
            else:
                recv_ref[c, me] = send[c, me]

    vis[...] = jnp.zeros(vis.shape, f32)
    lane2 = iota((st, 2 * LANES), 1)
    flip = jnp.where(lane2 % LANES < LANES // 2, 1.0, -1.0)
    for c in range(chans):
        for d in range(n_stn):
            x = own[c, d]
            xf = x.astype(f32)
            turned = jnp.concatenate(
                [
                    pltpu.roll(xf[:, p * LANES : (p + 1) * LANES], LANES // 2, 1)
                    for p in range(2)
                ],
                axis=1,
            )
            both = jnp.concatenate([x, (turned * flip).astype(bf16)], axis=0)
            got = dot_nt(both, jnp.concatenate([x, x], axis=0))
            for e in range(2):
                vis[d * 8 + c * 2 + e] = got[e * st : (e + 1) * st]

    half = n_stn * 8
    lane3 = iota((half, LANES), 1)
    for k in range(TILE // 2):
        even = jnp.where(lane3 % st < TILE, vis[:, 2 * k, :], vis[:, 2 * k + TILE, :])
        odd = jnp.where(lane3 % st < TILE, vis[:, 2 * k + 1, :], vis[:, 2 * k + 1 + TILE, :])
        top, low = split(jnp.where(lane3 < st, even, odd))
        left[0:half, k * LANES : (k + 1) * LANES] = top
        left[half:, k * LANES : (k + 1) * LANES] = low
    which = (st, stations)
    kap_col = dot_nt(ones_where(iota(which, 1) == me * st + iota(which, 0)), kap)
    base = kap_col.astype(i32) + iota((st, LANES), 1) - (SEPS * (SPREAD - 1) + SPREAD - 1)
    blank = jnp.zeros((TILE, LANES), bf16)
    row_t = iota((TILE, LANES), 0)
    for i in range(TILE):
        for a in range(2):
            at = me * st + a * TILE + i
            value = off_smem[0, at] * SEPS + off_smem[1, at]
            hit = ones_where((base[a * TILE : (a + 1) * TILE] == value) & (row_t > i))
            first = i * st + a * TILE
            picks[first : first + TILE, a * LANES : (a + 1) * LANES] = hit
            picks[first : first + TILE, (1 - a) * LANES : (2 - a) * LANES] = blank
    binned = dot(left[...], picks[...])
    binned = (binned[:half] + binned[half:]).reshape(n_stn, 8, 2 * LANES)
    dsend[...] = binned
    for k in order:
        to = lax.rem(me + k, n_stn)
        copy = pltpu.make_async_remote_copy(
            src_ref=dsend.at[to],
            dst_ref=drecv_ref.at[me],
            send_sem=dsend_sem.at[k],
            recv_sem=drecv_sem.at[k],
            device_id=(to, here),
            device_id_type=MESH,
        )
        copy.start()
        copies.append(copy)
    drecv_ref[me] = dsend[me]

    for copy in copies:
        copy.wait()

    @pl.when(here < n_grid - 1)
    def _():
        halo_copy.wait_send()


def back_kernel(
    dims, recv_ref, drecv_ref, cells_ref, table_ref, out_ref,
    perm, bands, vweights, xs, sums, placed,
):
    n_stn, n_grid, chans, taps, frame_len, st = dims
    me = lax.axis_index("stn")
    tiles = 2 * n_stn
    over, kern = table_ref.shape
    divisor = frame_len - 1
    side = SPREAD * tiles
    full = SPREAD * side
    depth = 2 * LANES
    wide = tiles * PATCH

    shape = (perm.shape[1], perm.shape[2])
    r, col = iota(shape, 0), iota(shape, 1)
    b, q = r % tiles, r // tiles
    for p in range(2):
        want = (b // 2) * ROWS + (p * 2 + b % 2) * CLASSES + q
        perm[p] = ones_where((col == want) & (r < full))

    npair = cells_ref.shape[2]

    def pair_number(a, b):
        return jnp.where(a <= b, a * tiles - a * (a - 1) // 2 + b - a, -1)

    kl = (npair, PAIR_ROWS)
    choose = ones_where(iota(kl, 0) == pair_number(iota(kl, 1) // tiles, iota(kl, 1) % tiles))
    kr = (PAIR_ROWS, npair)
    choose_t = ones_where(iota(kr, 1) == pair_number(iota(kr, 0) // tiles, iota(kr, 0) % tiles))
    lane_pair = iota((1, PAIR_ROWS), 1)
    absent = jnp.where(lane_pair // tiles <= lane_pair % tiles, 0.0, -1000.0)

    def weight_rows(c, d, r):
        scaled = (d * (me * chans + c + frame_len // 2)).astype(f32)
        cell = jnp.floor((scaled + 0.5) / divisor)
        rest = scaled - cell * divisor
        fine = jnp.floor((rest * over + 0.5) / divisor)
        tap = r - cell.astype(i32)
        code = jnp.where((tap >= 0) & (tap < kern), fine.astype(i32) * kern + tap, -1)
        got = jnp.zeros(code.shape, f32)
        for o in range(over):
            for t in range(kern):
                got = jnp.where(code == o * kern + t, table_ref[o, t], got)
        return got

    placed[...] = jnp.zeros(placed.shape, bf16)
    norm = 1.0 / (n_grid * depth // 2)
    rows_t = (16, UV)
    rows_w = (16, wide)
    same_tile = iota((tiles, wide), 0) == iota((tiles, wide), 1) // PATCH
    own_lane = iota((32, LANES), 1) // SEPS
    lane_p = (2 * tiles, LANES)
    for c in range(chans):
        cells = cells_ref[c].astype(f32)
        row_line = dot(jnp.broadcast_to(cells[0:1], (16, npair)).astype(bf16), choose)[0:1] + absent
        col_rows = dot_nt(choose_t, jnp.broadcast_to(cells[1:2], (LANES, npair)).astype(bf16))
        spot = iota((UV, PAIR_ROWS), 0).astype(f32) == row_line
        spots = ones_where(spot)
        lines = weight_rows(c, iota(rows_t, 0), (UV - iota(rows_t, 1)) % UV)
        for du in range(SEPS):
            band = pltpu.roll(
                jnp.broadcast_to(lines[du : du + 1], (UV, UV)), 0, 1, stride=1, stride_axis=0
            )
            top, low = split(band)
            bands[c, du] = dot(jnp.concatenate([top, low], axis=0), spots).astype(bf16)
        across = weight_rows(c, iota(rows_w, 0), iota(rows_w, 1) % PATCH)
        for s in range(SPREAD):
            for q in range(SPREAD):
                at = q - s + SPREAD - 1
                part = jnp.where(same_tile, across[at : at + 1], 0.0)
                top, low = split(part)
                vweights[0, s, q * tiles : (q + 1) * tiles, :] = top
                vweights[1, s, q * tiles : (q + 1) * tiles, :] = low
            vweights[0, s, side:, :] = jnp.zeros((LANES - side, wide), bf16)
            vweights[1, s, side:, :] = jnp.zeros((LANES - side, wide), bf16)
        onto = ones_where(iota((LANES, 16), 0) % SEPS == iota((LANES, 16), 1))
        a_top, a_low = split(across)
        own_top, own_low = dot(onto, a_top).astype(bf16), dot(onto, a_low).astype(bf16)

        got = recv_ref[c].reshape(n_stn * ROWS, LANES)
        lane_h = iota((full, LANES), 1) < LANES // 2
        turned = []
        for p in range(2):
            x = dot(perm[p], got)
            xs[:, p * LANES : (p + 1) * LANES] = x.astype(bf16)
            y = pltpu.roll(x[:full], LANES // 2, 1)
            turned.append(jnp.where(lane_h, -y, y).astype(bf16))
        lefts = [xs[:full], jnp.concatenate(turned, axis=1)]
        for e in range(2):
            blocks = [dot_nt(lefts[e], xs[q * side : q * side + LANES]) for q in range(SPREAD)]
            for du in range(SEPS):
                d = du - (SPREAD - 1)
                total = sum(
                    blocks[s + d][s * side : (s + 1) * side]
                    for s in range(SPREAD)
                    if 0 <= s + d < SPREAD
                )
                top, low = split(total)
                at = (e * SEPS + du) * tiles
                for s in range(SPREAD):
                    sums[0, s, at : at + tiles, :] = top[s * tiles : (s + 1) * tiles]
                    sums[1, s, at : at + tiles, :] = low[s * tiles : (s + 1) * tiles]
        patches = jnp.zeros((2 * SEPS * tiles, wide), f32)
        for s in range(SPREAD):
            for i, j in ((0, 0), (1, 0), (0, 1)):
                patches = patches + dot(sums[i, s], vweights[j, s])

        rr, cc = iota((32, n_stn * 8), 0), iota((32, n_stn * 8), 1)
        take = ones_where(cc == (rr % tiles // 2) * 8 + c * 2 + rr // tiles)
        d_top, d_low = split(drecv_ref[...].reshape(n_stn * 8, 2 * LANES))
        own = dot(take, d_top) + dot(take, d_low)
        odd = iota((32, LANES), 0) % 2 == 1
        own = jnp.where(odd, own[:, LANES:], own[:, :LANES])
        own_parts = []
        for e in range(2):
            for du in range(SEPS):
                own_parts.append(
                    jnp.where(own_lane == du, own, 0.0)[e * tiles : (e + 1) * tiles]
                )
        own_all = jnp.concatenate(own_parts, axis=0)
        o_top, o_low = split(own_all)
        own_patch = dot(o_top, own_top) + dot(o_low, own_top) + dot(o_top, own_low)
        rr, cc = iota(patches.shape, 0), iota(patches.shape, 1)
        patches = jnp.where(rr % tiles == cc // PATCH, own_patch, patches)

        for a in range(tiles):
            low_rows = 8 if a >= 8 else 0
            distance = iota((tiles, LANES), 1) - col_rows[a * tiles : (a + 1) * tiles].astype(i32)
            distance = distance[low_rows:]
            valid = (distance >= 0) & (distance < PATCH)
            index = jnp.where(valid, distance + (a % 8) * PATCH, 0)
            for du in range(SEPS):
                for e in range(2):
                    at = (e * SEPS + du) * tiles
                    source = patches[
                        at + low_rows : at + tiles, a // 8 * LANES : (a // 8 + 1) * LANES
                    ]
                    moved = jnp.where(valid, jnp.take_along_axis(source, index, axis=1), 0.0)
                    if low_rows:
                        moved = jnp.concatenate([jnp.zeros((8, LANES), f32), moved], axis=0)
                    placed[du, a * tiles : (a + 1) * tiles, e * LANES : (e + 1) * LANES] = (
                        moved.astype(bf16)
                    )
        plane = jnp.zeros((2 * UV, 2 * UV), f32)
        for du in range(SEPS):
            plane = plane + dot(bands[c, du], placed[du])
        plane = (plane[:UV] + plane[UV:]) * norm
        out_ref[c] = plane.astype(bf16)


def kernel_body(voltages, pfb_coeffs, station_offsets, tile_cells, kernel_table):
    st, pols, samples = voltages.shape
    taps, frame_len = pfb_coeffs.shape
    n_stn, n_grid = lax.axis_size("stn"), lax.axis_size("grid")
    chans = tile_cells.shape[0]
    dims = (n_stn, n_grid, chans, taps, frame_len, st)
    reach = (STEP + taps) * frame_len
    blocks = samples // (STEP * frame_len)

    table = dft_table(frame_len).astype(f32).T.reshape(n_stn, chans, 2, frame_len)
    table = jnp.transpose(table, (1, 0, 2, 3)).reshape(-1, frame_len)
    table = jnp.tile(table, (1, STEP + taps))
    vmem = pl.BlockSpec(memory_space=pltpu.VMEM)
    smem = pl.BlockSpec(memory_space=pltpu.SMEM)
    anywhere = pl.BlockSpec(memory_space=pl.ANY)
    flat = voltages.reshape(st * pols, samples)
    recv, drecv = pl.pallas_call(
        functools.partial(front_kernel, dims),
        out_shape=[
            jax.ShapeDtypeStruct((chans, n_stn, ROWS, LANES), bf16),
            jax.ShapeDtypeStruct((n_stn, 8, 2 * LANES), f32),
        ],
        in_specs=[anywhere, vmem, vmem, vmem, smem],
        out_specs=[vmem, vmem],
        scratch_shapes=[
            pltpu.VMEM((LANES, taps * frame_len + samples), bf16),
            pltpu.VMEM((2 * n_stn * chans * STEP, reach), bf16),
            pltpu.VMEM((chans, n_stn, 2, blocks, STEP, LANES), bf16),
            pltpu.VMEM((chans, n_stn, ROWS, LANES), bf16),
            pltpu.VMEM((chans, n_stn, st, 2 * LANES), bf16),
            pltpu.VMEM((n_stn * 8, st, LANES), f32),
            pltpu.VMEM((n_stn * 16, TILE * st), bf16),
            pltpu.VMEM((TILE * st, 2 * LANES), bf16),
            pltpu.VMEM((n_stn, 8, 2 * LANES), f32),
            pltpu.SemaphoreType.DMA,
            pltpu.SemaphoreType.DMA,
            pltpu.SemaphoreType.DMA,
            pltpu.SemaphoreType.DMA((chans, n_stn)),
            pltpu.SemaphoreType.DMA((chans, n_stn)),
            pltpu.SemaphoreType.DMA((n_stn,)),
            pltpu.SemaphoreType.DMA((n_stn,)),
        ],
        compiler_params=pltpu.CompilerParams(
            collective_id=0, has_side_effects=True, vmem_limit_bytes=48 << 20
        ),
    )(flat, pfb_coeffs, table, station_offsets, station_offsets)

    tiles = 2 * n_stn
    full = SPREAD * SPREAD * tiles
    planes = pl.pallas_call(
        functools.partial(back_kernel, dims),
        out_shape=jax.ShapeDtypeStruct((chans, UV, 2 * UV), bf16),
        in_specs=[vmem, vmem, vmem, smem],
        out_specs=vmem,
        scratch_shapes=[
            pltpu.VMEM((2, full + 48, n_stn * ROWS), bf16),
            pltpu.VMEM((chans, SEPS, 2 * UV, PAIR_ROWS), bf16),
            pltpu.VMEM((2, SPREAD, LANES, tiles * PATCH), bf16),
            pltpu.VMEM((full + 48, 2 * LANES), bf16),
            pltpu.VMEM((2, SPREAD, 2 * SEPS * tiles, LANES), bf16),
            pltpu.VMEM((SEPS, PAIR_ROWS, 2 * UV), bf16),
        ],
        compiler_params=pltpu.CompilerParams(vmem_limit_bytes=48 << 20),
    )(recv, drecv, tile_cells, kernel_table)
    planes = planes.reshape(chans, n_grid, UV // n_grid, 2 * UV)
    parts = lax.all_to_all(planes, "grid", split_axis=1, concat_axis=1, tiled=True)
    return jnp.transpose(parts.astype(f32).sum(axis=1), (1, 0, 2))


def kernels_fit(mesh, args):
    voltages, pfb_coeffs, offsets, cells, _ = args
    n_stn, n_grid = mesh.shape["stn"], mesh.shape["grid"]
    stations, pols, samples = voltages.shape
    taps, frame_len = pfb_coeffs.shape
    spectra = samples // frame_len // n_grid
    return (
        stations == 2 * TILE * n_stn
        and n_stn == 8
        and pols == 2
        and spectra == 64
        and taps == 16
        and frame_len // 2 == cells.shape[0] == 3 * n_stn
    )


def solution(mesh):
    placed = (P("stn", None, "grid"), P(), P(), P("stn", None, None), P())

    def run(*args):
        inner = kernel_body if kernels_fit(mesh, args) else body
        return jax.shard_map(
            inner, mesh=mesh, in_specs=placed, out_specs=P("grid", "stn", None), check_vma=False
        )(*args)

    return run
```

```python
import functools
import math

import jax
import jax.numpy as jnp
import numpy as np
from jax import lax
from jax.experimental import pallas as pl
from jax.experimental.pallas import tpu as pltpu
from jax.sharding import PartitionSpec as P

TILE = 32
PATCH = 16
SPREAD = 5
UV = 128


highest = lax.Precision.HIGHEST


def shifted(block, axis, distance):
    devices = range(lax.axis_size(axis))
    route = [(i - distance, i) for i in devices if i - distance in devices]
    return lax.ppermute(block, axis, route)


def dft_table(frame_len):
    chan_count = frame_len // 2
    sample_line = jnp.arange(frame_len, dtype=jnp.int32)[:, None]
    chan_line = jnp.arange(chan_count, dtype=jnp.int32)[None, :]
    angles = (sample_line * chan_line % frame_len).astype(jnp.float32) * (2.0 * math.pi / frame_len)
    norm_factor = 1.0 / math.sqrt(frame_len)
    twiddle = jnp.stack([jnp.cos(angles) * norm_factor, -jnp.sin(angles) * norm_factor], axis=2)
    return twiddle.reshape(frame_len, 2 * chan_count).astype(jnp.bfloat16)


CLASSES = SPREAD * SPREAD
high = lax.Precision.HIGH


def fused_filter(coeffs, twiddle, step):
    taps, frame_len = coeffs.shape
    flat = coeffs.reshape(-1)
    columns = [
        jnp.pad(flat, (frame_len * (f + 1), frame_len * (step - 1 - f))) for f in range(step)
    ]
    shifted_coeffs = jnp.stack(columns, axis=0)
    spread = np.kron(np.ones((1, frame_len), np.float32), np.eye(step, dtype=np.float32))
    wide = jnp.einsum("fm,fn->mn", shifted_coeffs, jnp.asarray(spread), precision=highest)
    tiled = jnp.tile(jnp.repeat(twiddle.astype(jnp.float32), step, axis=1), (step + taps, 1))
    return (wide * tiled).astype(jnp.bfloat16)

def separation_table(frequency, divisor, kernel_table):
    over_count = kernel_table.shape[0]
    separation = jnp.arange(2 * SPREAD - 1, dtype=jnp.int32)
    scaled = separation * frequency
    cell_index = scaled // divisor
    fine_index = scaled % divisor * over_count // divisor
    choose = (fine_index[:, None] == jnp.arange(over_count, dtype=jnp.int32)[None, :]).astype(
        jnp.float32
    )
    tap_values = jnp.dot(choose, kernel_table, precision=highest)
    place_rel = jnp.arange(PATCH, dtype=jnp.int32)[None, :] - cell_index[:, None]
    weights = jnp.zeros(place_rel.shape, jnp.float32)
    for tap_index in range(kernel_table.shape[1]):
        weights = weights + tap_values[:, tap_index : tap_index + 1] * (
            place_rel == tap_index
        ).astype(jnp.float32)
    return weights


def shifted_weights(weights, bases):
    place = jnp.arange(UV, dtype=jnp.int32)[None, :, None] - bases[:, None, :]
    taps = jnp.arange(PATCH, dtype=jnp.int32)[None, :, None, None]
    spots = place[:, None] == taps
    if weights.dtype == jnp.float32:
        return jnp.einsum("cdt,ctwp->cdwp", weights, spots.astype(jnp.float32), precision=highest)
    return jnp.einsum(
        "cdt,ctwp->cdwp", weights, spots.astype(jnp.bfloat16), preferred_element_type=jnp.float32
    ).astype(jnp.bfloat16)


def body(voltages, pfb_coeffs, station_offsets, tile_cells, kernel_table):
    stn_local, pol_count, samples = voltages.shape
    tap_count, frame_len = pfb_coeffs.shape
    spec_count = samples // frame_len
    step = 128 // math.gcd(128, frame_len)
    chunks = spec_count // step
    flat = jnp.transpose(voltages, (1, 0, 2))
    earlier = shifted(flat[:, :, samples - tap_count * frame_len :], "grid", 1)
    extended = jnp.concatenate([earlier, flat], axis=2)
    width = step * frame_len
    reach = (step + tap_count) * frame_len
    blocks = jnp.stack(
        [extended[:, :, c * width : c * width + reach] for c in range(chunks)], axis=1
    )
    matrix = fused_filter(pfb_coeffs, dft_table(frame_len), step)
    spectra = jnp.einsum(
        "pcsm,mn->npcs", blocks, matrix, preferred_element_type=jnp.float32
    ).astype(jnp.bfloat16)
    spectra = spectra.reshape(frame_len // 2, 2, step * pol_count * chunks, stn_local)
    spectra, tile_cells = lax.optimization_barrier((spectra, tile_cells))
    turned = lax.all_to_all(spectra, "stn", split_axis=0, concat_axis=3, tiled=True)
    turned = jnp.transpose(turned, (0, 1, 3, 2))
    ch_dev, _, stations, depth = turned.shape
    tiles = stations // TILE
    divisor = frame_len - 1
    first_chan = lax.axis_index("stn") * ch_dev + frame_len // 2
    norm_factor = 1.0 / (pol_count * spec_count * lax.axis_size("grid"))

    classes = (station_offsets[0] * SPREAD + station_offsets[1]).reshape(tiles, TILE)
    hot = classes[:, :, None] == jnp.arange(CLASSES, dtype=jnp.int32)
    hot_low = hot.astype(jnp.bfloat16)
    hot_full = hot.astype(jnp.float32)
    tiled = turned.reshape(ch_dev, 2, tiles, TILE, depth)
    summed = jnp.einsum(
        "aiq,ceaik->ceaqk", hot_low, tiled, preferred_element_type=jnp.float32
    ).astype(jnp.bfloat16)

    def stacked(z):
        real_part, imag_part = z[:, 0], z[:, 1]
        partner = jnp.concatenate([real_part, imag_part], axis=-1)
        turned_partner = jnp.concatenate([imag_part, -real_part], axis=-1)
        return jnp.stack([partner, turned_partner], axis=1), partner

    left, right = stacked(summed)
    shape = (SPREAD, SPREAD, 2 * depth)
    terms = []
    for i in range(ch_dev):
        taps = jnp.transpose(left[i].reshape((2 * tiles,) + shape), (1, 2, 3, 0))
        terms.append(
            lax.conv_general_dilated(
                right[i].reshape((tiles,) + shape),
                taps,
                (1, 1),
                [(SPREAD - 1, SPREAD - 1)] * 2,
                dimension_numbers=("NHWC", "HWIO", "HWNC"),
                preferred_element_type=jnp.float32,
            )
        )
    seps = 2 * SPREAD - 1
    cross = jnp.stack(terms).reshape(ch_dev, seps, seps, tiles, 2, tiles)
    cross = jnp.transpose(cross, (0, 4, 1, 2, 3, 5)).reshape(ch_dev, 2, seps, seps, tiles * tiles)
    own_left, own_right = stacked(tiled)
    own = jnp.einsum("ceaik,cajk->ceaij", own_left, own_right, preferred_element_type=jnp.float32)
    line = np.arange(TILE)
    own = jnp.where(jnp.asarray(line[:, None] < line[None, :]), own, 0.0)
    own = jnp.einsum("aiq,ceaij->ceaqj", hot_full, own, precision=high)
    own = jnp.einsum("ceaqj,ajs->ceasq", own, hot_full, precision=high)
    class_line = np.arange(CLASSES)
    back_u = class_line[:, None] // SPREAD - class_line[None, :] // SPREAD + SPREAD - 1
    back_v = class_line[:, None] % SPREAD - class_line[None, :] % SPREAD + SPREAD - 1
    pick = np.arange(seps * seps) == (back_u * seps + back_v).reshape(-1, 1)
    own = jnp.einsum(
        "ceam,mz->ceza",
        own.reshape(ch_dev, 2, tiles, CLASSES * CLASSES),
        jnp.asarray(pick.astype(np.float32)),
        precision=high,
    )
    diagonal = np.zeros((tiles, tiles * tiles), np.float32)
    diagonal[np.arange(tiles), np.arange(tiles) * (tiles + 1)] = 1.0
    own = jnp.einsum("ceza,ap->cezp", own, jnp.asarray(diagonal), precision=high)
    own = own.reshape(ch_dev, 2, seps, seps, tiles * tiles)
    same = jnp.asarray(diagonal.sum(axis=0) > 0)
    cross = jnp.where(same, own, cross)

    pair_first, pair_second = np.triu_indices(tiles)
    select = np.zeros((pair_first.size, tiles * tiles), np.float32)
    select[np.arange(pair_first.size), pair_second * tiles + pair_first] = 1.0
    missing = (1.0 - select.sum(axis=0)).astype(np.int32) * 4096
    cells = jnp.einsum(
        "cxk,kp->cxp", tile_cells.astype(jnp.float32), jnp.asarray(select), precision=highest
    )
    cells = jnp.round(cells).astype(jnp.int32) + jnp.asarray(missing)
    weights = jnp.stack(
        [separation_table(first_chan + i, divisor, kernel_table)[::-1] for i in range(ch_dev)]
    )
    scaled = weights * norm_factor
    coarse = lax.reduce_precision(scaled, 8, 7)
    rest = (scaled - coarse).astype(jnp.bfloat16)
    rows = [shifted_weights(part, cells[:, 0]) for part in (coarse.astype(jnp.bfloat16), rest)]
    place = jnp.arange(UV, dtype=jnp.int32)[None, :, None] - cells[:, 1][:, None, :]
    cols = []
    for v in range(seps):
        placed = jnp.zeros(place.shape, jnp.float32)
        for t in range(PATCH):
            placed = jnp.where(place == t, weights[:, v, t][:, None, None], placed)
        cols.append(placed)
    cols = lax.optimization_barrier(tuple(cols))
    spread_cols = sum(
        cross[:, :, :, v, None, :] * cols[v][:, None, None] for v in range(seps)
    )
    spread_cols = spread_cols.astype(jnp.bfloat16)
    planes = sum(
        jnp.einsum(
            "cdup,cedwp->ucew", part, spread_cols, preferred_element_type=jnp.float32
        )
        for part in rows
    )
    grid_count = lax.axis_size("grid")
    planes = planes.reshape(grid_count, UV // grid_count, ch_dev, 2 * UV).astype(jnp.bfloat16)
    parts = lax.all_to_all(planes, "grid", split_axis=0, concat_axis=0, tiled=True)
    return parts.astype(jnp.float32).sum(axis=0)


f32, bf16, i32 = jnp.float32, jnp.bfloat16, jnp.int32
MESH = pl.DeviceIdType.MESH
SEPS = 2 * SPREAD - 1
STEP = 16
ROWS = 112
LANES = 128
PAIR_ROWS = 256


def iota(shape, axis):
    return lax.broadcasted_iota(i32, shape, axis)


def ones_where(mask, kind=bf16):
    return jnp.where(mask, 1.0, 0.0).astype(kind)


def dot(a, b):
    return lax.dot_general(a, b, (((1,), (0,)), ((), ())), preferred_element_type=f32)


def dot_nt(a, b):
    return lax.dot_general(a, b, (((1,), (1,)), ((), ())), preferred_element_type=f32)


def split(x):
    top = x.astype(bf16)
    return top, (x - top.astype(f32)).astype(bf16)


def send_order(n):
    return sorted(range(1, n), key=lambda k: abs(2 * k - n))


def whole_kernel(
    dims, v_ref, coef_ref, tw_ref, off_ref, cells_ref, off_smem, table_ref, out_ref,
    vext, wide, spec, send, own, vis, left, picks, dsend, recv_ref, drecv_ref,
    perm, bands, vweights, oweights, cols, xs, sums, placed, rs_send, rs_recv,
    in_sem, halo_send, halo_recv, send_sem, recv_sem, dsend_sem, drecv_sem,
    rs_send_sem, rs_recv_sem,
):
    n_stn, n_grid, chans, taps, frame_len, st = dims
    me, here = lax.axis_index("stn"), lax.axis_index("grid")
    reach = (STEP + taps) * frame_len
    halo = taps * frame_len
    samples = v_ref.shape[1]
    blocks = samples // (STEP * frame_len)
    order = send_order(n_stn)

    barrier = pltpu.get_barrier_semaphore()
    for k in range(1, n_stn):
        pl.semaphore_signal(
            barrier, inc=1, device_id=(lax.rem(me + k, n_stn), here), device_id_type=MESH
        )
    for k in range(1, n_grid):
        pl.semaphore_signal(
            barrier, inc=1, device_id=(me, lax.rem(here + k, n_grid)), device_id_type=MESH
        )
    load = pltpu.make_async_copy(v_ref, vext.at[:, pl.ds(halo, samples)], in_sem)
    load.start()

    coef = coef_ref[...]
    line = jnp.concatenate(
        [jnp.zeros((1, frame_len), f32)]
        + [coef[k : k + 1, :] for k in range(taps)]
        + [jnp.zeros((1, reach - (taps + 1) * frame_len), f32)],
        axis=1,
    )
    shifted_line = jnp.concatenate(
        [line if f == 0 else pltpu.roll(line, f * frame_len, 1) for f in range(STEP)], axis=0
    )

    def build(c):
        for r in range(2 * n_stn * c, 2 * n_stn * (c + 1)):
            wide[r * STEP : (r + 1) * STEP, :] = (tw_ref[r : r + 1, :] * shifted_line).astype(bf16)

    build(0)

    offs = off_ref[...].astype(f32)
    stations = offs.shape[1]
    cls = jnp.broadcast_to(SPREAD * offs[0:1] + offs[1:2], (16, stations)).astype(bf16)
    kap = jnp.broadcast_to(SEPS * offs[0:1] + offs[1:2], (LANES, stations)).astype(bf16)
    row_of = (stations, LANES)
    mine = ones_where(iota(row_of, 0) == me * st + iota(row_of, 1) // 2)
    cls_line = dot(cls, mine)[0:1]
    lane = iota((1, LANES), 1)
    code = ((lane % 2) * 2 + lane // 2 // TILE).astype(f32) * CLASSES + cls_line
    line_a = iota((ROWS, LANES), 0).astype(f32)
    sum_rows = ones_where(line_a == code)
    line_b = iota((LANES, LANES), 0)
    lane_b = iota((LANES, LANES), 1)
    own_rows = ones_where(line_b == (lane_b % 2) * st + lane_b // 2)
    gather_rows = jnp.concatenate([sum_rows, own_rows], axis=0)

    pl.semaphore_wait(barrier, n_stn + n_grid - 2)

    @pl.when(here < n_grid - 1)
    def _():
        pltpu.make_async_remote_copy(
            src_ref=v_ref.at[:, pl.ds(samples - halo, halo)],
            dst_ref=vext.at[:, pl.ds(0, halo)],
            send_sem=halo_send,
            recv_sem=halo_recv,
            device_id=(me, here + 1),
            device_id_type=MESH,
        ).start()

    load.wait()

    def filtered(c, t):
        rows = wide[c * 2 * n_stn * STEP : (c + 1) * 2 * n_stn * STEP, :]
        window = vext[:, t * STEP * frame_len : t * STEP * frame_len + reach]
        got = dot_nt(rows, window).astype(bf16)
        spec[c, :, :, t] = got.reshape(n_stn, 2, STEP, LANES)

    for t in range(1, blocks):
        filtered(0, t)

    halo_copy = pltpu.make_async_remote_copy(
        src_ref=v_ref.at[:, pl.ds(samples - halo, halo)],
        dst_ref=vext.at[:, pl.ds(0, halo)],
        send_sem=halo_send,
        recv_sem=halo_recv,
        device_id=(me, lax.rem(here + 1, n_grid)),
        device_id_type=MESH,
    )

    @pl.when(here > 0)
    def _():
        halo_copy.wait_recv()

    @pl.when(here == 0)
    def _():
        vext[:, 0:halo] = jnp.zeros((LANES, halo), bf16)

    copies, arrivals = [], []

    def summed(c, k):
        to = lax.rem(me + k, n_stn)
        got = dot_nt(gather_rows, spec[c, to].reshape(LANES, LANES))
        alone = got[ROWS:].astype(bf16)
        own[c, to] = jnp.concatenate([alone[:st], alone[st:]], axis=1)
        send[c, to] = got[:ROWS].astype(bf16)
        if not k:
            recv_ref[c, me] = send[c, me]

    def sent(c, k):
        to = lax.rem(me + k, n_stn)
        copy = pltpu.make_async_remote_copy(
            src_ref=send.at[c, to],
            dst_ref=recv_ref.at[c, me],
            send_sem=send_sem.at[c, k],
            recv_sem=recv_sem.at[c, k],
            device_id=(to, here),
            device_id_type=MESH,
        )
        copy.start()
        copies.append(copy)
        arrivals[c].append(copy)

    for c in range(chans):
        if c:
            build(c)
        for t in range(blocks) if c else (0,):
            filtered(c, t)
        arrivals.append([])
        for k in order:
            summed(c, k)
            if c < chans - 1:
                sent(c, k)
        summed(c, 0)

    vis[...] = jnp.zeros(vis.shape, f32)
    lane2 = iota((st, 2 * LANES), 1)
    flip = jnp.where(lane2 % LANES < LANES // 2, 1.0, -1.0)
    for c in range(chans):
        for d in range(n_stn):
            x = own[c, d]
            xf = x.astype(f32)
            turned = jnp.concatenate(
                [
                    pltpu.roll(xf[:, p * LANES : (p + 1) * LANES], LANES // 2, 1)
                    for p in range(2)
                ],
                axis=1,
            )
            both = jnp.concatenate([x, (turned * flip).astype(bf16)], axis=0)
            got = dot_nt(both, jnp.concatenate([x, x], axis=0))
            for e in range(2):
                vis[d * 8 + c * 2 + e] = got[e * st : (e + 1) * st]

    half = n_stn * 8
    lane3 = iota((half, LANES), 1)
    for k in range(TILE // 2):
        even = jnp.where(lane3 % st < TILE, vis[:, 2 * k, :], vis[:, 2 * k + TILE, :])
        odd = jnp.where(lane3 % st < TILE, vis[:, 2 * k + 1, :], vis[:, 2 * k + 1 + TILE, :])
        top, low = split(jnp.where(lane3 < st, even, odd))
        left[0:half, k * LANES : (k + 1) * LANES] = top
        left[half:, k * LANES : (k + 1) * LANES] = low
    which = (st, stations)
    kap_col = dot_nt(ones_where(iota(which, 1) == me * st + iota(which, 0)), kap)
    base = kap_col.astype(i32) + iota((st, LANES), 1) - (SEPS * (SPREAD - 1) + SPREAD - 1)
    blank = jnp.zeros((TILE, LANES), bf16)
    row_t = iota((TILE, LANES), 0)
    for i in range(TILE):
        for a in range(2):
            at = me * st + a * TILE + i
            value = off_smem[0, at] * SEPS + off_smem[1, at]
            hit = ones_where((base[a * TILE : (a + 1) * TILE] == value) & (row_t > i))
            first = i * st + a * TILE
            picks[first : first + TILE, a * LANES : (a + 1) * LANES] = hit
            picks[first : first + TILE, (1 - a) * LANES : (2 - a) * LANES] = blank
    binned = dot(left[...], picks[...])
    binned = binned[:half] + binned[half:]
    dsend[...] = jnp.concatenate(
        [
            binned[:, a * LANES : (a + 1) * LANES].reshape(n_stn, 8, LANES)
            for a in range(2)
        ],
        axis=1,
    ).astype(bf16)
    own_arrivals = []
    for k in order:
        to = lax.rem(me + k, n_stn)
        copy = pltpu.make_async_remote_copy(
            src_ref=dsend.at[to],
            dst_ref=drecv_ref.at[me],
            send_sem=dsend_sem.at[k],
            recv_sem=drecv_sem.at[k],
            device_id=(to, here),
            device_id_type=MESH,
        )
        copy.start()
        copies.append(copy)
        own_arrivals.append(copy)
    drecv_ref[me] = dsend[me]
    for k in order:
        sent(chans - 1, k)

    tiles = 2 * n_stn
    over, kern = table_ref.shape
    divisor = frame_len - 1
    side = SPREAD * tiles
    full = SPREAD * side
    depth = 2 * LANES
    across_w = tiles * PATCH

    shape = (perm.shape[1], perm.shape[2])
    r, col = iota(shape, 0), iota(shape, 1)
    b, q = r % tiles, r // tiles
    for p in range(2):
        want = (b // 2) * ROWS + (p * 2 + b % 2) * CLASSES + q
        perm[p] = ones_where((col == want) & (r < full))

    npair = cells_ref.shape[2]

    def pair_number(a, b):
        return jnp.where(a <= b, a * tiles - a * (a - 1) // 2 + b - a, -1)

    kl = (npair, PAIR_ROWS)
    choose = ones_where(iota(kl, 0) == pair_number(iota(kl, 1) // tiles, iota(kl, 1) % tiles))
    kr = (PAIR_ROWS, npair)
    choose_t = ones_where(iota(kr, 1) == pair_number(iota(kr, 0) // tiles, iota(kr, 0) % tiles))
    lane_pair = iota((1, PAIR_ROWS), 1)
    absent = jnp.where(lane_pair // tiles <= lane_pair % tiles, 0.0, -1000.0)

    def weight_rows(c, d, r):
        scaled = (d * (me * chans + c + frame_len // 2)).astype(f32)
        cell = jnp.floor((scaled + 0.5) / divisor)
        rest = scaled - cell * divisor
        fine = jnp.floor((rest * over + 0.5) / divisor)
        tap = r - cell.astype(i32)
        code = jnp.where((tap >= 0) & (tap < kern), fine.astype(i32) * kern + tap, -1)
        got = jnp.zeros(code.shape, f32)
        for o in range(over):
            for t in range(kern):
                got = jnp.where(code == o * kern + t, table_ref[o, t], got)
        return got

    placed[...] = jnp.zeros(placed.shape, bf16)
    norm = 1.0 / (n_grid * depth // 2)
    rows_t = (16, UV)
    rows_w = (16, across_w)
    same_tile = iota((tiles, across_w), 0) == iota((tiles, across_w), 1) // PATCH
    own_lane = iota((32, LANES), 1) // SEPS
    lane_p = (2 * tiles, LANES)
    for c in range(chans):
        cells = cells_ref[c].astype(f32)
        row_line = dot(jnp.broadcast_to(cells[0:1], (16, npair)).astype(bf16), choose)[0:1] + absent
        cols[c] = dot_nt(choose_t, jnp.broadcast_to(cells[1:2], (LANES, npair)).astype(bf16))
        spot = iota((UV, PAIR_ROWS), 0).astype(f32) == row_line
        spots = ones_where(spot)
        lines = weight_rows(c, iota(rows_t, 0), (UV - iota(rows_t, 1)) % UV)
        for du in range(SEPS):
            band = pltpu.roll(
                jnp.broadcast_to(lines[du : du + 1], (UV, UV)), 0, 1, stride=1, stride_axis=0
            )
            top, low = split(band)
            bands[c, du] = dot(jnp.concatenate([top, low], axis=0), spots).astype(bf16)
        across = weight_rows(c, iota(rows_w, 0), iota(rows_w, 1) % PATCH)
        for s in range(SPREAD):
            for q in range(SPREAD):
                at = q - s + SPREAD - 1
                part = jnp.where(same_tile, across[at : at + 1], 0.0)
                top, low = split(part)
                vweights[c, 0, s, q * tiles : (q + 1) * tiles, :] = top
                vweights[c, 1, s, q * tiles : (q + 1) * tiles, :] = low
            vweights[c, 0, s, side:, :] = jnp.zeros((LANES - side, across_w), bf16)
            vweights[c, 1, s, side:, :] = jnp.zeros((LANES - side, across_w), bf16)
        onto = ones_where(iota((LANES, 16), 0) % SEPS == iota((LANES, 16), 1))
        a_top, a_low = split(across)
        oweights[c, 0] = dot(onto, a_top).astype(bf16)
        oweights[c, 1] = dot(onto, a_low).astype(bf16)

    reduced = []
    for c in range(chans):
        for copy in arrivals[c]:
            copy.wait_recv()
        if c == 0:
            for copy in own_arrivals:
                copy.wait_recv()

        got = recv_ref[c].reshape(n_stn * ROWS, LANES)
        lane_h = iota((full, LANES), 1) < LANES // 2
        turned = []
        for p in range(2):
            x = dot(perm[p], got)
            xs[:, p * LANES : (p + 1) * LANES] = x.astype(bf16)
            y = pltpu.roll(x[:full], LANES // 2, 1)
            turned.append(jnp.where(lane_h, -y, y).astype(bf16))
        lefts = [xs[:full], jnp.concatenate(turned, axis=1)]
        for e in range(2):
            blocks = [dot_nt(lefts[e], xs[q * side : q * side + LANES]) for q in range(SPREAD)]
            for du in range(SEPS):
                d = du - (SPREAD - 1)
                total = sum(
                    blocks[s + d][s * side : (s + 1) * side]
                    for s in range(SPREAD)
                    if 0 <= s + d < SPREAD
                )
                top, low = split(total)
                at = (e * SEPS + du) * tiles
                for s in range(SPREAD):
                    sums[0, s, at : at + tiles, :] = top[s * tiles : (s + 1) * tiles]
                    sums[1, s, at : at + tiles, :] = low[s * tiles : (s + 1) * tiles]
        patches = jnp.zeros((2 * SEPS * tiles, across_w), f32)
        for s in range(SPREAD):
            for i, j in ((0, 0), (1, 0), (0, 1)):
                patches = patches + dot(sums[i, s], vweights[c, j, s])

        rr, cc = iota((32, n_stn * 16), 0), iota((32, n_stn * 16), 1)
        b = rr % tiles
        take = ones_where(cc == (b // 2) * 16 + (b % 2) * 8 + c * 2 + rr // tiles)
        mine = dot(take, drecv_ref[...].reshape(n_stn * 16, LANES))
        own_parts = []
        for e in range(2):
            for du in range(SEPS):
                own_parts.append(
                    jnp.where(own_lane == du, mine, 0.0)[e * tiles : (e + 1) * tiles]
                )
        own_all = jnp.concatenate(own_parts, axis=0)
        o_top, o_low = split(own_all)
        own_patch = (
            dot(o_top, oweights[c, 0]) + dot(o_low, oweights[c, 0]) + dot(o_top, oweights[c, 1])
        )
        rr, cc = iota(patches.shape, 0), iota(patches.shape, 1)
        patches = jnp.where(rr % tiles == cc // PATCH, own_patch, patches)

        for a in range(tiles):
            low_rows = 8 if a >= 8 else 0
            distance = iota((tiles, LANES), 1) - cols[c, a * tiles : (a + 1) * tiles].astype(i32)
            distance = distance[low_rows:]
            valid = (distance >= 0) & (distance < PATCH)
            index = jnp.where(valid, distance + (a % 8) * PATCH, 0)
            for du in range(SEPS):
                for e in range(2):
                    at = (e * SEPS + du) * tiles
                    source = patches[
                        at + low_rows : at + tiles, a // 8 * LANES : (a // 8 + 1) * LANES
                    ]
                    moved = jnp.where(valid, jnp.take_along_axis(source, index, axis=1), 0.0)
                    if low_rows:
                        moved = jnp.concatenate([jnp.zeros((8, LANES), f32), moved], axis=0)
                    placed[du, a * tiles : (a + 1) * tiles, e * LANES : (e + 1) * LANES] = (
                        moved.astype(bf16)
                    )
        plane = jnp.zeros((2 * UV, 2 * UV), f32)
        for du in range(SEPS):
            plane = plane + dot(bands[c, du], placed[du])
        plane = (plane[:UV] + plane[UV:]) * norm
        rs_send[c] = plane.astype(bf16).reshape(n_grid, UV // n_grid, 2 * UV)
        for k in range(1, n_grid):
            to = lax.rem(here + k, n_grid)
            copy = pltpu.make_async_remote_copy(
                src_ref=rs_send.at[c, to],
                dst_ref=rs_recv.at[c, k],
                send_sem=rs_send_sem.at[c, k],
                recv_sem=rs_recv_sem.at[c, k],
                device_id=(me, to),
                device_id_type=MESH,
            )
            copy.start()
            reduced.append(copy)

    for c in range(chans):
        total = rs_send[c, here].astype(f32)
        for k in range(1, n_grid):
            reduced[c * (n_grid - 1) + k - 1].wait_recv()
            total = total + rs_recv[c, k].astype(f32)
        out_ref[c] = total
    for copy in copies + reduced:
        copy.wait_send()

    @pl.when(here < n_grid - 1)
    def _():
        halo_copy.wait_send()


def kernel_body(voltages, pfb_coeffs, station_offsets, tile_cells, kernel_table):
    st, pols, samples = voltages.shape
    taps, frame_len = pfb_coeffs.shape
    n_stn, n_grid = lax.axis_size("stn"), lax.axis_size("grid")
    chans = tile_cells.shape[0]
    dims = (n_stn, n_grid, chans, taps, frame_len, st)
    reach = (STEP + taps) * frame_len
    blocks = samples // (STEP * frame_len)

    table = dft_table(frame_len).astype(f32).T.reshape(n_stn, chans, 2, frame_len)
    table = jnp.transpose(table, (1, 0, 2, 3)).reshape(-1, frame_len)
    table = jnp.tile(table, (1, STEP + taps))
    vmem = pl.BlockSpec(memory_space=pltpu.VMEM)
    smem = pl.BlockSpec(memory_space=pltpu.SMEM)
    anywhere = pl.BlockSpec(memory_space=pl.ANY)
    flat = voltages.reshape(st * pols, samples)
    tiles = 2 * n_stn
    full = SPREAD * SPREAD * tiles
    strip = UV // n_grid
    summed = pl.pallas_call(
        functools.partial(whole_kernel, dims),
        out_shape=jax.ShapeDtypeStruct((chans, strip, 2 * UV), f32),
        in_specs=[anywhere, vmem, vmem, vmem, vmem, smem, smem],
        out_specs=vmem,
        scratch_shapes=[
            pltpu.VMEM((LANES, taps * frame_len + samples), bf16),
            pltpu.VMEM((2 * n_stn * chans * STEP, reach), bf16),
            pltpu.VMEM((chans, n_stn, 2, blocks, STEP, LANES), bf16),
            pltpu.VMEM((chans, n_stn, ROWS, LANES), bf16),
            pltpu.VMEM((chans, n_stn, st, 2 * LANES), bf16),
            pltpu.VMEM((n_stn * 8, st, LANES), f32),
            pltpu.VMEM((n_stn * 16, TILE * st), bf16),
            pltpu.VMEM((TILE * st, 2 * LANES), bf16),
            pltpu.VMEM((n_stn, 16, LANES), bf16),
            pltpu.VMEM((chans, n_stn, ROWS, LANES), bf16),
            pltpu.VMEM((n_stn, 16, LANES), bf16),
            pltpu.VMEM((2, full + 48, n_stn * ROWS), bf16),
            pltpu.VMEM((chans, SEPS, 2 * UV, PAIR_ROWS), bf16),
            pltpu.VMEM((chans, 2, SPREAD, LANES, tiles * PATCH), bf16),
            pltpu.VMEM((chans, 2, LANES, tiles * PATCH), bf16),
            pltpu.VMEM((chans, PAIR_ROWS, LANES), f32),
            pltpu.VMEM((full + 48, 2 * LANES), bf16),
            pltpu.VMEM((2, SPREAD, 2 * SEPS * tiles, LANES), bf16),
            pltpu.VMEM((SEPS, PAIR_ROWS, 2 * UV), bf16),
            pltpu.VMEM((chans, n_grid, strip, 2 * UV), bf16),
            pltpu.VMEM((chans, n_grid, strip, 2 * UV), bf16),
            pltpu.SemaphoreType.DMA,
            pltpu.SemaphoreType.DMA,
            pltpu.SemaphoreType.DMA,
            pltpu.SemaphoreType.DMA((chans, n_stn)),
            pltpu.SemaphoreType.DMA((chans, n_stn)),
            pltpu.SemaphoreType.DMA((n_stn,)),
            pltpu.SemaphoreType.DMA((n_stn,)),
            pltpu.SemaphoreType.DMA((chans, n_grid)),
            pltpu.SemaphoreType.DMA((chans, n_grid)),
        ],
        compiler_params=pltpu.CompilerParams(
            collective_id=0, has_side_effects=True, vmem_limit_bytes=48 << 20
        ),
    )(flat, pfb_coeffs, table, station_offsets, tile_cells, station_offsets, kernel_table)
    return jnp.transpose(summed, (1, 0, 2))


def kernels_fit(mesh, args):
    voltages, pfb_coeffs, offsets, cells, _ = args
    n_stn, n_grid = mesh.shape["stn"], mesh.shape["grid"]
    stations, pols, samples = voltages.shape
    taps, frame_len = pfb_coeffs.shape
    spectra = samples // frame_len // n_grid
    return (
        stations == 2 * TILE * n_stn
        and n_stn == 8
        and pols == 2
        and spectra == 64
        and taps == 16
        and frame_len // 2 == cells.shape[0] == 3 * n_stn
    )


def solution(mesh):
    placed = (P("stn", None, "grid"), P(), P(), P("stn", None, None), P())

    def run(*args):
        inner = kernel_body if kernels_fit(mesh, args) else body
        return jax.shard_map(
            inner, mesh=mesh, in_specs=placed, out_specs=P("grid", "stn", None), check_vma=False
        )(*args)

    return run
```

```python
import functools
import math

import jax
import jax.numpy as jnp
import numpy as np
from jax import lax
from jax.experimental import pallas as pl
from jax.experimental.pallas import tpu as pltpu
from jax.sharding import PartitionSpec as P

TILE = 32
PATCH = 16
SPREAD = 5
UV = 128


highest = lax.Precision.HIGHEST


def shifted(block, axis, distance):
    devices = range(lax.axis_size(axis))
    route = [(i - distance, i) for i in devices if i - distance in devices]
    return lax.ppermute(block, axis, route)


def dft_table(frame_len):
    chan_count = frame_len // 2
    sample_line = jnp.arange(frame_len, dtype=jnp.int32)[:, None]
    chan_line = jnp.arange(chan_count, dtype=jnp.int32)[None, :]
    angles = (sample_line * chan_line % frame_len).astype(jnp.float32) * (2.0 * math.pi / frame_len)
    norm_factor = 1.0 / math.sqrt(frame_len)
    twiddle = jnp.stack([jnp.cos(angles) * norm_factor, -jnp.sin(angles) * norm_factor], axis=2)
    return twiddle.reshape(frame_len, 2 * chan_count).astype(jnp.bfloat16)


CLASSES = SPREAD * SPREAD
high = lax.Precision.HIGH


def fused_filter(coeffs, twiddle, step):
    taps, frame_len = coeffs.shape
    flat = coeffs.reshape(-1)
    columns = [
        jnp.pad(flat, (frame_len * (f + 1), frame_len * (step - 1 - f))) for f in range(step)
    ]
    shifted_coeffs = jnp.stack(columns, axis=0)
    spread = np.kron(np.ones((1, frame_len), np.float32), np.eye(step, dtype=np.float32))
    wide = jnp.einsum("fm,fn->mn", shifted_coeffs, jnp.asarray(spread), precision=highest)
    tiled = jnp.tile(jnp.repeat(twiddle.astype(jnp.float32), step, axis=1), (step + taps, 1))
    return (wide * tiled).astype(jnp.bfloat16)

def separation_table(frequency, divisor, kernel_table):
    over_count = kernel_table.shape[0]
    separation = jnp.arange(2 * SPREAD - 1, dtype=jnp.int32)
    scaled = separation * frequency
    cell_index = scaled // divisor
    fine_index = scaled % divisor * over_count // divisor
    choose = (fine_index[:, None] == jnp.arange(over_count, dtype=jnp.int32)[None, :]).astype(
        jnp.float32
    )
    tap_values = jnp.dot(choose, kernel_table, precision=highest)
    place_rel = jnp.arange(PATCH, dtype=jnp.int32)[None, :] - cell_index[:, None]
    weights = jnp.zeros(place_rel.shape, jnp.float32)
    for tap_index in range(kernel_table.shape[1]):
        weights = weights + tap_values[:, tap_index : tap_index + 1] * (
            place_rel == tap_index
        ).astype(jnp.float32)
    return weights


def shifted_weights(weights, bases):
    place = jnp.arange(UV, dtype=jnp.int32)[None, :, None] - bases[:, None, :]
    taps = jnp.arange(PATCH, dtype=jnp.int32)[None, :, None, None]
    spots = place[:, None] == taps
    if weights.dtype == jnp.float32:
        return jnp.einsum("cdt,ctwp->cdwp", weights, spots.astype(jnp.float32), precision=highest)
    return jnp.einsum(
        "cdt,ctwp->cdwp", weights, spots.astype(jnp.bfloat16), preferred_element_type=jnp.float32
    ).astype(jnp.bfloat16)


def body(voltages, pfb_coeffs, station_offsets, tile_cells, kernel_table):
    stn_local, pol_count, samples = voltages.shape
    tap_count, frame_len = pfb_coeffs.shape
    spec_count = samples // frame_len
    step = 128 // math.gcd(128, frame_len)
    chunks = spec_count // step
    flat = jnp.transpose(voltages, (1, 0, 2))
    earlier = shifted(flat[:, :, samples - tap_count * frame_len :], "grid", 1)
    extended = jnp.concatenate([earlier, flat], axis=2)
    width = step * frame_len
    reach = (step + tap_count) * frame_len
    blocks = jnp.stack(
        [extended[:, :, c * width : c * width + reach] for c in range(chunks)], axis=1
    )
    matrix = fused_filter(pfb_coeffs, dft_table(frame_len), step)
    spectra = jnp.einsum(
        "pcsm,mn->npcs", blocks, matrix, preferred_element_type=jnp.float32
    ).astype(jnp.bfloat16)
    spectra = spectra.reshape(frame_len // 2, 2, step * pol_count * chunks, stn_local)
    spectra, tile_cells = lax.optimization_barrier((spectra, tile_cells))
    turned = lax.all_to_all(spectra, "stn", split_axis=0, concat_axis=3, tiled=True)
    turned = jnp.transpose(turned, (0, 1, 3, 2))
    ch_dev, _, stations, depth = turned.shape
    tiles = stations // TILE
    divisor = frame_len - 1
    first_chan = lax.axis_index("stn") * ch_dev + frame_len // 2
    norm_factor = 1.0 / (pol_count * spec_count * lax.axis_size("grid"))

    classes = (station_offsets[0] * SPREAD + station_offsets[1]).reshape(tiles, TILE)
    hot = classes[:, :, None] == jnp.arange(CLASSES, dtype=jnp.int32)
    hot_low = hot.astype(jnp.bfloat16)
    hot_full = hot.astype(jnp.float32)
    tiled = turned.reshape(ch_dev, 2, tiles, TILE, depth)
    summed = jnp.einsum(
        "aiq,ceaik->ceaqk", hot_low, tiled, preferred_element_type=jnp.float32
    ).astype(jnp.bfloat16)

    def stacked(z):
        real_part, imag_part = z[:, 0], z[:, 1]
        partner = jnp.concatenate([real_part, imag_part], axis=-1)
        turned_partner = jnp.concatenate([imag_part, -real_part], axis=-1)
        return jnp.stack([partner, turned_partner], axis=1), partner

    left, right = stacked(summed)
    shape = (SPREAD, SPREAD, 2 * depth)
    terms = []
    for i in range(ch_dev):
        taps = jnp.transpose(left[i].reshape((2 * tiles,) + shape), (1, 2, 3, 0))
        terms.append(
            lax.conv_general_dilated(
                right[i].reshape((tiles,) + shape),
                taps,
                (1, 1),
                [(SPREAD - 1, SPREAD - 1)] * 2,
                dimension_numbers=("NHWC", "HWIO", "HWNC"),
                preferred_element_type=jnp.float32,
            )
        )
    seps = 2 * SPREAD - 1
    cross = jnp.stack(terms).reshape(ch_dev, seps, seps, tiles, 2, tiles)
    cross = jnp.transpose(cross, (0, 4, 1, 2, 3, 5)).reshape(ch_dev, 2, seps, seps, tiles * tiles)
    own_left, own_right = stacked(tiled)
    own = jnp.einsum("ceaik,cajk->ceaij", own_left, own_right, preferred_element_type=jnp.float32)
    line = np.arange(TILE)
    own = jnp.where(jnp.asarray(line[:, None] < line[None, :]), own, 0.0)
    own = jnp.einsum("aiq,ceaij->ceaqj", hot_full, own, precision=high)
    own = jnp.einsum("ceaqj,ajs->ceasq", own, hot_full, precision=high)
    class_line = np.arange(CLASSES)
    back_u = class_line[:, None] // SPREAD - class_line[None, :] // SPREAD + SPREAD - 1
    back_v = class_line[:, None] % SPREAD - class_line[None, :] % SPREAD + SPREAD - 1
    pick = np.arange(seps * seps) == (back_u * seps + back_v).reshape(-1, 1)
    own = jnp.einsum(
        "ceam,mz->ceza",
        own.reshape(ch_dev, 2, tiles, CLASSES * CLASSES),
        jnp.asarray(pick.astype(np.float32)),
        precision=high,
    )
    diagonal = np.zeros((tiles, tiles * tiles), np.float32)
    diagonal[np.arange(tiles), np.arange(tiles) * (tiles + 1)] = 1.0
    own = jnp.einsum("ceza,ap->cezp", own, jnp.asarray(diagonal), precision=high)
    own = own.reshape(ch_dev, 2, seps, seps, tiles * tiles)
    same = jnp.asarray(diagonal.sum(axis=0) > 0)
    cross = jnp.where(same, own, cross)

    pair_first, pair_second = np.triu_indices(tiles)
    select = np.zeros((pair_first.size, tiles * tiles), np.float32)
    select[np.arange(pair_first.size), pair_second * tiles + pair_first] = 1.0
    missing = (1.0 - select.sum(axis=0)).astype(np.int32) * 4096
    cells = jnp.einsum(
        "cxk,kp->cxp", tile_cells.astype(jnp.float32), jnp.asarray(select), precision=highest
    )
    cells = jnp.round(cells).astype(jnp.int32) + jnp.asarray(missing)
    weights = jnp.stack(
        [separation_table(first_chan + i, divisor, kernel_table)[::-1] for i in range(ch_dev)]
    )
    scaled = weights * norm_factor
    coarse = lax.reduce_precision(scaled, 8, 7)
    rest = (scaled - coarse).astype(jnp.bfloat16)
    rows = [shifted_weights(part, cells[:, 0]) for part in (coarse.astype(jnp.bfloat16), rest)]
    place = jnp.arange(UV, dtype=jnp.int32)[None, :, None] - cells[:, 1][:, None, :]
    cols = []
    for v in range(seps):
        placed = jnp.zeros(place.shape, jnp.float32)
        for t in range(PATCH):
            placed = jnp.where(place == t, weights[:, v, t][:, None, None], placed)
        cols.append(placed)
    cols = lax.optimization_barrier(tuple(cols))
    spread_cols = sum(
        cross[:, :, :, v, None, :] * cols[v][:, None, None] for v in range(seps)
    )
    spread_cols = spread_cols.astype(jnp.bfloat16)
    planes = sum(
        jnp.einsum(
            "cdup,cedwp->ucew", part, spread_cols, preferred_element_type=jnp.float32
        )
        for part in rows
    )
    grid_count = lax.axis_size("grid")
    planes = planes.reshape(grid_count, UV // grid_count, ch_dev, 2 * UV).astype(jnp.bfloat16)
    parts = lax.all_to_all(planes, "grid", split_axis=0, concat_axis=0, tiled=True)
    return parts.astype(jnp.float32).sum(axis=0)


f32, bf16, i32 = jnp.float32, jnp.bfloat16, jnp.int32
MESH = pl.DeviceIdType.MESH
SEPS = 2 * SPREAD - 1
STEP = 16
LANES = 128
SUMS = 2 * CLASSES
PAIR_ROWS = 256


def iota(shape, axis):
    return lax.broadcasted_iota(i32, shape, axis)


def ones_where(mask, kind=bf16):
    return jnp.where(mask, 1.0, 0.0).astype(kind)


def dot(a, b):
    return lax.dot_general(a, b, (((1,), (0,)), ((), ())), preferred_element_type=f32)


def dot_nt(a, b):
    return lax.dot_general(a, b, (((1,), (1,)), ((), ())), preferred_element_type=f32)


def split(x):
    top = x.astype(bf16)
    return top, (x - top.astype(f32)).astype(bf16)


def send_order(n):
    return sorted(range(1, n), key=lambda k: abs(2 * k - n))


def padded(rows):
    return -(-rows // 16) * 16


def channels_of(start, stop):
    return range(start // SUMS, (stop - 1) // SUMS + 1)


def whole_kernel(
    dims, groups, v_ref, coef_ref, tw_ref, off_ref, cells_ref, table_ref, out_ref,
    vext, wide, spec, own, vis, left, picks, dsend, drecv_ref,
    bands, vweights, oweights, cols, xs, sums, placed, rs_send, rs_recv, *rest
):
    n_stn, n_grid, chans, taps, frame_len, st = dims
    n_msg = len(groups)
    sends, recvs, flats = rest[:n_msg], rest[n_msg : 2 * n_msg], rest[2 * n_msg : 3 * n_msg]
    (
        in_sem, halo_send, halo_recv, send_sem, recv_sem, dsend_sem, drecv_sem,
        rs_send_sem, rs_recv_sem,
    ) = rest[3 * n_msg :]
    me, here = lax.axis_index("stn"), lax.axis_index("grid")
    reach = (STEP + taps) * frame_len
    halo = taps * frame_len
    samples = v_ref.shape[1]
    order = send_order(n_stn)

    barrier = pltpu.get_barrier_semaphore()
    for k in range(1, n_stn):
        pl.semaphore_signal(
            barrier, inc=1, device_id=(lax.rem(me + k, n_stn), here), device_id_type=MESH
        )
    for k in range(1, n_grid):
        pl.semaphore_signal(
            barrier, inc=1, device_id=(me, lax.rem(here + k, n_grid)), device_id_type=MESH
        )
    load = pltpu.make_async_copy(v_ref, vext.at[:, pl.ds(halo, samples)], in_sem)
    load.start()

    coef = coef_ref[...]
    line = jnp.concatenate(
        [jnp.zeros((1, frame_len), f32)]
        + [coef[k : k + 1, :] for k in range(taps)]
        + [jnp.zeros((1, reach - (taps + 1) * frame_len), f32)],
        axis=1,
    )
    shifted_line = jnp.concatenate(
        [line if f == 0 else pltpu.roll(line, f * frame_len, 1) for f in range(STEP)], axis=0
    )
    built = set()

    def build(c):
        built.add(c)
        for r in range(2 * n_stn * c, 2 * n_stn * (c + 1)):
            wide[r * STEP : (r + 1) * STEP, :] = (tw_ref[r : r + 1, :] * shifted_line).astype(bf16)

    build(0)

    offs = off_ref[...].astype(f32)
    stations = offs.shape[1]
    cls = jnp.broadcast_to(SPREAD * offs[0:1] + offs[1:2], (16, stations)).astype(bf16)
    kap = jnp.broadcast_to(SEPS * offs[0:1] + offs[1:2], (LANES, stations)).astype(bf16)
    row_of = (stations, LANES)
    mine = ones_where(iota(row_of, 0) == me * st + iota(row_of, 1) // 2)
    cls_line = dot(cls, mine)[0:1]
    kap_line = dot(kap[:16], mine)[0:1]
    lane = iota((1, LANES), 1)
    code = (lane // 2 // TILE).astype(f32) * CLASSES + cls_line

    def class_rows(start, stop):
        lines = iota((padded(stop - start), LANES), 0)
        lines = jnp.where(lines < stop - start, lines + start, -1).astype(f32)
        return jnp.concatenate(
            [ones_where(lines == code + c * SUMS) for c in channels_of(start, stop)], axis=1
        )

    own_rows = ones_where(iota((st, LANES), 0) == iota((st, LANES), 1) // 2)

    pl.semaphore_wait(barrier, n_stn + n_grid - 2)

    @pl.when(here < n_grid - 1)
    def _():
        pltpu.make_async_remote_copy(
            src_ref=v_ref.at[:, pl.ds(samples - halo, halo)],
            dst_ref=vext.at[:, pl.ds(0, halo)],
            send_sem=halo_send,
            recv_sem=halo_recv,
            device_id=(me, here + 1),
            device_id_type=MESH,
        ).start()

    load.wait()
    even = iota((2 * n_stn * STEP, LANES), 1) % 2 == 0

    def filtered(h, c):
        rows = wide[c * 2 * n_stn * STEP : (c + 1) * 2 * n_stn * STEP, :]
        first = 2 * h * STEP * frame_len
        second = first + STEP * frame_len
        window = jnp.concatenate(
            [vext[:, first : first + reach], vext[:, second : second + reach]], axis=0
        )
        got = dot_nt(rows, window)
        for t in range(2):
            part = got[:, t * LANES : (t + 1) * LANES]
            for p in range(2):
                only = jnp.where(even if p == 0 else ~even, part, 0.0).astype(bf16)
                spec[h, :, :, p, t, :, c * LANES : (c + 1) * LANES] = only.reshape(
                    n_stn, 2, STEP, LANES
                )

    copies, arrivals = [], [[] for _ in groups]

    passed = set()

    def made(m, send_now):
        h, start, stop = groups[m]
        for c in channels_of(start, stop):
            if c not in built:
                build(c)
            if (h, c) not in passed:
                passed.add((h, c))
                filtered(h, c)
        cs = channels_of(start, stop)
        pick_rows = class_rows(start, stop)
        for k in order + [0]:
            to = lax.rem(me + k, n_stn)
            block = spec[h, to, :, :, :, :, cs[0] * LANES : (cs[-1] + 1) * LANES]
            got = dot_nt(pick_rows, block.reshape(LANES, len(cs) * LANES)).astype(bf16)
            sends[m][to] = got
            if k and send_now:
                sent(m, k)
        recvs[m][me] = sends[m][me]

    def sent(m, k):
        to = lax.rem(me + k, n_stn)
        copy = pltpu.make_async_remote_copy(
            src_ref=sends[m].at[to],
            dst_ref=recvs[m].at[me],
            send_sem=send_sem.at[m, k],
            recv_sem=recv_sem.at[m, k],
            device_id=(to, here),
            device_id_type=MESH,
        )
        copy.start()
        copies.append(copy)
        arrivals[m].append(copy)

    def kept(h):
        for c in range(chans):
            for d in range(0, n_stn, 2):
                block = spec[h, d : d + 2, :, :, :, :, c * LANES : (c + 1) * LANES]
                got = dot_nt(own_rows, block.reshape(2 * LANES, LANES)).astype(bf16)
                for j in range(2):
                    own[c, d + j, :, h * LANES : (h + 1) * LANES] = got[
                        :, j * LANES : (j + 1) * LANES
                    ]

    early = [m for m, group in enumerate(groups) if group[0] == 1]
    late = [m for m, group in enumerate(groups) if group[0] == 0]
    for m in early:
        made(m, True)
    kept(1)

    halo_copy = pltpu.make_async_remote_copy(
        src_ref=v_ref.at[:, pl.ds(samples - halo, halo)],
        dst_ref=vext.at[:, pl.ds(0, halo)],
        send_sem=halo_send,
        recv_sem=halo_recv,
        device_id=(me, lax.rem(here + 1, n_grid)),
        device_id_type=MESH,
    )

    @pl.when(here > 0)
    def _():
        halo_copy.wait_recv()

    @pl.when(here == 0)
    def _():
        vext[:, 0:halo] = jnp.zeros((LANES, halo), bf16)

    for m in late:
        made(m, m == late[0])
    kept(0)

    half = n_stn * 8
    lane2 = iota((st, 2 * LANES), 1)
    flip = jnp.where(lane2 % LANES < LANES // 2, 1.0, -1.0)
    for c in range(chans, 4):
        for d in range(n_stn):
            vis[d * 8 + c * 2 : d * 8 + c * 2 + 2] = jnp.zeros((2, st, LANES), f32)
    for c in range(chans):
        for d in range(n_stn):
            x = own[c, d]
            xf = x.astype(f32)
            turned = jnp.concatenate(
                [
                    pltpu.roll(xf[:, p * LANES : (p + 1) * LANES], LANES // 2, 1)
                    for p in range(2)
                ],
                axis=1,
            )
            both = jnp.concatenate([x, (turned * flip).astype(bf16)], axis=0)
            got = dot_nt(both, jnp.concatenate([x, x], axis=0))
            for e in range(2):
                vis[d * 8 + c * 2 + e] = got[e * st : (e + 1) * st]
    lane3 = iota((half, LANES), 1)
    for k in range(TILE // 2):
        first = jnp.where(lane3 % st < TILE, vis[:, 2 * k, :], vis[:, 2 * k + TILE, :])
        second = jnp.where(lane3 % st < TILE, vis[:, 2 * k + 1, :], vis[:, 2 * k + 1 + TILE, :])
        left[:, k * LANES : (k + 1) * LANES] = jnp.where(lane3 < st, first, second).astype(bf16)
    which = (st, stations)
    kap_col = dot_nt(ones_where(iota(which, 1) == me * st + iota(which, 0)), kap)
    base = kap_col + iota((st, LANES), 1).astype(f32) - (SEPS * (SPREAD - 1) + SPREAD - 1)
    blank = jnp.zeros((TILE, LANES), bf16)
    row_t = iota((TILE, LANES), 0)
    for i in range(TILE):
        for a in range(2):
            at = 2 * (a * TILE + i)
            value = kap_line[0:1, at : at + 1]
            hit = ones_where((base[a * TILE : (a + 1) * TILE] == value) & (row_t > i))
            first = i * st + a * TILE
            picks[first : first + TILE, a * LANES : (a + 1) * LANES] = hit
            picks[first : first + TILE, (1 - a) * LANES : (2 - a) * LANES] = blank
    binned = dot(left[...], picks[...])
    dsend[...] = jnp.concatenate(
        [
            binned[:, a * LANES : (a + 1) * LANES].reshape(n_stn, 8, LANES)
            for a in range(2)
        ],
        axis=1,
    ).astype(bf16)
    own_arrivals = []
    for k in order:
        to = lax.rem(me + k, n_stn)
        copy = pltpu.make_async_remote_copy(
            src_ref=dsend.at[to],
            dst_ref=drecv_ref.at[me],
            send_sem=dsend_sem.at[k],
            recv_sem=drecv_sem.at[k],
            device_id=(to, here),
            device_id_type=MESH,
        )
        copy.start()
        copies.append(copy)
        own_arrivals.append(copy)
    drecv_ref[me] = dsend[me]
    for k in order:
        sent(late[1], k)

    tiles = 2 * n_stn
    over, kern = table_ref.shape
    divisor = frame_len - 1
    side = SPREAD * tiles
    full = SPREAD * side
    depth = 2 * LANES
    across_w = tiles * PATCH
    npair = cells_ref.shape[2]

    def tile_of(x):
        return 2 * (x % n_stn) + x // n_stn

    def pair_number(x):
        b = tile_of(x % tiles)
        last = x // tiles == tiles - 1
        a = jnp.where(last, b, tile_of(x // tiles))
        return jnp.where((a < b) | last, a * tiles - a * (a - 1) // 2 + b - a, -1)

    choose = ones_where(iota((npair, PAIR_ROWS), 0) == pair_number(iota((1, PAIR_ROWS), 1)))
    choose_t = ones_where(iota((PAIR_ROWS, npair), 1) == pair_number(iota((PAIR_ROWS, 1), 0)))
    absent = jnp.where(pair_number(iota((1, PAIR_ROWS), 1)) < 0, -1000.0, 0.0)

    def weight_rows(c, d, r):
        scaled = (d * (me * chans + c + frame_len // 2)).astype(f32)
        cell = jnp.floor((scaled + 0.5) / divisor)
        rest = scaled - cell * divisor
        fine = jnp.floor((rest * over + 0.5) / divisor)
        tap = r - cell.astype(i32)
        code = jnp.where((tap >= 0) & (tap < kern), fine.astype(i32) * kern + tap, -1)
        got = jnp.zeros(code.shape, f32)
        for o in range(over):
            for t in range(kern):
                got = jnp.where(code == o * kern + t, table_ref[o, t], got)
        return got

    xs[full:, :] = jnp.zeros((xs.shape[0] - full, depth), bf16)
    norm = 1.0 / (n_grid * depth // 2)
    rows_t = (16, UV)
    rows_w = (16, across_w)
    same_tile = iota((tiles, across_w), 0) == iota((tiles, across_w), 1) // PATCH
    own_block = iota((LANES, across_w), 0) // SEPS == iota((LANES, across_w), 1) // PATCH
    onto = ones_where(iota((LANES, 16), 0) % SEPS == iota((LANES, 16), 1))
    for c in range(chans):
        cells = cells_ref[c].astype(f32)
        row_line = dot(jnp.broadcast_to(cells[0:1], (16, npair)).astype(bf16), choose)[0:1] + absent
        cols[c] = dot_nt(choose_t, jnp.broadcast_to(cells[1:2], (LANES, npair)).astype(bf16))
        spots = ones_where(iota((UV, PAIR_ROWS), 0).astype(f32) == row_line)
        lines = weight_rows(c, iota(rows_t, 0), (UV - iota(rows_t, 1)) % UV)
        for du in range(SEPS):
            band = pltpu.roll(
                jnp.broadcast_to(lines[du : du + 1], (UV, UV)), 0, 1, stride=1, stride_axis=0
            )
            top, low = split(band)
            bands[c, :, du * PAIR_ROWS : (du + 1) * PAIR_ROWS] = dot(
                jnp.concatenate([top, low], axis=0), spots
            ).astype(bf16)
        across = weight_rows(c, iota(rows_w, 0), iota(rows_w, 1) % PATCH)
        for at in range(SEPS):
            parts = split(jnp.where(same_tile, across[at : at + 1], 0.0))
            for j in range(2):
                vweights[c, j, at * tiles : (at + 1) * tiles, :] = parts[j]
        for j in range(2):
            vweights[c, j, SEPS * tiles :, :] = jnp.zeros((depth - SEPS * tiles, across_w), bf16)
        for j, part in enumerate(split(across)):
            oweights[c, j] = jnp.where(own_block, dot(onto, part), 0.0).astype(bf16)

    for k in order:
        sent(late[2], k)

    ready = set()
    reduced = []
    lane_h = iota((tiles, LANES), 1) < LANES // 2
    rows_p = 2 * SEPS * tiles
    lane_s = iota((side, LANES), 1) < side
    lane_p = iota((tiles, LANES), 1)

    def found(h, g):
        for m, (half, start, stop) in enumerate(groups):
            if half == h and start <= g < stop:
                if m not in ready:
                    ready.add(m)
                    for copy in arrivals[m]:
                        copy.wait_recv()
                    flats[m][...] = recvs[m][...].astype(f32)
                return flats[m][:, g - start, :]

    def moves(c, a):
        distance = iota((tiles, LANES), 1) - cols[c, a * tiles : (a + 1) * tiles].astype(i32)
        valid = (distance >= 0) & (distance < PATCH)
        return valid, jnp.where(valid, distance, 0)

    def correlated(c):
        turned = []
        for q in range(SPREAD * SPREAD):
            pieces = []
            for h in range(2):
                x = jnp.concatenate(
                    [found(h, c * SUMS + a * CLASSES + q) for a in range(2)], axis=0
                )
                xs[q * tiles : (q + 1) * tiles, h * LANES : (h + 1) * LANES] = x.astype(bf16)
                y = pltpu.roll(x, LANES // 2, 1)
                pieces.append(jnp.where(lane_h, -y, y).astype(bf16))
            turned.append(jnp.concatenate(pieces, axis=1))
        lefts = [xs[:full], jnp.concatenate(turned, axis=0)]
        for e in range(2):
            blocks = []
            for q in range(0, SPREAD, 2):
                names = [r for r in (q, q + 1) if r < SPREAD]
                rights = [xs[r * side : r * side + LANES] for r in names]
                got = dot_nt(lefts[e], jnp.concatenate(rights, axis=0))
                blocks += [got[:, j * LANES : (j + 1) * LANES] for j in range(len(names))]
            for du in range(SEPS):
                d = du - (SPREAD - 1)
                total = sum(
                    blocks[s + d][s * side : (s + 1) * side]
                    for s in range(SPREAD)
                    if 0 <= s + d < SPREAD
                )
                total = jnp.where(lane_s, total, 0.0)
                shifts = [
                    pltpu.roll(
                        total[x * tiles : (x + 1) * tiles], (SPREAD - 1 - x) * tiles, 1
                    )
                    for x in range(SPREAD - 1)
                ]
                wrap = (2 * SPREAD - 1) * tiles - LANES
                main = total[(SPREAD - 1) * tiles :] + jnp.where(lane_p < wrap, 0.0, shifts[0])
                for part in shifts[1:]:
                    main = main + part
                over_part = jnp.where(lane_p < wrap, shifts[0], 0.0)
                top, low = split(jnp.concatenate([main, over_part], axis=1))
                at = (e * SEPS + du) * tiles
                sums[at : at + tiles, :] = top
                sums[rows_p + at : rows_p + at + tiles, :] = low
        patches = dot(sums[...], vweights[c, 0])
        patches = patches[:rows_p] + patches[rows_p:] + dot(sums[:rows_p], vweights[c, 1])

        for a in range(tiles - 1):
            valid, index = moves(c, a)
            index = index + (a % 8) * PATCH
            for du in range(SEPS):
                for e in range(2):
                    at = (e * SEPS + du) * tiles
                    source = patches[at : at + tiles, a // 8 * LANES : (a // 8 + 1) * LANES]
                    moved = jnp.where(valid, jnp.take_along_axis(source, index, axis=1), 0.0)
                    first = du * PAIR_ROWS + a * tiles
                    placed[c, first : first + tiles, e * LANES : (e + 1) * LANES] = moved.astype(
                        bf16
                    )

    def gridded(c):
        rr, cc = iota((32, n_stn * 16), 0), iota((32, n_stn * 16), 1)
        b = rr % tiles
        take = ones_where(cc == (b % n_stn) * 16 + (b // n_stn) * 8 + c * 2 + rr // tiles)
        alone = dot(take, drecv_ref[...].reshape(n_stn * 16, LANES)).astype(bf16)
        alone = dot(alone, oweights[c, 0]) + dot(alone, oweights[c, 1])
        valid, index = moves(c, tiles - 1)
        for du in range(SEPS):
            for e in range(2):
                source = alone[e * tiles : (e + 1) * tiles, du // 8 * LANES : (du // 8 + 1) * LANES]
                moved = jnp.take_along_axis(source, index + (du % 8) * PATCH, axis=1)
                first = du * PAIR_ROWS + (tiles - 1) * tiles
                placed[c, first : first + tiles, e * LANES : (e + 1) * LANES] = jnp.where(
                    valid, moved, 0.0
                ).astype(bf16)
        plane = dot(bands[c], placed[c])
        plane = (plane[:UV] + plane[UV:]) * norm
        rs_send[c] = plane.astype(bf16).reshape(n_grid, UV // n_grid, 2 * UV)
        for k in range(1, n_grid):
            to = lax.rem(here + k, n_grid)
            copy = pltpu.make_async_remote_copy(
                src_ref=rs_send.at[c, to],
                dst_ref=rs_recv.at[c, k],
                send_sem=rs_send_sem.at[c, k],
                recv_sem=rs_recv_sem.at[c, k],
                device_id=(me, to),
                device_id_type=MESH,
            )
            copy.start()
            reduced.append(copy)

    for c in range(chans - 1):
        correlated(c)
    for copy in own_arrivals:
        copy.wait_recv()
    for c in range(chans - 1):
        gridded(c)
    correlated(chans - 1)
    gridded(chans - 1)

    for c in range(chans):
        total = rs_send[c, here].astype(f32)
        for k in range(1, n_grid):
            reduced[c * (n_grid - 1) + k - 1].wait_recv()
            total = total + rs_recv[c, k].astype(f32)
        out_ref[c] = total
    for copy in copies + reduced:
        copy.wait_send()

    @pl.when(here < n_grid - 1)
    def _():
        halo_copy.wait_send()


def kernel_body(voltages, pfb_coeffs, station_offsets, tile_cells, kernel_table):
    st, pols, samples = voltages.shape
    taps, frame_len = pfb_coeffs.shape
    n_stn, n_grid = lax.axis_size("stn"), lax.axis_size("grid")
    chans = tile_cells.shape[0]
    dims = (n_stn, n_grid, chans, taps, frame_len, st)
    reach = (STEP + taps) * frame_len
    whole, first = chans * SUMS, padded(SUMS)
    second = first + padded(2 * SUMS - first)
    third = SUMS // 16 * 16
    groups = (
        (1, 0, third), (1, third, whole), (0, 0, first), (0, first, second), (0, second, whole),
    )

    line = np.arange(frame_len)[:, None] * np.arange(frame_len // 2)[None, :] % frame_len
    angles = line.astype(np.float32) * np.float32(2.0 * math.pi / frame_len)
    scale = np.float32(1.0 / math.sqrt(frame_len))
    table = np.stack([np.cos(angles) * scale, -np.sin(angles) * scale], axis=2)
    table = table.astype(jnp.bfloat16).astype(np.float32)
    table = table.transpose(1, 2, 0).reshape(n_stn, chans, 2, frame_len).transpose(1, 0, 2, 3)
    table = jnp.asarray(np.tile(table.reshape(-1, frame_len), (1, STEP + taps)))
    vmem = pl.BlockSpec(memory_space=pltpu.VMEM)
    smem = pl.BlockSpec(memory_space=pltpu.SMEM)
    anywhere = pl.BlockSpec(memory_space=pl.ANY)
    flat = voltages.reshape(st * pols, samples)
    tiles = 2 * n_stn
    full = SPREAD * SPREAD * tiles
    strip = UV // n_grid
    heights = [padded(stop - start) for _, start, stop in groups]
    summed = pl.pallas_call(
        functools.partial(whole_kernel, dims, groups),
        out_shape=jax.ShapeDtypeStruct((chans, strip, 2 * UV), f32),
        in_specs=[anywhere, vmem, vmem, vmem, vmem, smem],
        out_specs=vmem,
        scratch_shapes=[
            pltpu.VMEM((LANES, taps * frame_len + samples), bf16),
            pltpu.VMEM((2 * n_stn * chans * STEP, reach), bf16),
            pltpu.VMEM((2, n_stn, 2, 2, 2, STEP, chans * LANES), bf16),
            pltpu.VMEM((chans, n_stn, st, 2 * LANES), bf16),
            pltpu.VMEM((n_stn * 8, st, LANES), f32),
            pltpu.VMEM((n_stn * 8, TILE * st), bf16),
            pltpu.VMEM((TILE * st, 2 * LANES), bf16),
            pltpu.VMEM((n_stn, 16, LANES), bf16),
            pltpu.VMEM((n_stn, 16, LANES), bf16),
            pltpu.VMEM((chans, 2 * UV, SEPS * PAIR_ROWS), bf16),
            pltpu.VMEM((chans, 2, 2 * LANES, tiles * PATCH), bf16),
            pltpu.VMEM((chans, 2, LANES, tiles * PATCH), bf16),
            pltpu.VMEM((chans, PAIR_ROWS, LANES), f32),
            pltpu.VMEM((full + 48, 2 * LANES), bf16),
            pltpu.VMEM((4 * SEPS * tiles, 2 * LANES), bf16),
            pltpu.VMEM((chans, SEPS * PAIR_ROWS, 2 * UV), bf16),
            pltpu.VMEM((chans, n_grid, strip, 2 * UV), bf16),
            pltpu.VMEM((chans, n_grid, strip, 2 * UV), bf16),
            *[pltpu.VMEM((n_stn, h, LANES), bf16) for h in heights],
            *[pltpu.VMEM((n_stn, h, LANES), bf16) for h in heights],
            *[pltpu.VMEM((n_stn, h, LANES), f32) for h in heights],
            pltpu.SemaphoreType.DMA,
            pltpu.SemaphoreType.DMA,
            pltpu.SemaphoreType.DMA,
            pltpu.SemaphoreType.DMA((len(groups), n_stn)),
            pltpu.SemaphoreType.DMA((len(groups), n_stn)),
            pltpu.SemaphoreType.DMA((n_stn,)),
            pltpu.SemaphoreType.DMA((n_stn,)),
            pltpu.SemaphoreType.DMA((chans, n_grid)),
            pltpu.SemaphoreType.DMA((chans, n_grid)),
        ],
        compiler_params=pltpu.CompilerParams(
            collective_id=0, has_side_effects=True, vmem_limit_bytes=48 << 20
        ),
    )(flat, pfb_coeffs, table, station_offsets, tile_cells, kernel_table)
    return jnp.transpose(summed, (1, 0, 2))


def kernels_fit(mesh, args):
    voltages, pfb_coeffs, offsets, cells, _ = args
    n_stn, n_grid = mesh.shape["stn"], mesh.shape["grid"]
    stations, pols, samples = voltages.shape
    taps, frame_len = pfb_coeffs.shape
    spectra = samples // frame_len // n_grid
    return (
        stations == 2 * TILE * n_stn
        and n_stn == 8
        and pols == 2
        and spectra == 64
        and taps == 16
        and frame_len // 2 == cells.shape[0] == 3 * n_stn
    )


def solution(mesh):
    placed = (P("stn", None, "grid"), P(), P(), P("stn", None, None), P())

    def run(*args):
        inner = kernel_body if kernels_fit(mesh, args) else body
        return jax.shard_map(
            inner, mesh=mesh, in_specs=placed, out_specs=P("grid", "stn", None), check_vma=False
        )(*args)

    return run
```

```python
import functools
import math

import jax
import jax.numpy as jnp
import numpy as np
from jax import lax
from jax.experimental import pallas as pl
from jax.experimental.pallas import tpu as pltpu
from jax.sharding import PartitionSpec as P

TILE = 32
PATCH = 16
SPREAD = 5
UV = 128


highest = lax.Precision.HIGHEST


def shifted(block, axis, distance):
    devices = range(lax.axis_size(axis))
    route = [(i - distance, i) for i in devices if i - distance in devices]
    return lax.ppermute(block, axis, route)


def dft_table(frame_len):
    chan_count = frame_len // 2
    sample_line = jnp.arange(frame_len, dtype=jnp.int32)[:, None]
    chan_line = jnp.arange(chan_count, dtype=jnp.int32)[None, :]
    angles = (sample_line * chan_line % frame_len).astype(jnp.float32) * (2.0 * math.pi / frame_len)
    norm_factor = 1.0 / math.sqrt(frame_len)
    twiddle = jnp.stack([jnp.cos(angles) * norm_factor, -jnp.sin(angles) * norm_factor], axis=2)
    return twiddle.reshape(frame_len, 2 * chan_count).astype(jnp.bfloat16)


CLASSES = SPREAD * SPREAD
high = lax.Precision.HIGH


def fused_filter(coeffs, twiddle, step):
    taps, frame_len = coeffs.shape
    flat = coeffs.reshape(-1)
    columns = [
        jnp.pad(flat, (frame_len * (f + 1), frame_len * (step - 1 - f))) for f in range(step)
    ]
    shifted_coeffs = jnp.stack(columns, axis=0)
    spread = np.kron(np.ones((1, frame_len), np.float32), np.eye(step, dtype=np.float32))
    wide = jnp.einsum("fm,fn->mn", shifted_coeffs, jnp.asarray(spread), precision=highest)
    tiled = jnp.tile(jnp.repeat(twiddle.astype(jnp.float32), step, axis=1), (step + taps, 1))
    return (wide * tiled).astype(jnp.bfloat16)

def separation_table(frequency, divisor, kernel_table):
    over_count = kernel_table.shape[0]
    separation = jnp.arange(2 * SPREAD - 1, dtype=jnp.int32)
    scaled = separation * frequency
    cell_index = scaled // divisor
    fine_index = scaled % divisor * over_count // divisor
    choose = (fine_index[:, None] == jnp.arange(over_count, dtype=jnp.int32)[None, :]).astype(
        jnp.float32
    )
    tap_values = jnp.dot(choose, kernel_table, precision=highest)
    place_rel = jnp.arange(PATCH, dtype=jnp.int32)[None, :] - cell_index[:, None]
    weights = jnp.zeros(place_rel.shape, jnp.float32)
    for tap_index in range(kernel_table.shape[1]):
        weights = weights + tap_values[:, tap_index : tap_index + 1] * (
            place_rel == tap_index
        ).astype(jnp.float32)
    return weights


def shifted_weights(weights, bases):
    place = jnp.arange(UV, dtype=jnp.int32)[None, :, None] - bases[:, None, :]
    taps = jnp.arange(PATCH, dtype=jnp.int32)[None, :, None, None]
    spots = place[:, None] == taps
    if weights.dtype == jnp.float32:
        return jnp.einsum("cdt,ctwp->cdwp", weights, spots.astype(jnp.float32), precision=highest)
    return jnp.einsum(
        "cdt,ctwp->cdwp", weights, spots.astype(jnp.bfloat16), preferred_element_type=jnp.float32
    ).astype(jnp.bfloat16)


def body(voltages, pfb_coeffs, station_offsets, tile_cells, kernel_table):
    stn_local, pol_count, samples = voltages.shape
    tap_count, frame_len = pfb_coeffs.shape
    spec_count = samples // frame_len
    step = 128 // math.gcd(128, frame_len)
    chunks = spec_count // step
    flat = jnp.transpose(voltages, (1, 0, 2))
    earlier = shifted(flat[:, :, samples - tap_count * frame_len :], "grid", 1)
    extended = jnp.concatenate([earlier, flat], axis=2)
    width = step * frame_len
    reach = (step + tap_count) * frame_len
    blocks = jnp.stack(
        [extended[:, :, c * width : c * width + reach] for c in range(chunks)], axis=1
    )
    matrix = fused_filter(pfb_coeffs, dft_table(frame_len), step)
    spectra = jnp.einsum(
        "pcsm,mn->npcs", blocks, matrix, preferred_element_type=jnp.float32
    ).astype(jnp.bfloat16)
    spectra = spectra.reshape(frame_len // 2, 2, step * pol_count * chunks, stn_local)
    spectra, tile_cells = lax.optimization_barrier((spectra, tile_cells))
    turned = lax.all_to_all(spectra, "stn", split_axis=0, concat_axis=3, tiled=True)
    turned = jnp.transpose(turned, (0, 1, 3, 2))
    ch_dev, _, stations, depth = turned.shape
    tiles = stations // TILE
    divisor = frame_len - 1
    first_chan = lax.axis_index("stn") * ch_dev + frame_len // 2
    norm_factor = 1.0 / (pol_count * spec_count * lax.axis_size("grid"))

    classes = (station_offsets[0] * SPREAD + station_offsets[1]).reshape(tiles, TILE)
    hot = classes[:, :, None] == jnp.arange(CLASSES, dtype=jnp.int32)
    hot_low = hot.astype(jnp.bfloat16)
    hot_full = hot.astype(jnp.float32)
    tiled = turned.reshape(ch_dev, 2, tiles, TILE, depth)
    summed = jnp.einsum(
        "aiq,ceaik->ceaqk", hot_low, tiled, preferred_element_type=jnp.float32
    ).astype(jnp.bfloat16)

    def stacked(z):
        real_part, imag_part = z[:, 0], z[:, 1]
        partner = jnp.concatenate([real_part, imag_part], axis=-1)
        turned_partner = jnp.concatenate([imag_part, -real_part], axis=-1)
        return jnp.stack([partner, turned_partner], axis=1), partner

    left, right = stacked(summed)
    shape = (SPREAD, SPREAD, 2 * depth)
    terms = []
    for i in range(ch_dev):
        taps = jnp.transpose(left[i].reshape((2 * tiles,) + shape), (1, 2, 3, 0))
        terms.append(
            lax.conv_general_dilated(
                right[i].reshape((tiles,) + shape),
                taps,
                (1, 1),
                [(SPREAD - 1, SPREAD - 1)] * 2,
                dimension_numbers=("NHWC", "HWIO", "HWNC"),
                preferred_element_type=jnp.float32,
            )
        )
    seps = 2 * SPREAD - 1
    cross = jnp.stack(terms).reshape(ch_dev, seps, seps, tiles, 2, tiles)
    cross = jnp.transpose(cross, (0, 4, 1, 2, 3, 5)).reshape(ch_dev, 2, seps, seps, tiles * tiles)
    own_left, own_right = stacked(tiled)
    own = jnp.einsum("ceaik,cajk->ceaij", own_left, own_right, preferred_element_type=jnp.float32)
    line = np.arange(TILE)
    own = jnp.where(jnp.asarray(line[:, None] < line[None, :]), own, 0.0)
    own = jnp.einsum("aiq,ceaij->ceaqj", hot_full, own, precision=high)
    own = jnp.einsum("ceaqj,ajs->ceasq", own, hot_full, precision=high)
    class_line = np.arange(CLASSES)
    back_u = class_line[:, None] // SPREAD - class_line[None, :] // SPREAD + SPREAD - 1
    back_v = class_line[:, None] % SPREAD - class_line[None, :] % SPREAD + SPREAD - 1
    pick = np.arange(seps * seps) == (back_u * seps + back_v).reshape(-1, 1)
    own = jnp.einsum(
        "ceam,mz->ceza",
        own.reshape(ch_dev, 2, tiles, CLASSES * CLASSES),
        jnp.asarray(pick.astype(np.float32)),
        precision=high,
    )
    diagonal = np.zeros((tiles, tiles * tiles), np.float32)
    diagonal[np.arange(tiles), np.arange(tiles) * (tiles + 1)] = 1.0
    own = jnp.einsum("ceza,ap->cezp", own, jnp.asarray(diagonal), precision=high)
    own = own.reshape(ch_dev, 2, seps, seps, tiles * tiles)
    same = jnp.asarray(diagonal.sum(axis=0) > 0)
    cross = jnp.where(same, own, cross)

    pair_first, pair_second = np.triu_indices(tiles)
    select = np.zeros((pair_first.size, tiles * tiles), np.float32)
    select[np.arange(pair_first.size), pair_second * tiles + pair_first] = 1.0
    missing = (1.0 - select.sum(axis=0)).astype(np.int32) * 4096
    cells = jnp.einsum(
        "cxk,kp->cxp", tile_cells.astype(jnp.float32), jnp.asarray(select), precision=highest
    )
    cells = jnp.round(cells).astype(jnp.int32) + jnp.asarray(missing)
    weights = jnp.stack(
        [separation_table(first_chan + i, divisor, kernel_table)[::-1] for i in range(ch_dev)]
    )
    scaled = weights * norm_factor
    coarse = lax.reduce_precision(scaled, 8, 7)
    rest = (scaled - coarse).astype(jnp.bfloat16)
    rows = [shifted_weights(part, cells[:, 0]) for part in (coarse.astype(jnp.bfloat16), rest)]
    place = jnp.arange(UV, dtype=jnp.int32)[None, :, None] - cells[:, 1][:, None, :]
    cols = []
    for v in range(seps):
        placed = jnp.zeros(place.shape, jnp.float32)
        for t in range(PATCH):
            placed = jnp.where(place == t, weights[:, v, t][:, None, None], placed)
        cols.append(placed)
    cols = lax.optimization_barrier(tuple(cols))
    spread_cols = sum(
        cross[:, :, :, v, None, :] * cols[v][:, None, None] for v in range(seps)
    )
    spread_cols = spread_cols.astype(jnp.bfloat16)
    planes = sum(
        jnp.einsum(
            "cdup,cedwp->ucew", part, spread_cols, preferred_element_type=jnp.float32
        )
        for part in rows
    )
    grid_count = lax.axis_size("grid")
    planes = planes.reshape(grid_count, UV // grid_count, ch_dev, 2 * UV).astype(jnp.bfloat16)
    parts = lax.all_to_all(planes, "grid", split_axis=0, concat_axis=0, tiled=True)
    return parts.astype(jnp.float32).sum(axis=0)


f32, bf16, i32 = jnp.float32, jnp.bfloat16, jnp.int32
MESH = pl.DeviceIdType.MESH
SEPS = 2 * SPREAD - 1
STEP = 16
LANES = 128
SUMS = 2 * CLASSES
PAIR_ROWS = 256


def iota(shape, axis):
    return lax.broadcasted_iota(i32, shape, axis)


def ones_where(mask, kind=bf16):
    return jnp.where(mask, 1.0, 0.0).astype(kind)


def dot(a, b):
    return lax.dot_general(a, b, (((1,), (0,)), ((), ())), preferred_element_type=f32)


def dot_nt(a, b):
    return lax.dot_general(a, b, (((1,), (1,)), ((), ())), preferred_element_type=f32)


def split(x):
    top = x.astype(bf16)
    return top, (x - top.astype(f32)).astype(bf16)


def send_order(n):
    return sorted(range(1, n), key=lambda k: abs(2 * k - n))


def padded(rows):
    return -(-rows // 16) * 16


def channels_of(start, stop):
    return range(start // SUMS, (stop - 1) // SUMS + 1)


def whole_kernel(
    dims, groups, v_ref, coef_ref, tw_ref, off_ref, cells_ref, table_ref, out_ref,
    vext, wide, spec, own, vis, left, picks, dsend, drecv_ref,
    bands, vweights, oweights, cols, xs, sums, placed, rs_send, rs_recv, *rest
):
    n_stn, n_grid, chans, taps, frame_len, st = dims
    n_msg = len(groups)
    sends, recvs, flats = rest[:n_msg], rest[n_msg : 2 * n_msg], rest[2 * n_msg : 3 * n_msg]
    (
        in_sem, halo_send, halo_recv, send_sem, recv_sem, dsend_sem, drecv_sem,
        rs_send_sem, rs_recv_sem,
    ) = rest[3 * n_msg :]
    me, here = lax.axis_index("stn"), lax.axis_index("grid")
    reach = (STEP + taps) * frame_len
    halo = taps * frame_len
    samples = v_ref.shape[1]
    order = send_order(n_stn)

    barrier = pltpu.get_barrier_semaphore()
    for k in range(1, n_stn):
        pl.semaphore_signal(
            barrier, inc=1, device_id=(lax.rem(me + k, n_stn), here), device_id_type=MESH
        )
    for k in range(1, n_grid):
        pl.semaphore_signal(
            barrier, inc=1, device_id=(me, lax.rem(here + k, n_grid)), device_id_type=MESH
        )
    load = pltpu.make_async_copy(v_ref, vext.at[:, pl.ds(halo, samples)], in_sem)
    load.start()

    coef = coef_ref[...]
    line = jnp.concatenate(
        [jnp.zeros((1, frame_len), f32)]
        + [coef[k : k + 1, :] for k in range(taps)]
        + [jnp.zeros((1, reach - (taps + 1) * frame_len), f32)],
        axis=1,
    )
    shifted_line = jnp.concatenate(
        [line if f == 0 else pltpu.roll(line, f * frame_len, 1) for f in range(STEP)], axis=0
    )
    built = set()

    def build(c):
        built.add(c)
        for r in range(2 * n_stn * c, 2 * n_stn * (c + 1)):
            wide[r * STEP : (r + 1) * STEP, :] = (tw_ref[r : r + 1, :] * shifted_line).astype(bf16)

    build(0)

    offs = off_ref[...].astype(f32)
    stations = offs.shape[1]
    cls = jnp.broadcast_to(SPREAD * offs[0:1] + offs[1:2], (16, stations)).astype(bf16)
    kap = jnp.broadcast_to(SEPS * offs[0:1] + offs[1:2], (LANES, stations)).astype(bf16)
    row_of = (stations, LANES)
    mine = ones_where(iota(row_of, 0) == me * st + iota(row_of, 1) % st)
    cls_line = dot(cls, mine)[0:1]
    kap_line = dot(kap[:16], mine)[0:1]
    lane = iota((1, LANES), 1)
    code = (lane % st // TILE).astype(f32) * CLASSES + cls_line

    def class_rows(start, stop):
        lines = iota((padded(stop - start), LANES), 0)
        lines = jnp.where(lines < stop - start, lines + start, -1).astype(f32)
        return jnp.concatenate(
            [ones_where(lines == code + c * SUMS) for c in channels_of(start, stop)], axis=1
        )

    own_rows = ones_where(iota((st, LANES), 0) == iota((st, LANES), 1) % st)

    pl.semaphore_wait(barrier, n_stn + n_grid - 2)

    @pl.when(here < n_grid - 1)
    def _():
        pltpu.make_async_remote_copy(
            src_ref=v_ref.at[:, pl.ds(samples - halo, halo)],
            dst_ref=vext.at[:, pl.ds(0, halo)],
            send_sem=halo_send,
            recv_sem=halo_recv,
            device_id=(me, here + 1),
            device_id_type=MESH,
        ).start()

    load.wait()
    even = iota((2 * n_stn * STEP, LANES), 1) < st

    def filtered(h, c):
        rows = wide[c * 2 * n_stn * STEP : (c + 1) * 2 * n_stn * STEP, :]
        first = 2 * h * STEP * frame_len
        second = first + STEP * frame_len
        window = jnp.concatenate(
            [vext[:, first : first + reach], vext[:, second : second + reach]], axis=0
        )
        got = dot_nt(rows, window)
        for t in range(2):
            part = got[:, t * LANES : (t + 1) * LANES]
            for p in range(2):
                only = jnp.where(even if p == 0 else ~even, part, 0.0).astype(bf16)
                spec[h, :, :, p, t, :, c * LANES : (c + 1) * LANES] = only.reshape(
                    n_stn, 2, STEP, LANES
                )

    copies, arrivals = [], [[] for _ in groups]

    passed = set()

    def made(m, send_now):
        h, start, stop = groups[m]
        for c in channels_of(start, stop):
            if c not in built:
                build(c)
            if (h, c) not in passed:
                passed.add((h, c))
                filtered(h, c)
        cs = channels_of(start, stop)
        pick_rows = class_rows(start, stop)
        for k in order + [0]:
            to = lax.rem(me + k, n_stn)
            block = spec[h, to, :, :, :, :, cs[0] * LANES : (cs[-1] + 1) * LANES]
            got = dot_nt(pick_rows, block.reshape(LANES, len(cs) * LANES)).astype(bf16)
            sends[m][to] = got
            if k and send_now:
                sent(m, k)
        recvs[m][me] = sends[m][me]

    def sent(m, k):
        to = lax.rem(me + k, n_stn)
        copy = pltpu.make_async_remote_copy(
            src_ref=sends[m].at[to],
            dst_ref=recvs[m].at[me],
            send_sem=send_sem.at[m, k],
            recv_sem=recv_sem.at[m, k],
            device_id=(to, here),
            device_id_type=MESH,
        )
        copy.start()
        copies.append(copy)
        arrivals[m].append(copy)

    def kept(h):
        for c in range(chans):
            for d in range(0, n_stn, 2):
                block = spec[h, d : d + 2, :, :, :, :, c * LANES : (c + 1) * LANES]
                got = dot_nt(own_rows, block.reshape(2 * LANES, LANES)).astype(bf16)
                for j in range(2):
                    own[c, d + j, :, h * LANES : (h + 1) * LANES] = got[
                        :, j * LANES : (j + 1) * LANES
                    ]

    early = [m for m, group in enumerate(groups) if group[0] == 1]
    late = [m for m, group in enumerate(groups) if group[0] == 0]
    for m in early:
        made(m, True)
    kept(1)

    halo_copy = pltpu.make_async_remote_copy(
        src_ref=v_ref.at[:, pl.ds(samples - halo, halo)],
        dst_ref=vext.at[:, pl.ds(0, halo)],
        send_sem=halo_send,
        recv_sem=halo_recv,
        device_id=(me, lax.rem(here + 1, n_grid)),
        device_id_type=MESH,
    )

    @pl.when(here > 0)
    def _():
        halo_copy.wait_recv()

    @pl.when(here == 0)
    def _():
        vext[:, 0:halo] = jnp.zeros((LANES, halo), bf16)

    for m in late:
        made(m, m == late[0])
    kept(0)

    half = n_stn * 8
    lane2 = iota((st, 2 * LANES), 1)
    flip = jnp.where(lane2 % LANES < LANES // 2, 1.0, -1.0)
    for c in range(chans, 4):
        for d in range(n_stn):
            vis[d * 8 + c * 2 : d * 8 + c * 2 + 2] = jnp.zeros((2, st, LANES), f32)
    for c in range(chans):
        for d in range(n_stn):
            x = own[c, d]
            xf = x.astype(f32)
            turned = jnp.concatenate(
                [
                    pltpu.roll(xf[:, p * LANES : (p + 1) * LANES], LANES // 2, 1)
                    for p in range(2)
                ],
                axis=1,
            )
            both = jnp.concatenate([x, (turned * flip).astype(bf16)], axis=0)
            got = dot_nt(both, jnp.concatenate([x, x], axis=0))
            for e in range(2):
                vis[d * 8 + c * 2 + e] = got[e * st : (e + 1) * st]
    lane3 = iota((half, LANES), 1)
    for k in range(TILE // 2):
        first = jnp.where(lane3 % st < TILE, vis[:, 2 * k, :], vis[:, 2 * k + TILE, :])
        second = jnp.where(lane3 % st < TILE, vis[:, 2 * k + 1, :], vis[:, 2 * k + 1 + TILE, :])
        left[:, k * LANES : (k + 1) * LANES] = jnp.where(lane3 < st, first, second).astype(bf16)
    which = (st, stations)
    kap_col = dot_nt(ones_where(iota(which, 1) == me * st + iota(which, 0)), kap)
    base = kap_col + iota((st, LANES), 1).astype(f32) - (SEPS * (SPREAD - 1) + SPREAD - 1)
    blank = jnp.zeros((TILE, LANES), bf16)
    row_t = iota((TILE, LANES), 0)
    for i in range(TILE):
        for a in range(2):
            at = a * TILE + i
            value = kap_line[0:1, at : at + 1]
            hit = ones_where((base[a * TILE : (a + 1) * TILE] == value) & (row_t > i))
            first = i * st + a * TILE
            picks[first : first + TILE, a * LANES : (a + 1) * LANES] = hit
            picks[first : first + TILE, (1 - a) * LANES : (2 - a) * LANES] = blank
    binned = dot(left[...], picks[...])
    dsend[...] = jnp.concatenate(
        [
            binned[:, a * LANES : (a + 1) * LANES].reshape(n_stn, 8, LANES)
            for a in range(2)
        ],
        axis=1,
    ).astype(bf16)
    own_arrivals = []
    for k in order:
        to = lax.rem(me + k, n_stn)
        copy = pltpu.make_async_remote_copy(
            src_ref=dsend.at[to],
            dst_ref=drecv_ref.at[me],
            send_sem=dsend_sem.at[k],
            recv_sem=drecv_sem.at[k],
            device_id=(to, here),
            device_id_type=MESH,
        )
        copy.start()
        copies.append(copy)
        own_arrivals.append(copy)
    drecv_ref[me] = dsend[me]
    for k in order:
        sent(late[1], k)
    for k in order:
        sent(late[2], k)


    tiles = 2 * n_stn
    over, kern = table_ref.shape
    divisor = frame_len - 1
    side = SPREAD * tiles
    full = SPREAD * side
    depth = 2 * LANES
    across_w = tiles * PATCH
    npair = cells_ref.shape[2]

    def tile_of(x):
        return 2 * (x % n_stn) + x // n_stn

    def pair_number(x):
        b = tile_of(x % tiles)
        last = x // tiles == tiles - 1
        a = jnp.where(last, b, tile_of(x // tiles))
        return jnp.where((a < b) | last, a * tiles - a * (a - 1) // 2 + b - a, -1)

    choose = ones_where(iota((npair, PAIR_ROWS), 0) == pair_number(iota((1, PAIR_ROWS), 1)))
    choose_t = ones_where(iota((PAIR_ROWS, npair), 1) == pair_number(iota((PAIR_ROWS, 1), 0)))
    absent = jnp.where(pair_number(iota((1, PAIR_ROWS), 1)) < 0, -1000.0, 0.0)

    def weight_rows(c, d, r):
        scaled = (d * (me * chans + c + frame_len // 2)).astype(f32)
        cell = jnp.floor((scaled + 0.5) / divisor)
        rest = scaled - cell * divisor
        fine = jnp.floor((rest * over + 0.5) / divisor)
        tap = r - cell.astype(i32)
        code = jnp.where((tap >= 0) & (tap < kern), fine.astype(i32) * kern + tap, -1)
        got = jnp.zeros(code.shape, f32)
        for o in range(over):
            for t in range(kern):
                got = jnp.where(code == o * kern + t, table_ref[o, t], got)
        return got

    xs[full:, :] = jnp.zeros((xs.shape[0] - full, depth), bf16)
    norm = 1.0 / (n_grid * depth // 2)
    rows_t = (16, UV)
    rows_w = (16, across_w)
    same_tile = iota((tiles, across_w), 0) == iota((tiles, across_w), 1) // PATCH
    own_block = iota((LANES, across_w), 0) // SEPS == iota((LANES, across_w), 1) // PATCH
    onto = ones_where(iota((LANES, 16), 0) % SEPS == iota((LANES, 16), 1))
    for c in range(chans):
        cells = cells_ref[c].astype(f32)
        row_line = dot(jnp.broadcast_to(cells[0:1], (16, npair)).astype(bf16), choose)[0:1] + absent
        cols[c] = dot_nt(choose_t, jnp.broadcast_to(cells[1:2], (LANES, npair)).astype(bf16))
        spots = ones_where(iota((UV, PAIR_ROWS), 0).astype(f32) == row_line)
        lines = weight_rows(c, iota(rows_t, 0), (UV - iota(rows_t, 1)) % UV)
        for du in range(SEPS):
            band = pltpu.roll(
                jnp.broadcast_to(lines[du : du + 1], (UV, UV)), 0, 1, stride=1, stride_axis=0
            )
            top, low = split(band)
            bands[c, :, du * PAIR_ROWS : (du + 1) * PAIR_ROWS] = dot(
                jnp.concatenate([top, low], axis=0), spots
            ).astype(bf16)
        across = weight_rows(c, iota(rows_w, 0), iota(rows_w, 1) % PATCH)
        for at in range(SEPS):
            parts = split(jnp.where(same_tile, across[at : at + 1], 0.0))
            for j in range(2):
                vweights[c, j, at * tiles : (at + 1) * tiles, :] = parts[j]
        for j in range(2):
            vweights[c, j, SEPS * tiles :, :] = jnp.zeros((depth - SEPS * tiles, across_w), bf16)
        for j, part in enumerate(split(across)):
            oweights[c, j] = jnp.where(own_block, dot(onto, part), 0.0).astype(bf16)

    ready = set()
    reduced = []
    lane_h = iota((tiles, LANES), 1) < LANES // 2
    rows_p = 2 * SEPS * tiles
    lane_s = iota((side, LANES), 1) < side
    lane_p = iota((tiles, LANES), 1)

    def found(h, g):
        for m, (half, start, stop) in enumerate(groups):
            if half == h and start <= g < stop:
                if m not in ready:
                    ready.add(m)
                    for copy in arrivals[m]:
                        copy.wait_recv()
                    flats[m][...] = recvs[m][...].astype(f32)
                return flats[m][:, g - start, :]

    def moves(c, a):
        distance = iota((tiles, LANES), 1) - cols[c, a * tiles : (a + 1) * tiles].astype(i32)
        valid = (distance >= 0) & (distance < PATCH)
        return valid, jnp.where(valid, distance, 0)

    def correlated(c):
        turned = []
        for q in range(SPREAD * SPREAD):
            pieces = []
            for h in range(2):
                x = jnp.concatenate(
                    [found(h, c * SUMS + a * CLASSES + q) for a in range(2)], axis=0
                )
                xs[q * tiles : (q + 1) * tiles, h * LANES : (h + 1) * LANES] = x.astype(bf16)
                y = pltpu.roll(x, LANES // 2, 1)
                pieces.append(jnp.where(lane_h, -y, y).astype(bf16))
            turned.append(jnp.concatenate(pieces, axis=1))
        lefts = [xs[:full], jnp.concatenate(turned, axis=0)]
        for e in range(2):
            blocks = []
            for q in range(0, SPREAD, 2):
                names = [r for r in (q, q + 1) if r < SPREAD]
                rights = [xs[r * side : r * side + LANES] for r in names]
                got = dot_nt(lefts[e], jnp.concatenate(rights, axis=0))
                blocks += [got[:, j * LANES : (j + 1) * LANES] for j in range(len(names))]
            for du in range(SEPS):
                d = du - (SPREAD - 1)
                total = sum(
                    blocks[s + d][s * side : (s + 1) * side]
                    for s in range(SPREAD)
                    if 0 <= s + d < SPREAD
                )
                total = jnp.where(lane_s, total, 0.0)
                shifts = [
                    pltpu.roll(
                        total[x * tiles : (x + 1) * tiles], (SPREAD - 1 - x) * tiles, 1
                    )
                    for x in range(SPREAD - 1)
                ]
                wrap = (2 * SPREAD - 1) * tiles - LANES
                main = total[(SPREAD - 1) * tiles :] + jnp.where(lane_p < wrap, 0.0, shifts[0])
                for part in shifts[1:]:
                    main = main + part
                over_part = jnp.where(lane_p < wrap, shifts[0], 0.0)
                top, low = split(jnp.concatenate([main, over_part], axis=1))
                at = (e * SEPS + du) * tiles
                sums[at : at + tiles, :] = top
                sums[rows_p + at : rows_p + at + tiles, :] = low
        patches = dot(sums[...], vweights[c, 0])
        patches = patches[:rows_p] + patches[rows_p:] + dot(sums[:rows_p], vweights[c, 1])

        for a in range(tiles - 1):
            valid, index = moves(c, a)
            index = index + (a % 8) * PATCH
            for du in range(SEPS):
                for e in range(2):
                    at = (e * SEPS + du) * tiles
                    source = patches[at : at + tiles, a // 8 * LANES : (a // 8 + 1) * LANES]
                    moved = jnp.where(valid, jnp.take_along_axis(source, index, axis=1), 0.0)
                    first = du * PAIR_ROWS + a * tiles
                    placed[c, first : first + tiles, e * LANES : (e + 1) * LANES] = moved.astype(
                        bf16
                    )

    def gridded(c):
        rr, cc = iota((32, n_stn * 16), 0), iota((32, n_stn * 16), 1)
        b = rr % tiles
        take = ones_where(cc == (b % n_stn) * 16 + (b // n_stn) * 8 + c * 2 + rr // tiles)
        alone = dot(take, drecv_ref[...].reshape(n_stn * 16, LANES)).astype(bf16)
        alone = dot(alone, oweights[c, 0]) + dot(alone, oweights[c, 1])
        valid, index = moves(c, tiles - 1)
        for du in range(SEPS):
            for e in range(2):
                source = alone[e * tiles : (e + 1) * tiles, du // 8 * LANES : (du // 8 + 1) * LANES]
                moved = jnp.take_along_axis(source, index + (du % 8) * PATCH, axis=1)
                first = du * PAIR_ROWS + (tiles - 1) * tiles
                placed[c, first : first + tiles, e * LANES : (e + 1) * LANES] = jnp.where(
                    valid, moved, 0.0
                ).astype(bf16)
        plane = dot(bands[c], placed[c])
        plane = (plane[:UV] + plane[UV:]) * norm
        rs_send[c] = plane.astype(bf16).reshape(n_grid, UV // n_grid, 2 * UV)
        for k in range(1, n_grid):
            to = lax.rem(here + k, n_grid)
            copy = pltpu.make_async_remote_copy(
                src_ref=rs_send.at[c, to],
                dst_ref=rs_recv.at[c, k],
                send_sem=rs_send_sem.at[c, k],
                recv_sem=rs_recv_sem.at[c, k],
                device_id=(me, to),
                device_id_type=MESH,
            )
            copy.start()
            reduced.append(copy)

    for c in range(chans):
        correlated(c)
        if c == 0:
            for copy in own_arrivals:
                copy.wait_recv()
        gridded(c)

    for c in range(chans):
        total = rs_send[c, here].astype(f32)
        for k in range(1, n_grid):
            reduced[c * (n_grid - 1) + k - 1].wait_recv()
            total = total + rs_recv[c, k].astype(f32)
        out_ref[c] = total
    for copy in copies + reduced:
        copy.wait_send()

    @pl.when(here < n_grid - 1)
    def _():
        halo_copy.wait_send()


def kernel_body(voltages, pfb_coeffs, station_offsets, tile_cells, kernel_table):
    st, pols, samples = voltages.shape
    taps, frame_len = pfb_coeffs.shape
    n_stn, n_grid = lax.axis_size("stn"), lax.axis_size("grid")
    chans = tile_cells.shape[0]
    dims = (n_stn, n_grid, chans, taps, frame_len, st)
    reach = (STEP + taps) * frame_len
    whole, first = chans * SUMS, padded(SUMS)
    second = first + padded(2 * SUMS - first)
    third = SUMS // 16 * 16
    groups = (
        (1, 0, third), (1, third, whole), (0, 0, first), (0, first, second), (0, second, whole),
    )

    line = np.arange(frame_len)[:, None] * np.arange(frame_len // 2)[None, :] % frame_len
    angles = line.astype(np.float32) * np.float32(2.0 * math.pi / frame_len)
    scale = np.float32(1.0 / math.sqrt(frame_len))
    table = np.stack([np.cos(angles) * scale, -np.sin(angles) * scale], axis=2)
    table = table.astype(jnp.bfloat16).astype(np.float32)
    table = table.transpose(1, 2, 0).reshape(n_stn, chans, 2, frame_len).transpose(1, 0, 2, 3)
    table = jnp.asarray(np.tile(table.reshape(-1, frame_len), (1, STEP + taps)))
    vmem = pl.BlockSpec(memory_space=pltpu.VMEM)
    smem = pl.BlockSpec(memory_space=pltpu.SMEM)
    anywhere = pl.BlockSpec(memory_space=pl.ANY)
    flat = jnp.transpose(voltages, (1, 0, 2)).reshape(pols * st, samples)
    tiles = 2 * n_stn
    full = SPREAD * SPREAD * tiles
    strip = UV // n_grid
    heights = [padded(stop - start) for _, start, stop in groups]
    summed = pl.pallas_call(
        functools.partial(whole_kernel, dims, groups),
        out_shape=jax.ShapeDtypeStruct((chans, strip, 2 * UV), f32),
        in_specs=[anywhere, vmem, vmem, vmem, vmem, smem],
        out_specs=vmem,
        scratch_shapes=[
            pltpu.VMEM((LANES, taps * frame_len + samples), bf16),
            pltpu.VMEM((2 * n_stn * chans * STEP, reach), bf16),
            pltpu.VMEM((2, n_stn, 2, 2, 2, STEP, chans * LANES), bf16),
            pltpu.VMEM((chans, n_stn, st, 2 * LANES), bf16),
            pltpu.VMEM((n_stn * 8, st, LANES), f32),
            pltpu.VMEM((n_stn * 8, TILE * st), bf16),
            pltpu.VMEM((TILE * st, 2 * LANES), bf16),
            pltpu.VMEM((n_stn, 16, LANES), bf16),
            pltpu.VMEM((n_stn, 16, LANES), bf16),
            pltpu.VMEM((chans, 2 * UV, SEPS * PAIR_ROWS), bf16),
            pltpu.VMEM((chans, 2, 2 * LANES, tiles * PATCH), bf16),
            pltpu.VMEM((chans, 2, LANES, tiles * PATCH), bf16),
            pltpu.VMEM((chans, PAIR_ROWS, LANES), f32),
            pltpu.VMEM((full + 48, 2 * LANES), bf16),
            pltpu.VMEM((4 * SEPS * tiles, 2 * LANES), bf16),
            pltpu.VMEM((chans, SEPS * PAIR_ROWS, 2 * UV), bf16),
            pltpu.VMEM((chans, n_grid, strip, 2 * UV), bf16),
            pltpu.VMEM((chans, n_grid, strip, 2 * UV), bf16),
            *[pltpu.VMEM((n_stn, h, LANES), bf16) for h in heights],
            *[pltpu.VMEM((n_stn, h, LANES), bf16) for h in heights],
            *[pltpu.VMEM((n_stn, h, LANES), f32) for h in heights],
            pltpu.SemaphoreType.DMA,
            pltpu.SemaphoreType.DMA,
            pltpu.SemaphoreType.DMA,
            pltpu.SemaphoreType.DMA((len(groups), n_stn)),
            pltpu.SemaphoreType.DMA((len(groups), n_stn)),
            pltpu.SemaphoreType.DMA((n_stn,)),
            pltpu.SemaphoreType.DMA((n_stn,)),
            pltpu.SemaphoreType.DMA((chans, n_grid)),
            pltpu.SemaphoreType.DMA((chans, n_grid)),
        ],
        compiler_params=pltpu.CompilerParams(
            collective_id=0, has_side_effects=True, vmem_limit_bytes=48 << 20
        ),
    )(flat, pfb_coeffs, table, station_offsets, tile_cells, kernel_table)
    return jnp.transpose(summed, (1, 0, 2))


def kernels_fit(mesh, args):
    voltages, pfb_coeffs, offsets, cells, _ = args
    n_stn, n_grid = mesh.shape["stn"], mesh.shape["grid"]
    stations, pols, samples = voltages.shape
    taps, frame_len = pfb_coeffs.shape
    spectra = samples // frame_len // n_grid
    return (
        stations == 2 * TILE * n_stn
        and n_stn == 8
        and pols == 2
        and spectra == 64
        and taps == 16
        and frame_len // 2 == cells.shape[0] == 3 * n_stn
    )


def solution(mesh):
    placed = (P("stn", None, "grid"), P(), P(), P("stn", None, None), P())

    def run(*args):
        inner = kernel_body if kernels_fit(mesh, args) else body
        return jax.shard_map(
            inner, mesh=mesh, in_specs=placed, out_specs=P("grid", "stn", None), check_vma=False
        )(*args)

    return run
```

```python
import functools
import math

import jax
import jax.numpy as jnp
import numpy as np
from jax import lax
from jax.experimental import pallas as pl
from jax.experimental.pallas import tpu as pltpu
from jax.sharding import PartitionSpec as P

TILE = 32
PATCH = 16
SPREAD = 5
UV = 128


highest = lax.Precision.HIGHEST


def shifted(block, axis, distance):
    devices = range(lax.axis_size(axis))
    route = [(i - distance, i) for i in devices if i - distance in devices]
    return lax.ppermute(block, axis, route)


def dft_table(frame_len):
    chan_count = frame_len // 2
    sample_line = jnp.arange(frame_len, dtype=jnp.int32)[:, None]
    chan_line = jnp.arange(chan_count, dtype=jnp.int32)[None, :]
    angles = (sample_line * chan_line % frame_len).astype(jnp.float32) * (2.0 * math.pi / frame_len)
    norm_factor = 1.0 / math.sqrt(frame_len)
    twiddle = jnp.stack([jnp.cos(angles) * norm_factor, -jnp.sin(angles) * norm_factor], axis=2)
    return twiddle.reshape(frame_len, 2 * chan_count).astype(jnp.bfloat16)


CLASSES = SPREAD * SPREAD
high = lax.Precision.HIGH


def fused_filter(coeffs, twiddle, step):
    taps, frame_len = coeffs.shape
    flat = coeffs.reshape(-1)
    columns = [
        jnp.pad(flat, (frame_len * (f + 1), frame_len * (step - 1 - f))) for f in range(step)
    ]
    shifted_coeffs = jnp.stack(columns, axis=0)
    spread = np.kron(np.ones((1, frame_len), np.float32), np.eye(step, dtype=np.float32))
    wide = jnp.einsum("fm,fn->mn", shifted_coeffs, jnp.asarray(spread), precision=highest)
    tiled = jnp.tile(jnp.repeat(twiddle.astype(jnp.float32), step, axis=1), (step + taps, 1))
    return (wide * tiled).astype(jnp.bfloat16)

def separation_table(frequency, divisor, kernel_table):
    over_count = kernel_table.shape[0]
    separation = jnp.arange(2 * SPREAD - 1, dtype=jnp.int32)
    scaled = separation * frequency
    cell_index = scaled // divisor
    fine_index = scaled % divisor * over_count // divisor
    choose = (fine_index[:, None] == jnp.arange(over_count, dtype=jnp.int32)[None, :]).astype(
        jnp.float32
    )
    tap_values = jnp.dot(choose, kernel_table, precision=highest)
    place_rel = jnp.arange(PATCH, dtype=jnp.int32)[None, :] - cell_index[:, None]
    weights = jnp.zeros(place_rel.shape, jnp.float32)
    for tap_index in range(kernel_table.shape[1]):
        weights = weights + tap_values[:, tap_index : tap_index + 1] * (
            place_rel == tap_index
        ).astype(jnp.float32)
    return weights


def shifted_weights(weights, bases):
    place = jnp.arange(UV, dtype=jnp.int32)[None, :, None] - bases[:, None, :]
    taps = jnp.arange(PATCH, dtype=jnp.int32)[None, :, None, None]
    spots = place[:, None] == taps
    if weights.dtype == jnp.float32:
        return jnp.einsum("cdt,ctwp->cdwp", weights, spots.astype(jnp.float32), precision=highest)
    return jnp.einsum(
        "cdt,ctwp->cdwp", weights, spots.astype(jnp.bfloat16), preferred_element_type=jnp.float32
    ).astype(jnp.bfloat16)


def body(voltages, pfb_coeffs, station_offsets, tile_cells, kernel_table):
    stn_local, pol_count, samples = voltages.shape
    tap_count, frame_len = pfb_coeffs.shape
    spec_count = samples // frame_len
    step = 128 // math.gcd(128, frame_len)
    chunks = spec_count // step
    flat = jnp.transpose(voltages, (1, 0, 2))
    earlier = shifted(flat[:, :, samples - tap_count * frame_len :], "grid", 1)
    extended = jnp.concatenate([earlier, flat], axis=2)
    width = step * frame_len
    reach = (step + tap_count) * frame_len
    blocks = jnp.stack(
        [extended[:, :, c * width : c * width + reach] for c in range(chunks)], axis=1
    )
    matrix = fused_filter(pfb_coeffs, dft_table(frame_len), step)
    spectra = jnp.einsum(
        "pcsm,mn->npcs", blocks, matrix, preferred_element_type=jnp.float32
    ).astype(jnp.bfloat16)
    spectra = spectra.reshape(frame_len // 2, 2, step * pol_count * chunks, stn_local)
    spectra, tile_cells = lax.optimization_barrier((spectra, tile_cells))
    turned = lax.all_to_all(spectra, "stn", split_axis=0, concat_axis=3, tiled=True)
    turned = jnp.transpose(turned, (0, 1, 3, 2))
    ch_dev, _, stations, depth = turned.shape
    tiles = stations // TILE
    divisor = frame_len - 1
    first_chan = lax.axis_index("stn") * ch_dev + frame_len // 2
    norm_factor = 1.0 / (pol_count * spec_count * lax.axis_size("grid"))

    classes = (station_offsets[0] * SPREAD + station_offsets[1]).reshape(tiles, TILE)
    hot = classes[:, :, None] == jnp.arange(CLASSES, dtype=jnp.int32)
    hot_low = hot.astype(jnp.bfloat16)
    hot_full = hot.astype(jnp.float32)
    tiled = turned.reshape(ch_dev, 2, tiles, TILE, depth)
    summed = jnp.einsum(
        "aiq,ceaik->ceaqk", hot_low, tiled, preferred_element_type=jnp.float32
    ).astype(jnp.bfloat16)

    def stacked(z):
        real_part, imag_part = z[:, 0], z[:, 1]
        partner = jnp.concatenate([real_part, imag_part], axis=-1)
        turned_partner = jnp.concatenate([imag_part, -real_part], axis=-1)
        return jnp.stack([partner, turned_partner], axis=1), partner

    left, right = stacked(summed)
    shape = (SPREAD, SPREAD, 2 * depth)
    terms = []
    for i in range(ch_dev):
        taps = jnp.transpose(left[i].reshape((2 * tiles,) + shape), (1, 2, 3, 0))
        terms.append(
            lax.conv_general_dilated(
                right[i].reshape((tiles,) + shape),
                taps,
                (1, 1),
                [(SPREAD - 1, SPREAD - 1)] * 2,
                dimension_numbers=("NHWC", "HWIO", "HWNC"),
                preferred_element_type=jnp.float32,
            )
        )
    seps = 2 * SPREAD - 1
    cross = jnp.stack(terms).reshape(ch_dev, seps, seps, tiles, 2, tiles)
    cross = jnp.transpose(cross, (0, 4, 1, 2, 3, 5)).reshape(ch_dev, 2, seps, seps, tiles * tiles)
    own_left, own_right = stacked(tiled)
    own = jnp.einsum("ceaik,cajk->ceaij", own_left, own_right, preferred_element_type=jnp.float32)
    line = np.arange(TILE)
    own = jnp.where(jnp.asarray(line[:, None] < line[None, :]), own, 0.0)
    own = jnp.einsum("aiq,ceaij->ceaqj", hot_full, own, precision=high)
    own = jnp.einsum("ceaqj,ajs->ceasq", own, hot_full, precision=high)
    class_line = np.arange(CLASSES)
    back_u = class_line[:, None] // SPREAD - class_line[None, :] // SPREAD + SPREAD - 1
    back_v = class_line[:, None] % SPREAD - class_line[None, :] % SPREAD + SPREAD - 1
    pick = np.arange(seps * seps) == (back_u * seps + back_v).reshape(-1, 1)
    own = jnp.einsum(
        "ceam,mz->ceza",
        own.reshape(ch_dev, 2, tiles, CLASSES * CLASSES),
        jnp.asarray(pick.astype(np.float32)),
        precision=high,
    )
    diagonal = np.zeros((tiles, tiles * tiles), np.float32)
    diagonal[np.arange(tiles), np.arange(tiles) * (tiles + 1)] = 1.0
    own = jnp.einsum("ceza,ap->cezp", own, jnp.asarray(diagonal), precision=high)
    own = own.reshape(ch_dev, 2, seps, seps, tiles * tiles)
    same = jnp.asarray(diagonal.sum(axis=0) > 0)
    cross = jnp.where(same, own, cross)

    pair_first, pair_second = np.triu_indices(tiles)
    select = np.zeros((pair_first.size, tiles * tiles), np.float32)
    select[np.arange(pair_first.size), pair_second * tiles + pair_first] = 1.0
    missing = (1.0 - select.sum(axis=0)).astype(np.int32) * 4096
    cells = jnp.einsum(
        "cxk,kp->cxp", tile_cells.astype(jnp.float32), jnp.asarray(select), precision=highest
    )
    cells = jnp.round(cells).astype(jnp.int32) + jnp.asarray(missing)
    weights = jnp.stack(
        [separation_table(first_chan + i, divisor, kernel_table)[::-1] for i in range(ch_dev)]
    )
    scaled = weights * norm_factor
    coarse = lax.reduce_precision(scaled, 8, 7)
    rest = (scaled - coarse).astype(jnp.bfloat16)
    rows = [shifted_weights(part, cells[:, 0]) for part in (coarse.astype(jnp.bfloat16), rest)]
    place = jnp.arange(UV, dtype=jnp.int32)[None, :, None] - cells[:, 1][:, None, :]
    cols = []
    for v in range(seps):
        placed = jnp.zeros(place.shape, jnp.float32)
        for t in range(PATCH):
            placed = jnp.where(place == t, weights[:, v, t][:, None, None], placed)
        cols.append(placed)
    cols = lax.optimization_barrier(tuple(cols))
    spread_cols = sum(
        cross[:, :, :, v, None, :] * cols[v][:, None, None] for v in range(seps)
    )
    spread_cols = spread_cols.astype(jnp.bfloat16)
    planes = sum(
        jnp.einsum(
            "cdup,cedwp->ucew", part, spread_cols, preferred_element_type=jnp.float32
        )
        for part in rows
    )
    grid_count = lax.axis_size("grid")
    planes = planes.reshape(grid_count, UV // grid_count, ch_dev, 2 * UV).astype(jnp.bfloat16)
    parts = lax.all_to_all(planes, "grid", split_axis=0, concat_axis=0, tiled=True)
    return parts.astype(jnp.float32).sum(axis=0)


f32, bf16, i32 = jnp.float32, jnp.bfloat16, jnp.int32
MESH = pl.DeviceIdType.MESH
SEPS = 2 * SPREAD - 1
STEP = 16
LANES = 128
SUMS = 2 * CLASSES
PAIR_ROWS = 256


def iota(shape, axis):
    return lax.broadcasted_iota(i32, shape, axis)


def ones_where(mask, kind=bf16):
    return jnp.where(mask, 1.0, 0.0).astype(kind)


def dot(a, b):
    return lax.dot_general(a, b, (((1,), (0,)), ((), ())), preferred_element_type=f32)


def dot_nt(a, b):
    return lax.dot_general(a, b, (((1,), (1,)), ((), ())), preferred_element_type=f32)


def split(x):
    top = x.astype(bf16)
    return top, (x - top.astype(f32)).astype(bf16)


def send_order(n):
    return sorted(range(1, n), key=lambda k: abs(2 * k - n))


def padded(rows):
    return -(-rows // 16) * 16


def channels_of(start, stop):
    return range(start // SUMS, (stop - 1) // SUMS + 1)


def whole_kernel(
    dims, groups, v_ref, coef_ref, tw_ref, off_ref, cells_ref, table_ref, out_ref,
    vext, wide, spec, own, vis, left, picks, dsend, drecv_ref,
    bands, vweights, oweights, cols, xs, sums, placed, rs_send, rs_recv, *rest
):
    n_stn, n_grid, chans, taps, frame_len, st = dims
    n_msg = len(groups)
    sends, recvs, flats = rest[:n_msg], rest[n_msg : 2 * n_msg], rest[2 * n_msg : 3 * n_msg]
    (
        halo_send, halo_recv, send_sem, recv_sem, dsend_sem, drecv_sem,
        rs_send_sem, rs_recv_sem,
    ) = rest[3 * n_msg :]
    me, here = lax.axis_index("stn"), lax.axis_index("grid")
    reach = (STEP + taps) * frame_len
    halo = taps * frame_len
    samples = v_ref.shape[1]
    stride = STEP * frame_len
    order = send_order(n_stn)

    barrier = pltpu.get_barrier_semaphore()
    for k in range(1, n_stn):
        pl.semaphore_signal(
            barrier, inc=1, device_id=(lax.rem(me + k, n_stn), here), device_id_type=MESH
        )
    for k in range(1, n_grid):
        pl.semaphore_signal(
            barrier, inc=1, device_id=(me, lax.rem(here + k, n_grid)), device_id_type=MESH
        )

    coef = coef_ref[...]
    line = jnp.concatenate(
        [jnp.zeros((1, frame_len), f32)]
        + [coef[k : k + 1, :] for k in range(taps)]
        + [jnp.zeros((1, reach - (taps + 1) * frame_len), f32)],
        axis=1,
    )
    shifted_line = jnp.concatenate(
        [line if f == 0 else pltpu.roll(line, f * frame_len, 1) for f in range(STEP)], axis=0
    )
    built = set()

    def build(c):
        built.add(c)
        for r in range(2 * n_stn * c, 2 * n_stn * (c + 1)):
            wide[r * STEP : (r + 1) * STEP, :] = (tw_ref[r : r + 1, :] * shifted_line).astype(bf16)

    build(0)

    offs = off_ref[...].astype(f32)
    stations = offs.shape[1]
    cls = jnp.broadcast_to(SPREAD * offs[0:1] + offs[1:2], (16, stations)).astype(bf16)
    kap = jnp.broadcast_to(SEPS * offs[0:1] + offs[1:2], (LANES, stations)).astype(bf16)
    row_of = (stations, LANES)
    mine = ones_where(iota(row_of, 0) == me * st + iota(row_of, 1) % st)
    cls_line = dot(cls, mine)[0:1]
    kap_line = dot(kap[:16], mine)[0:1]
    lane = iota((1, LANES), 1)
    code = (lane % st // TILE).astype(f32) * CLASSES + cls_line

    def class_rows(start, stop):
        lines = iota((padded(stop - start), LANES), 0)
        lines = jnp.where(lines < stop - start, lines + start, -1).astype(f32)
        return jnp.concatenate(
            [ones_where(lines == code + c * SUMS) for c in channels_of(start, stop)], axis=1
        )

    own_rows = ones_where(iota((st, LANES), 0) == iota((st, LANES), 1) % st)

    pl.semaphore_wait(barrier, n_stn + n_grid - 2)

    @pl.when(here < n_grid - 1)
    def _():
        pltpu.make_async_remote_copy(
            src_ref=v_ref.at[:, pl.ds(samples - halo, halo)],
            dst_ref=vext.at[:, pl.ds(0, halo)],
            send_sem=halo_send,
            recv_sem=halo_recv,
            device_id=(me, here + 1),
            device_id_type=MESH,
        ).start()

    vext[:, halo:] = v_ref[:, :stride]
    even = iota((2 * n_stn * STEP, LANES), 1) < st

    def filtered(h, c):
        rows = wide[c * 2 * n_stn * STEP : (c + 1) * 2 * n_stn * STEP, :]
        windows = [
            v_ref[:, t * stride - halo : t * stride - halo + reach] if t else vext[...]
            for t in (2 * h, 2 * h + 1)
        ]
        window = jnp.concatenate(windows, axis=0)
        got = dot_nt(rows, window)
        for t in range(2):
            part = got[:, t * LANES : (t + 1) * LANES]
            for p in range(2):
                only = jnp.where(even if p == 0 else ~even, part, 0.0).astype(bf16)
                spec[h, :, :, p, t, :, c * LANES : (c + 1) * LANES] = only.reshape(
                    n_stn, 2, STEP, LANES
                )

    copies, arrivals = [], [[] for _ in groups]

    passed = set()

    def made(m, send_now):
        h, start, stop = groups[m]
        for c in channels_of(start, stop):
            if c not in built:
                build(c)
            if (h, c) not in passed:
                passed.add((h, c))
                filtered(h, c)
        cs = channels_of(start, stop)
        pick_rows = class_rows(start, stop)
        for k in order + [0]:
            to = lax.rem(me + k, n_stn)
            block = spec[h, to, :, :, :, :, cs[0] * LANES : (cs[-1] + 1) * LANES]
            got = dot_nt(pick_rows, block.reshape(LANES, len(cs) * LANES)).astype(bf16)
            sends[m][to] = got
            if k and send_now:
                sent(m, k)
        recvs[m][me] = sends[m][me]

    def sent(m, k):
        to = lax.rem(me + k, n_stn)
        copy = pltpu.make_async_remote_copy(
            src_ref=sends[m].at[to],
            dst_ref=recvs[m].at[me],
            send_sem=send_sem.at[m, k],
            recv_sem=recv_sem.at[m, k],
            device_id=(to, here),
            device_id_type=MESH,
        )
        copy.start()
        copies.append(copy)
        arrivals[m].append(copy)

    def kept(h):
        for c in range(chans):
            for d in range(0, n_stn, 2):
                block = spec[h, d : d + 2, :, :, :, :, c * LANES : (c + 1) * LANES]
                got = dot_nt(own_rows, block.reshape(2 * LANES, LANES)).astype(bf16)
                for j in range(2):
                    own[c, d + j, :, h * LANES : (h + 1) * LANES] = got[
                        :, j * LANES : (j + 1) * LANES
                    ]

    early = [m for m, group in enumerate(groups) if group[0] == 1]
    late = [m for m, group in enumerate(groups) if group[0] == 0]
    for m in early:
        made(m, True)
    kept(1)

    which = (st, stations)
    kap_col = dot_nt(ones_where(iota(which, 1) == me * st + iota(which, 0)), kap)
    base = kap_col + iota((st, LANES), 1).astype(f32) - (SEPS * (SPREAD - 1) + SPREAD - 1)
    blank = jnp.zeros((TILE, LANES), bf16)
    row_t = iota((TILE, LANES), 0)
    for i in range(TILE):
        for a in range(2):
            at = a * TILE + i
            value = kap_line[0:1, at : at + 1]
            hit = ones_where((base[a * TILE : (a + 1) * TILE] == value) & (row_t > i))
            first = i * st + a * TILE
            picks[first : first + TILE, a * LANES : (a + 1) * LANES] = hit
            picks[first : first + TILE, (1 - a) * LANES : (2 - a) * LANES] = blank

    halo_copy = pltpu.make_async_remote_copy(
        src_ref=v_ref.at[:, pl.ds(samples - halo, halo)],
        dst_ref=vext.at[:, pl.ds(0, halo)],
        send_sem=halo_send,
        recv_sem=halo_recv,
        device_id=(me, lax.rem(here + 1, n_grid)),
        device_id_type=MESH,
    )

    @pl.when(here > 0)
    def _():
        halo_copy.wait_recv()

    @pl.when(here == 0)
    def _():
        vext[:, 0:halo] = jnp.zeros((LANES, halo), bf16)

    for m in late:
        made(m, m == late[0])
    kept(0)

    half = n_stn * 8
    lane2 = iota((st, 2 * LANES), 1)
    flip = jnp.where(lane2 % LANES < LANES // 2, 1.0, -1.0)
    for c in range(chans, 4):
        for d in range(n_stn):
            vis[d * 8 + c * 2 : d * 8 + c * 2 + 2] = jnp.zeros((2, st, LANES), f32)
    for c in range(chans):
        for d in range(n_stn):
            x = own[c, d]
            xf = x.astype(f32)
            turned = jnp.concatenate(
                [
                    pltpu.roll(xf[:, p * LANES : (p + 1) * LANES], LANES // 2, 1)
                    for p in range(2)
                ],
                axis=1,
            )
            both = jnp.concatenate([x, (turned * flip).astype(bf16)], axis=0)
            got = dot_nt(both, jnp.concatenate([x, x], axis=0))
            for e in range(2):
                vis[d * 8 + c * 2 + e] = got[e * st : (e + 1) * st]
    lane3 = iota((half, LANES), 1)
    for k in range(TILE // 2):
        first = jnp.where(lane3 % st < TILE, vis[:, 2 * k, :], vis[:, 2 * k + TILE, :])
        second = jnp.where(lane3 % st < TILE, vis[:, 2 * k + 1, :], vis[:, 2 * k + 1 + TILE, :])
        left[:, k * LANES : (k + 1) * LANES] = jnp.where(lane3 < st, first, second).astype(bf16)
    binned = dot(left[...], picks[...])
    dsend[...] = jnp.concatenate(
        [
            binned[:, a * LANES : (a + 1) * LANES].reshape(n_stn, 8, LANES)
            for a in range(2)
        ],
        axis=1,
    ).astype(bf16)
    own_arrivals = []
    for k in order:
        to = lax.rem(me + k, n_stn)
        copy = pltpu.make_async_remote_copy(
            src_ref=dsend.at[to],
            dst_ref=drecv_ref.at[me],
            send_sem=dsend_sem.at[k],
            recv_sem=drecv_sem.at[k],
            device_id=(to, here),
            device_id_type=MESH,
        )
        copy.start()
        copies.append(copy)
        own_arrivals.append(copy)
    drecv_ref[me] = dsend[me]
    for k in order:
        sent(late[1], k)
    for k in order:
        sent(late[2], k)


    tiles = 2 * n_stn
    over, kern = table_ref.shape
    divisor = frame_len - 1
    side = SPREAD * tiles
    full = SPREAD * side
    depth = 2 * LANES
    across_w = tiles * PATCH
    npair = cells_ref.shape[2]

    def tile_of(x):
        return 2 * (x % n_stn) + x // n_stn

    def pair_number(x):
        b = tile_of(x % tiles)
        last = x // tiles == tiles - 1
        a = jnp.where(last, b, tile_of(x // tiles))
        return jnp.where((a < b) | last, a * tiles - a * (a - 1) // 2 + b - a, -1)

    choose = ones_where(iota((npair, PAIR_ROWS), 0) == pair_number(iota((1, PAIR_ROWS), 1)))
    choose_t = ones_where(iota((PAIR_ROWS, npair), 1) == pair_number(iota((PAIR_ROWS, 1), 0)))
    absent = jnp.where(pair_number(iota((1, PAIR_ROWS), 1)) < 0, -1000.0, 0.0)

    def weight_rows(c, d, r):
        scaled = (d * (me * chans + c + frame_len // 2)).astype(f32)
        cell = jnp.floor((scaled + 0.5) / divisor)
        rest = scaled - cell * divisor
        fine = jnp.floor((rest * over + 0.5) / divisor)
        tap = r - cell.astype(i32)
        code = jnp.where((tap >= 0) & (tap < kern), fine.astype(i32) * kern + tap, -1)
        got = jnp.zeros(code.shape, f32)
        for o in range(over):
            for t in range(kern):
                got = jnp.where(code == o * kern + t, table_ref[o, t], got)
        return got

    xs[full:, :] = jnp.zeros((xs.shape[0] - full, depth), bf16)
    norm = 1.0 / (n_grid * depth // 2)
    rows_t = (16, UV)
    rows_w = (16, across_w)
    same_tile = iota((tiles, across_w), 0) == iota((tiles, across_w), 1) // PATCH
    own_block = iota((LANES, across_w), 0) // SEPS == iota((LANES, across_w), 1) // PATCH
    onto = ones_where(iota((LANES, 16), 0) % SEPS == iota((LANES, 16), 1))
    for c in range(chans):
        cells = cells_ref[c].astype(f32)
        row_line = dot(jnp.broadcast_to(cells[0:1], (16, npair)).astype(bf16), choose)[0:1] + absent
        cols[c] = dot_nt(choose_t, jnp.broadcast_to(cells[1:2], (LANES, npair)).astype(bf16))
        spots = ones_where(iota((UV, PAIR_ROWS), 0).astype(f32) == row_line)
        lines = weight_rows(c, iota(rows_t, 0), (UV - iota(rows_t, 1)) % UV)
        for du in range(SEPS):
            band = pltpu.roll(
                jnp.broadcast_to(lines[du : du + 1], (UV, UV)), 0, 1, stride=1, stride_axis=0
            )
            top, low = split(band)
            bands[c, :, du * PAIR_ROWS : (du + 1) * PAIR_ROWS] = dot(
                jnp.concatenate([top, low], axis=0), spots
            ).astype(bf16)
        across = weight_rows(c, iota(rows_w, 0), iota(rows_w, 1) % PATCH)
        for at in range(SEPS):
            parts = split(jnp.where(same_tile, across[at : at + 1], 0.0))
            for j in range(2):
                vweights[c, j, at * tiles : (at + 1) * tiles, :] = parts[j]
        for j in range(2):
            vweights[c, j, SEPS * tiles :, :] = jnp.zeros((depth - SEPS * tiles, across_w), bf16)
        for j, part in enumerate(split(across)):
            oweights[c, j] = jnp.where(own_block, dot(onto, part), 0.0).astype(bf16)

    ready = set()
    reduced = []
    lane_h = iota((tiles, LANES), 1) < LANES // 2
    rows_p = 2 * SEPS * tiles
    lane_s = iota((side, LANES), 1) < side
    lane_p = iota((tiles, LANES), 1)

    def found(h, g):
        for m, (half, start, stop) in enumerate(groups):
            if half == h and start <= g < stop:
                if m not in ready:
                    ready.add(m)
                    for copy in arrivals[m]:
                        copy.wait_recv()
                    flats[m][...] = recvs[m][...].astype(f32)
                return flats[m][:, g - start, :]

    def moves(c, a):
        distance = iota((tiles, LANES), 1) - cols[c, a * tiles : (a + 1) * tiles].astype(i32)
        valid = (distance >= 0) & (distance < PATCH)
        return valid, jnp.where(valid, distance, 0)

    def correlated(c):
        turned = []
        for q in range(SPREAD * SPREAD):
            pieces = []
            for h in range(2):
                x = jnp.concatenate(
                    [found(h, c * SUMS + a * CLASSES + q) for a in range(2)], axis=0
                )
                xs[q * tiles : (q + 1) * tiles, h * LANES : (h + 1) * LANES] = x.astype(bf16)
                y = pltpu.roll(x, LANES // 2, 1)
                pieces.append(jnp.where(lane_h, -y, y).astype(bf16))
            turned.append(jnp.concatenate(pieces, axis=1))
        lefts = [xs[:full], jnp.concatenate(turned, axis=0)]
        for e in range(2):
            blocks = []
            for q in range(0, SPREAD, 2):
                names = [r for r in (q, q + 1) if r < SPREAD]
                rights = [xs[r * side : r * side + LANES] for r in names]
                got = dot_nt(lefts[e], jnp.concatenate(rights, axis=0))
                blocks += [got[:, j * LANES : (j + 1) * LANES] for j in range(len(names))]
            for du in range(SEPS):
                d = du - (SPREAD - 1)
                total = sum(
                    blocks[s + d][s * side : (s + 1) * side]
                    for s in range(SPREAD)
                    if 0 <= s + d < SPREAD
                )
                total = jnp.where(lane_s, total, 0.0)
                shifts = [
                    pltpu.roll(
                        total[x * tiles : (x + 1) * tiles], (SPREAD - 1 - x) * tiles, 1
                    )
                    for x in range(SPREAD - 1)
                ]
                wrap = (2 * SPREAD - 1) * tiles - LANES
                main = total[(SPREAD - 1) * tiles :] + jnp.where(lane_p < wrap, 0.0, shifts[0])
                for part in shifts[1:]:
                    main = main + part
                over_part = jnp.where(lane_p < wrap, shifts[0], 0.0)
                top, low = split(jnp.concatenate([main, over_part], axis=1))
                at = (e * SEPS + du) * tiles
                sums[at : at + tiles, :] = top
                sums[rows_p + at : rows_p + at + tiles, :] = low
        patches = dot(sums[...], vweights[c, 0])
        patches = patches[:rows_p] + patches[rows_p:] + dot(sums[:rows_p], vweights[c, 1])

        for a in range(tiles - 1):
            valid, index = moves(c, a)
            index = index + (a % 8) * PATCH
            for du in range(SEPS):
                for e in range(2):
                    at = (e * SEPS + du) * tiles
                    source = patches[at : at + tiles, a // 8 * LANES : (a // 8 + 1) * LANES]
                    moved = jnp.where(valid, jnp.take_along_axis(source, index, axis=1), 0.0)
                    first = du * PAIR_ROWS + a * tiles
                    placed[c, first : first + tiles, e * LANES : (e + 1) * LANES] = moved.astype(
                        bf16
                    )

    def alone_placed(c):
        rr, cc = iota((32, n_stn * 16), 0), iota((32, n_stn * 16), 1)
        b = rr % tiles
        take = ones_where(cc == (b % n_stn) * 16 + (b // n_stn) * 8 + c * 2 + rr // tiles)
        alone = dot(take, drecv_ref[...].reshape(n_stn * 16, LANES)).astype(bf16)
        alone = dot(alone, oweights[c, 0]) + dot(alone, oweights[c, 1])
        valid, index = moves(c, tiles - 1)
        for du in range(SEPS):
            for e in range(2):
                source = alone[e * tiles : (e + 1) * tiles, du // 8 * LANES : (du // 8 + 1) * LANES]
                moved = jnp.take_along_axis(source, index + (du % 8) * PATCH, axis=1)
                first = du * PAIR_ROWS + (tiles - 1) * tiles
                placed[c, first : first + tiles, e * LANES : (e + 1) * LANES] = jnp.where(
                    valid, moved, 0.0
                ).astype(bf16)

    def gridded(c):
        plane = dot(bands[c], placed[c])
        plane = (plane[:UV] + plane[UV:]) * norm
        rs_send[c] = plane.astype(bf16).reshape(n_grid, UV // n_grid, 2 * UV)
        for k in range(1, n_grid):
            to = lax.rem(here + k, n_grid)
            copy = pltpu.make_async_remote_copy(
                src_ref=rs_send.at[c, to],
                dst_ref=rs_recv.at[c, k],
                send_sem=rs_send_sem.at[c, k],
                recv_sem=rs_recv_sem.at[c, k],
                device_id=(me, to),
                device_id_type=MESH,
            )
            copy.start()
            reduced.append(copy)

    for c in range(chans):
        correlated(c)
        if c == 0:
            for copy in own_arrivals:
                copy.wait_recv()
            for other in range(chans):
                alone_placed(other)
        gridded(c)

    for c in range(chans):
        total = rs_send[c, here].astype(f32)
        for k in range(1, n_grid):
            reduced[c * (n_grid - 1) + k - 1].wait_recv()
            total = total + rs_recv[c, k].astype(f32)
        out_ref[c] = total
    for copy in copies + reduced:
        copy.wait_send()

    @pl.when(here < n_grid - 1)
    def _():
        halo_copy.wait_send()


def kernel_body(voltages, pfb_coeffs, station_offsets, tile_cells, kernel_table):
    st, pols, samples = voltages.shape
    taps, frame_len = pfb_coeffs.shape
    n_stn, n_grid = lax.axis_size("stn"), lax.axis_size("grid")
    chans = tile_cells.shape[0]
    dims = (n_stn, n_grid, chans, taps, frame_len, st)
    reach = (STEP + taps) * frame_len
    whole, first = chans * SUMS, padded(SUMS)
    second = first + padded(2 * SUMS - first)
    third = SUMS // 16 * 16
    groups = (
        (1, 0, third), (1, third, whole), (0, 0, first), (0, first, second), (0, second, whole),
    )

    line = np.arange(frame_len)[:, None] * np.arange(frame_len // 2)[None, :] % frame_len
    angles = line.astype(np.float32) * np.float32(2.0 * math.pi / frame_len)
    scale = np.float32(1.0 / math.sqrt(frame_len))
    table = np.stack([np.cos(angles) * scale, -np.sin(angles) * scale], axis=2)
    table = table.astype(jnp.bfloat16).astype(np.float32)
    table = table.transpose(1, 2, 0).reshape(n_stn, chans, 2, frame_len).transpose(1, 0, 2, 3)
    table = jnp.asarray(np.tile(table.reshape(-1, frame_len), (1, STEP + taps)))
    vmem = pl.BlockSpec(memory_space=pltpu.VMEM)
    smem = pl.BlockSpec(memory_space=pltpu.SMEM)
    flat = jnp.transpose(voltages, (1, 0, 2)).reshape(pols * st, samples)
    tiles = 2 * n_stn
    full = SPREAD * SPREAD * tiles
    strip = UV // n_grid
    heights = [padded(stop - start) for _, start, stop in groups]
    summed = pl.pallas_call(
        functools.partial(whole_kernel, dims, groups),
        out_shape=jax.ShapeDtypeStruct((chans, strip, 2 * UV), f32),
        in_specs=[vmem, vmem, vmem, vmem, vmem, smem],
        out_specs=vmem,
        scratch_shapes=[
            pltpu.VMEM((LANES, reach), bf16),
            pltpu.VMEM((2 * n_stn * chans * STEP, reach), bf16),
            pltpu.VMEM((2, n_stn, 2, 2, 2, STEP, chans * LANES), bf16),
            pltpu.VMEM((chans, n_stn, st, 2 * LANES), bf16),
            pltpu.VMEM((n_stn * 8, st, LANES), f32),
            pltpu.VMEM((n_stn * 8, TILE * st), bf16),
            pltpu.VMEM((TILE * st, 2 * LANES), bf16),
            pltpu.VMEM((n_stn, 16, LANES), bf16),
            pltpu.VMEM((n_stn, 16, LANES), bf16),
            pltpu.VMEM((chans, 2 * UV, SEPS * PAIR_ROWS), bf16),
            pltpu.VMEM((chans, 2, 2 * LANES, tiles * PATCH), bf16),
            pltpu.VMEM((chans, 2, LANES, tiles * PATCH), bf16),
            pltpu.VMEM((chans, PAIR_ROWS, LANES), f32),
            pltpu.VMEM((full + 48, 2 * LANES), bf16),
            pltpu.VMEM((4 * SEPS * tiles, 2 * LANES), bf16),
            pltpu.VMEM((chans, SEPS * PAIR_ROWS, 2 * UV), bf16),
            pltpu.VMEM((chans, n_grid, strip, 2 * UV), bf16),
            pltpu.VMEM((chans, n_grid, strip, 2 * UV), bf16),
            *[pltpu.VMEM((n_stn, h, LANES), bf16) for h in heights],
            *[pltpu.VMEM((n_stn, h, LANES), bf16) for h in heights],
            *[pltpu.VMEM((n_stn, h, LANES), f32) for h in heights],
            pltpu.SemaphoreType.DMA,
            pltpu.SemaphoreType.DMA,
            pltpu.SemaphoreType.DMA((len(groups), n_stn)),
            pltpu.SemaphoreType.DMA((len(groups), n_stn)),
            pltpu.SemaphoreType.DMA((n_stn,)),
            pltpu.SemaphoreType.DMA((n_stn,)),
            pltpu.SemaphoreType.DMA((chans, n_grid)),
            pltpu.SemaphoreType.DMA((chans, n_grid)),
        ],
        compiler_params=pltpu.CompilerParams(
            collective_id=0, has_side_effects=True, vmem_limit_bytes=48 << 20
        ),
    )(flat, pfb_coeffs, table, station_offsets, tile_cells, kernel_table)
    return jnp.transpose(summed, (1, 0, 2))


def kernels_fit(mesh, args):
    voltages, pfb_coeffs, offsets, cells, _ = args
    n_stn, n_grid = mesh.shape["stn"], mesh.shape["grid"]
    stations, pols, samples = voltages.shape
    taps, frame_len = pfb_coeffs.shape
    spectra = samples // frame_len // n_grid
    return (
        stations == 2 * TILE * n_stn
        and n_stn == 8
        and pols == 2
        and spectra == 64
        and taps == 16
        and frame_len // 2 == cells.shape[0] == 3 * n_stn
    )


def solution(mesh):
    placed = (P("stn", None, "grid"), P(), P(), P("stn", None, None), P())

    def run(*args):
        inner = kernel_body if kernels_fit(mesh, args) else body
        return jax.shard_map(
            inner, mesh=mesh, in_specs=placed, out_specs=P("grid", "stn", None), check_vma=False
        )(*args)

    return run
```

```python
import functools
import math

import jax
import jax.numpy as jnp
import numpy as np
from jax import lax
from jax.experimental import pallas as pl
from jax.experimental.pallas import tpu as pltpu
from jax.sharding import PartitionSpec as P

TILE = 32
PATCH = 16
SPREAD = 5
UV = 128


highest = lax.Precision.HIGHEST


def shifted(block, axis, distance):
    devices = range(lax.axis_size(axis))
    route = [(i - distance, i) for i in devices if i - distance in devices]
    return lax.ppermute(block, axis, route)


def dft_table(frame_len):
    chan_count = frame_len // 2
    sample_line = jnp.arange(frame_len, dtype=jnp.int32)[:, None]
    chan_line = jnp.arange(chan_count, dtype=jnp.int32)[None, :]
    angles = (sample_line * chan_line % frame_len).astype(jnp.float32) * (2.0 * math.pi / frame_len)
    norm_factor = 1.0 / math.sqrt(frame_len)
    twiddle = jnp.stack([jnp.cos(angles) * norm_factor, -jnp.sin(angles) * norm_factor], axis=2)
    return twiddle.reshape(frame_len, 2 * chan_count).astype(jnp.bfloat16)


CLASSES = SPREAD * SPREAD
high = lax.Precision.HIGH


def fused_filter(coeffs, twiddle, step):
    taps, frame_len = coeffs.shape
    flat = coeffs.reshape(-1)
    columns = [
        jnp.pad(flat, (frame_len * (f + 1), frame_len * (step - 1 - f))) for f in range(step)
    ]
    shifted_coeffs = jnp.stack(columns, axis=0)
    spread = np.kron(np.ones((1, frame_len), np.float32), np.eye(step, dtype=np.float32))
    wide = jnp.einsum("fm,fn->mn", shifted_coeffs, jnp.asarray(spread), precision=highest)
    tiled = jnp.tile(jnp.repeat(twiddle.astype(jnp.float32), step, axis=1), (step + taps, 1))
    return (wide * tiled).astype(jnp.bfloat16)

def separation_table(frequency, divisor, kernel_table):
    over_count = kernel_table.shape[0]
    separation = jnp.arange(2 * SPREAD - 1, dtype=jnp.int32)
    scaled = separation * frequency
    cell_index = scaled // divisor
    fine_index = scaled % divisor * over_count // divisor
    choose = (fine_index[:, None] == jnp.arange(over_count, dtype=jnp.int32)[None, :]).astype(
        jnp.float32
    )
    tap_values = jnp.dot(choose, kernel_table, precision=highest)
    place_rel = jnp.arange(PATCH, dtype=jnp.int32)[None, :] - cell_index[:, None]
    weights = jnp.zeros(place_rel.shape, jnp.float32)
    for tap_index in range(kernel_table.shape[1]):
        weights = weights + tap_values[:, tap_index : tap_index + 1] * (
            place_rel == tap_index
        ).astype(jnp.float32)
    return weights


def shifted_weights(weights, bases):
    place = jnp.arange(UV, dtype=jnp.int32)[None, :, None] - bases[:, None, :]
    taps = jnp.arange(PATCH, dtype=jnp.int32)[None, :, None, None]
    spots = place[:, None] == taps
    if weights.dtype == jnp.float32:
        return jnp.einsum("cdt,ctwp->cdwp", weights, spots.astype(jnp.float32), precision=highest)
    return jnp.einsum(
        "cdt,ctwp->cdwp", weights, spots.astype(jnp.bfloat16), preferred_element_type=jnp.float32
    ).astype(jnp.bfloat16)


def body(voltages, pfb_coeffs, station_offsets, tile_cells, kernel_table):
    stn_local, pol_count, samples = voltages.shape
    tap_count, frame_len = pfb_coeffs.shape
    spec_count = samples // frame_len
    step = 128 // math.gcd(128, frame_len)
    chunks = spec_count // step
    flat = jnp.transpose(voltages, (1, 0, 2))
    earlier = shifted(flat[:, :, samples - tap_count * frame_len :], "grid", 1)
    extended = jnp.concatenate([earlier, flat], axis=2)
    width = step * frame_len
    reach = (step + tap_count) * frame_len
    blocks = jnp.stack(
        [extended[:, :, c * width : c * width + reach] for c in range(chunks)], axis=1
    )
    matrix = fused_filter(pfb_coeffs, dft_table(frame_len), step)
    spectra = jnp.einsum(
        "pcsm,mn->npcs", blocks, matrix, preferred_element_type=jnp.float32
    ).astype(jnp.bfloat16)
    spectra = spectra.reshape(frame_len // 2, 2, step * pol_count * chunks, stn_local)
    spectra, tile_cells = lax.optimization_barrier((spectra, tile_cells))
    turned = lax.all_to_all(spectra, "stn", split_axis=0, concat_axis=3, tiled=True)
    turned = jnp.transpose(turned, (0, 1, 3, 2))
    ch_dev, _, stations, depth = turned.shape
    tiles = stations // TILE
    divisor = frame_len - 1
    first_chan = lax.axis_index("stn") * ch_dev + frame_len // 2
    norm_factor = 1.0 / (pol_count * spec_count * lax.axis_size("grid"))

    classes = (station_offsets[0] * SPREAD + station_offsets[1]).reshape(tiles, TILE)
    hot = classes[:, :, None] == jnp.arange(CLASSES, dtype=jnp.int32)
    hot_low = hot.astype(jnp.bfloat16)
    hot_full = hot.astype(jnp.float32)
    tiled = turned.reshape(ch_dev, 2, tiles, TILE, depth)
    summed = jnp.einsum(
        "aiq,ceaik->ceaqk", hot_low, tiled, preferred_element_type=jnp.float32
    ).astype(jnp.bfloat16)

    def stacked(z):
        real_part, imag_part = z[:, 0], z[:, 1]
        partner = jnp.concatenate([real_part, imag_part], axis=-1)
        turned_partner = jnp.concatenate([imag_part, -real_part], axis=-1)
        return jnp.stack([partner, turned_partner], axis=1), partner

    left, right = stacked(summed)
    shape = (SPREAD, SPREAD, 2 * depth)
    terms = []
    for i in range(ch_dev):
        taps = jnp.transpose(left[i].reshape((2 * tiles,) + shape), (1, 2, 3, 0))
        terms.append(
            lax.conv_general_dilated(
                right[i].reshape((tiles,) + shape),
                taps,
                (1, 1),
                [(SPREAD - 1, SPREAD - 1)] * 2,
                dimension_numbers=("NHWC", "HWIO", "HWNC"),
                preferred_element_type=jnp.float32,
            )
        )
    seps = 2 * SPREAD - 1
    cross = jnp.stack(terms).reshape(ch_dev, seps, seps, tiles, 2, tiles)
    cross = jnp.transpose(cross, (0, 4, 1, 2, 3, 5)).reshape(ch_dev, 2, seps, seps, tiles * tiles)
    own_left, own_right = stacked(tiled)
    own = jnp.einsum("ceaik,cajk->ceaij", own_left, own_right, preferred_element_type=jnp.float32)
    line = np.arange(TILE)
    own = jnp.where(jnp.asarray(line[:, None] < line[None, :]), own, 0.0)
    own = jnp.einsum("aiq,ceaij->ceaqj", hot_full, own, precision=high)
    own = jnp.einsum("ceaqj,ajs->ceasq", own, hot_full, precision=high)
    class_line = np.arange(CLASSES)
    back_u = class_line[:, None] // SPREAD - class_line[None, :] // SPREAD + SPREAD - 1
    back_v = class_line[:, None] % SPREAD - class_line[None, :] % SPREAD + SPREAD - 1
    pick = np.arange(seps * seps) == (back_u * seps + back_v).reshape(-1, 1)
    own = jnp.einsum(
        "ceam,mz->ceza",
        own.reshape(ch_dev, 2, tiles, CLASSES * CLASSES),
        jnp.asarray(pick.astype(np.float32)),
        precision=high,
    )
    diagonal = np.zeros((tiles, tiles * tiles), np.float32)
    diagonal[np.arange(tiles), np.arange(tiles) * (tiles + 1)] = 1.0
    own = jnp.einsum("ceza,ap->cezp", own, jnp.asarray(diagonal), precision=high)
    own = own.reshape(ch_dev, 2, seps, seps, tiles * tiles)
    same = jnp.asarray(diagonal.sum(axis=0) > 0)
    cross = jnp.where(same, own, cross)

    pair_first, pair_second = np.triu_indices(tiles)
    select = np.zeros((pair_first.size, tiles * tiles), np.float32)
    select[np.arange(pair_first.size), pair_second * tiles + pair_first] = 1.0
    missing = (1.0 - select.sum(axis=0)).astype(np.int32) * 4096
    cells = jnp.einsum(
        "cxk,kp->cxp", tile_cells.astype(jnp.float32), jnp.asarray(select), precision=highest
    )
    cells = jnp.round(cells).astype(jnp.int32) + jnp.asarray(missing)
    weights = jnp.stack(
        [separation_table(first_chan + i, divisor, kernel_table)[::-1] for i in range(ch_dev)]
    )
    scaled = weights * norm_factor
    coarse = lax.reduce_precision(scaled, 8, 7)
    rest = (scaled - coarse).astype(jnp.bfloat16)
    rows = [shifted_weights(part, cells[:, 0]) for part in (coarse.astype(jnp.bfloat16), rest)]
    place = jnp.arange(UV, dtype=jnp.int32)[None, :, None] - cells[:, 1][:, None, :]
    cols = []
    for v in range(seps):
        placed = jnp.zeros(place.shape, jnp.float32)
        for t in range(PATCH):
            placed = jnp.where(place == t, weights[:, v, t][:, None, None], placed)
        cols.append(placed)
    cols = lax.optimization_barrier(tuple(cols))
    spread_cols = sum(
        cross[:, :, :, v, None, :] * cols[v][:, None, None] for v in range(seps)
    )
    spread_cols = spread_cols.astype(jnp.bfloat16)
    planes = sum(
        jnp.einsum(
            "cdup,cedwp->ucew", part, spread_cols, preferred_element_type=jnp.float32
        )
        for part in rows
    )
    grid_count = lax.axis_size("grid")
    planes = planes.reshape(grid_count, UV // grid_count, ch_dev, 2 * UV).astype(jnp.bfloat16)
    parts = lax.all_to_all(planes, "grid", split_axis=0, concat_axis=0, tiled=True)
    return parts.astype(jnp.float32).sum(axis=0)


f32, bf16, i32 = jnp.float32, jnp.bfloat16, jnp.int32
MESH = pl.DeviceIdType.MESH
SEPS = 2 * SPREAD - 1
STEP = 16
LANES = 128
SUMS = 2 * CLASSES
PAIR_ROWS = 256


def iota(shape, axis):
    return lax.broadcasted_iota(i32, shape, axis)


def ones_where(mask, kind=bf16):
    return jnp.where(mask, 1.0, 0.0).astype(kind)


def dot(a, b):
    return lax.dot_general(a, b, (((1,), (0,)), ((), ())), preferred_element_type=f32)


def dot_nt(a, b):
    return lax.dot_general(a, b, (((1,), (1,)), ((), ())), preferred_element_type=f32)


def split(x):
    top = x.astype(bf16)
    return top, (x - top.astype(f32)).astype(bf16)


def send_order(n):
    return sorted(range(1, n), key=lambda k: abs(2 * k - n))


def padded(rows):
    return -(-rows // 16) * 16


def channels_of(start, stop):
    return range(start // SUMS, (stop - 1) // SUMS + 1)


def whole_kernel(
    dims, groups, v_ref, coef_ref, tw_ref, off_ref, cells_ref, table_ref, out_ref,
    vext, wide, spec, own, vis, left, picks, dsend, drecv_ref,
    bands, vweights, oweights, cols, xs, sums, placed, rs_send, rs_recv, *rest
):
    n_stn, n_grid, chans, taps, frame_len, st = dims
    n_msg = len(groups)
    sends, recvs, flats = rest[:n_msg], rest[n_msg : 2 * n_msg], rest[2 * n_msg : 3 * n_msg]
    (
        halo_send, halo_recv, send_sem, recv_sem, dsend_sem, drecv_sem,
        rs_send_sem, rs_recv_sem,
    ) = rest[3 * n_msg :]
    me, here = lax.axis_index("stn"), lax.axis_index("grid")
    reach = (STEP + taps) * frame_len
    halo = taps * frame_len
    samples = v_ref.shape[1]
    stride = STEP * frame_len
    order = send_order(n_stn)

    barrier = pltpu.get_barrier_semaphore()
    for k in range(1, n_stn):
        pl.semaphore_signal(
            barrier, inc=1, device_id=(lax.rem(me + k, n_stn), here), device_id_type=MESH
        )
    for k in range(1, n_grid):
        pl.semaphore_signal(
            barrier, inc=1, device_id=(me, lax.rem(here + k, n_grid)), device_id_type=MESH
        )

    coef = coef_ref[...]
    line = jnp.concatenate(
        [jnp.zeros((1, frame_len), f32)]
        + [coef[k : k + 1, :] for k in range(taps)]
        + [jnp.zeros((1, reach - (taps + 1) * frame_len), f32)],
        axis=1,
    )
    shifted_line = jnp.concatenate(
        [line if f == 0 else pltpu.roll(line, f * frame_len, 1) for f in range(STEP)], axis=0
    )
    built = set()

    def build(c):
        built.add(c)
        for r in range(2 * n_stn * c, 2 * n_stn * (c + 1)):
            wide[r * STEP : (r + 1) * STEP, :] = (tw_ref[r : r + 1, :] * shifted_line).astype(bf16)

    build(0)

    offs = off_ref[...].astype(f32)
    stations = offs.shape[1]
    cls = jnp.broadcast_to(SPREAD * offs[0:1] + offs[1:2], (16, stations)).astype(bf16)
    kap = jnp.broadcast_to(SEPS * offs[0:1] + offs[1:2], (LANES, stations)).astype(bf16)
    row_of = (stations, LANES)
    mine = ones_where(iota(row_of, 0) == me * st + iota(row_of, 1) % st)
    cls_line = dot(cls, mine)[0:1]
    kap_line = dot(kap[:16], mine)[0:1]
    lane = iota((1, LANES), 1)
    code = (lane % st // TILE).astype(f32) * CLASSES + cls_line

    def class_rows(start, stop):
        lines = iota((padded(stop - start), LANES), 0)
        lines = jnp.where(lines < stop - start, lines + start, -1).astype(f32)
        return jnp.concatenate(
            [ones_where(lines == code + c * SUMS) for c in channels_of(start, stop)], axis=1
        )

    own_rows = ones_where(iota((st, LANES), 0) == iota((st, LANES), 1) % st)

    pl.semaphore_wait(barrier, n_stn + n_grid - 2)

    @pl.when(here < n_grid - 1)
    def _():
        pltpu.make_async_remote_copy(
            src_ref=v_ref.at[:, pl.ds(samples - halo, halo)],
            dst_ref=vext.at[:, pl.ds(0, halo)],
            send_sem=halo_send,
            recv_sem=halo_recv,
            device_id=(me, here + 1),
            device_id_type=MESH,
        ).start()

    vext[:, halo:] = v_ref[:, :stride]
    even = iota((2 * n_stn * STEP, LANES), 1) < st

    def filtered(h, c):
        rows = wide[c * 2 * n_stn * STEP : (c + 1) * 2 * n_stn * STEP, :]
        windows = [
            v_ref[:, t * stride - halo : t * stride - halo + reach] if t else vext[...]
            for t in (2 * h, 2 * h + 1)
        ]
        window = jnp.concatenate(windows, axis=0)
        got = dot_nt(rows, window)
        for t in range(2):
            part = got[:, t * LANES : (t + 1) * LANES]
            for p in range(2):
                only = jnp.where(even if p == 0 else ~even, part, 0.0).astype(bf16)
                spec[h, :, :, p, t, :, c * LANES : (c + 1) * LANES] = only.reshape(
                    n_stn, 2, STEP, LANES
                )

    copies, arrivals = [], [[] for _ in groups]

    passed = set()

    def made(m, send_now):
        h, start, stop = groups[m]
        for c in channels_of(start, stop):
            if c not in built:
                build(c)
            if (h, c) not in passed:
                passed.add((h, c))
                filtered(h, c)
        cs = channels_of(start, stop)
        pick_rows = class_rows(start, stop)
        for k in order + [0]:
            to = lax.rem(me + k, n_stn)
            block = spec[h, to, :, :, :, :, cs[0] * LANES : (cs[-1] + 1) * LANES]
            got = dot_nt(pick_rows, block.reshape(LANES, len(cs) * LANES)).astype(bf16)
            sends[m][to] = got
            if k and send_now:
                sent(m, k)
        recvs[m][me] = sends[m][me]

    def sent(m, k):
        to = lax.rem(me + k, n_stn)
        copy = pltpu.make_async_remote_copy(
            src_ref=sends[m].at[to],
            dst_ref=recvs[m].at[me],
            send_sem=send_sem.at[m, k],
            recv_sem=recv_sem.at[m, k],
            device_id=(to, here),
            device_id_type=MESH,
        )
        copy.start()
        copies.append(copy)
        arrivals[m].append(copy)

    def kept(h):
        for c in range(chans):
            for d in range(0, n_stn, 2):
                block = spec[h, d : d + 2, :, :, :, :, c * LANES : (c + 1) * LANES]
                got = dot_nt(own_rows, block.reshape(2 * LANES, LANES)).astype(bf16)
                for j in range(2):
                    own[c, d + j, :, h * LANES : (h + 1) * LANES] = got[
                        :, j * LANES : (j + 1) * LANES
                    ]

    early = [m for m, group in enumerate(groups) if group[0] == 1]
    late = [m for m, group in enumerate(groups) if group[0] == 0]
    for m in early:
        made(m, True)
    kept(1)

    which = (st, stations)
    kap_col = dot_nt(ones_where(iota(which, 1) == me * st + iota(which, 0)), kap)
    base = kap_col + iota((st, LANES), 1).astype(f32) - (SEPS * (SPREAD - 1) + SPREAD - 1)
    blank = jnp.zeros((TILE, LANES), bf16)
    row_t = iota((TILE, LANES), 0)
    for i in range(TILE):
        for a in range(2):
            at = a * TILE + i
            value = kap_line[0:1, at : at + 1]
            hit = ones_where((base[a * TILE : (a + 1) * TILE] == value) & (row_t > i))
            first = i * st + a * TILE
            picks[first : first + TILE, a * LANES : (a + 1) * LANES] = hit
            picks[first : first + TILE, (1 - a) * LANES : (2 - a) * LANES] = blank

    halo_copy = pltpu.make_async_remote_copy(
        src_ref=v_ref.at[:, pl.ds(samples - halo, halo)],
        dst_ref=vext.at[:, pl.ds(0, halo)],
        send_sem=halo_send,
        recv_sem=halo_recv,
        device_id=(me, lax.rem(here + 1, n_grid)),
        device_id_type=MESH,
    )

    @pl.when(here > 0)
    def _():
        halo_copy.wait_recv()

    @pl.when(here == 0)
    def _():
        vext[:, 0:halo] = jnp.zeros((LANES, halo), bf16)

    for m in late:
        made(m, m == late[0])
    kept(0)

    half = n_stn * 8
    lane2 = iota((st, 2 * LANES), 1)
    flip = jnp.where(lane2 % LANES < LANES // 2, 1.0, -1.0)
    for c in range(chans, 4):
        for d in range(n_stn):
            vis[d * 8 + c * 2 : d * 8 + c * 2 + 2] = jnp.zeros((2, st, LANES), f32)
    for c in range(chans):
        for d in range(n_stn):
            x = own[c, d]
            xf = x.astype(f32)
            turned = jnp.concatenate(
                [
                    pltpu.roll(xf[:, p * LANES : (p + 1) * LANES], LANES // 2, 1)
                    for p in range(2)
                ],
                axis=1,
            )
            both = jnp.concatenate([x, (turned * flip).astype(bf16)], axis=0)
            got = dot_nt(both, jnp.concatenate([x, x], axis=0))
            for e in range(2):
                vis[d * 8 + c * 2 + e] = got[e * st : (e + 1) * st]
    lane3 = iota((half, LANES), 1)
    for k in range(TILE // 2):
        first = jnp.where(lane3 % st < TILE, vis[:, 2 * k, :], vis[:, 2 * k + TILE, :])
        second = jnp.where(lane3 % st < TILE, vis[:, 2 * k + 1, :], vis[:, 2 * k + 1 + TILE, :])
        left[:, k * LANES : (k + 1) * LANES] = jnp.where(lane3 < st, first, second).astype(bf16)
    binned = dot(left[...], picks[...])
    dsend[...] = jnp.concatenate(
        [
            binned[:, a * LANES : (a + 1) * LANES].reshape(n_stn, 8, LANES)
            for a in range(2)
        ],
        axis=1,
    ).astype(bf16)
    own_arrivals = []
    for k in order:
        to = lax.rem(me + k, n_stn)
        copy = pltpu.make_async_remote_copy(
            src_ref=dsend.at[to],
            dst_ref=drecv_ref.at[me],
            send_sem=dsend_sem.at[k],
            recv_sem=drecv_sem.at[k],
            device_id=(to, here),
            device_id_type=MESH,
        )
        copy.start()
        copies.append(copy)
        own_arrivals.append(copy)
    drecv_ref[me] = dsend[me]
    for k in order:
        sent(late[1], k)
    for k in order:
        sent(late[2], k)


    tiles = 2 * n_stn
    over, kern = table_ref.shape
    divisor = frame_len - 1
    side = SPREAD * tiles
    full = SPREAD * side
    depth = 2 * LANES
    across_w = tiles * PATCH
    npair = cells_ref.shape[2]

    def tile_of(x):
        return 2 * (x % n_stn) + x // n_stn

    def pair_number(x):
        b = tile_of(x % tiles)
        last = x // tiles == tiles - 1
        a = jnp.where(last, b, tile_of(x // tiles))
        return jnp.where((a < b) | last, a * tiles - a * (a - 1) // 2 + b - a, -1)

    choose = ones_where(iota((npair, PAIR_ROWS), 0) == pair_number(iota((1, PAIR_ROWS), 1)))
    choose_t = ones_where(iota((PAIR_ROWS, npair), 1) == pair_number(iota((PAIR_ROWS, 1), 0)))
    absent = jnp.where(pair_number(iota((1, PAIR_ROWS), 1)) < 0, -1000.0, 0.0)

    def weight_rows(c, d, r):
        scaled = (d * (me * chans + c + frame_len // 2)).astype(f32)
        cell = jnp.floor((scaled + 0.5) / divisor)
        rest = scaled - cell * divisor
        fine = jnp.floor((rest * over + 0.5) / divisor)
        tap = r - cell.astype(i32)
        code = jnp.where((tap >= 0) & (tap < kern), fine.astype(i32) * kern + tap, -1)
        got = jnp.zeros(code.shape, f32)
        for o in range(over):
            for t in range(kern):
                got = jnp.where(code == o * kern + t, table_ref[o, t], got)
        return got

    xs[full:, :] = jnp.zeros((xs.shape[0] - full, depth), bf16)
    norm = 1.0 / (n_grid * depth // 2)
    rows_t = (16, UV)
    rows_w = (16, across_w)
    same_tile = iota((tiles, across_w), 0) == iota((tiles, across_w), 1) // PATCH
    own_block = iota((LANES, across_w), 0) // SEPS == iota((LANES, across_w), 1) // PATCH
    onto = ones_where(iota((LANES, 16), 0) % SEPS == iota((LANES, 16), 1))
    for c in range(chans):
        cells = cells_ref[c].astype(f32)
        row_line = dot(jnp.broadcast_to(cells[0:1], (16, npair)).astype(bf16), choose)[0:1] + absent
        cols[c] = dot_nt(choose_t, jnp.broadcast_to(cells[1:2], (LANES, npair)).astype(bf16))
        spots = ones_where(iota((UV, PAIR_ROWS), 0).astype(f32) == row_line)
        lines = weight_rows(c, iota(rows_t, 0), (UV - iota(rows_t, 1)) % UV)
        for du in range(SEPS):
            band = pltpu.roll(
                jnp.broadcast_to(lines[du : du + 1], (UV, UV)), 0, 1, stride=1, stride_axis=0
            )
            top, low = split(band)
            bands[c, :, du * PAIR_ROWS : (du + 1) * PAIR_ROWS] = dot(
                jnp.concatenate([top, low], axis=0), spots
            ).astype(bf16)
        across = weight_rows(c, iota(rows_w, 0), iota(rows_w, 1) % PATCH)
        for at in range(SEPS):
            parts = split(jnp.where(same_tile, across[at : at + 1], 0.0))
            for j in range(2):
                vweights[c, j, at * tiles : (at + 1) * tiles, :] = parts[j]
        for j in range(2):
            vweights[c, j, SEPS * tiles :, :] = jnp.zeros((depth - SEPS * tiles, across_w), bf16)
        for j, part in enumerate(split(across)):
            oweights[c, j] = jnp.where(own_block, dot(onto, part), 0.0).astype(bf16)

    ready = set()
    reduced = []
    lane_h = iota((tiles, LANES), 1) < LANES // 2
    rows_p = 2 * SEPS * tiles
    lane_s = iota((side, LANES), 1) < side
    lane_p = iota((tiles, LANES), 1)

    def found(h, g):
        for m, (half, start, stop) in enumerate(groups):
            if half == h and start <= g < stop:
                if m not in ready:
                    ready.add(m)
                    for copy in arrivals[m]:
                        copy.wait_recv()
                    flats[m][...] = recvs[m][...].astype(f32)
                return flats[m][:, g - start, :]

    def moves(c, a):
        distance = iota((tiles, LANES), 1) - cols[c, a * tiles : (a + 1) * tiles].astype(i32)
        valid = (distance >= 0) & (distance < PATCH)
        return valid, jnp.where(valid, distance, 0)

    def correlated(c):
        turned = []
        for q in range(SPREAD * SPREAD):
            pieces = []
            for h in range(2):
                x = jnp.concatenate(
                    [found(h, c * SUMS + a * CLASSES + q) for a in range(2)], axis=0
                )
                xs[q * tiles : (q + 1) * tiles, h * LANES : (h + 1) * LANES] = x.astype(bf16)
                y = pltpu.roll(x, LANES // 2, 1)
                pieces.append(jnp.where(lane_h, -y, y).astype(bf16))
            turned.append(jnp.concatenate(pieces, axis=1))
        lefts = [xs[:full], jnp.concatenate(turned, axis=0)]
        for e in range(2):
            blocks = []
            for q in range(0, SPREAD, 2):
                names = [r for r in (q, q + 1) if r < SPREAD]
                rights = [xs[r * side : r * side + LANES] for r in names]
                got = dot_nt(lefts[e], jnp.concatenate(rights, axis=0))
                blocks += [got[:, j * LANES : (j + 1) * LANES] for j in range(len(names))]
            for du in range(SEPS):
                d = du - (SPREAD - 1)
                total = sum(
                    blocks[s + d][s * side : (s + 1) * side]
                    for s in range(SPREAD)
                    if 0 <= s + d < SPREAD
                )
                total = jnp.where(lane_s, total, 0.0)
                shifts = [
                    pltpu.roll(
                        total[x * tiles : (x + 1) * tiles], (SPREAD - 1 - x) * tiles, 1
                    )
                    for x in range(SPREAD - 1)
                ]
                wrap = (2 * SPREAD - 1) * tiles - LANES
                main = total[(SPREAD - 1) * tiles :] + jnp.where(lane_p < wrap, 0.0, shifts[0])
                for part in shifts[1:]:
                    main = main + part
                over_part = jnp.where(lane_p < wrap, shifts[0], 0.0)
                top, low = split(jnp.concatenate([main, over_part], axis=1))
                at = (e * SEPS + du) * tiles
                sums[at : at + tiles, :] = top
                sums[rows_p + at : rows_p + at + tiles, :] = low
        patches = dot(sums[...], vweights[c, 0])
        patches = patches[:rows_p] + patches[rows_p:] + dot(sums[:rows_p], vweights[c, 1])

        for a in range(tiles - 1):
            valid, index = moves(c, a)
            index = index + (a % 8) * PATCH
            for du in range(SEPS):
                for e in range(2):
                    at = (e * SEPS + du) * tiles
                    source = patches[at : at + tiles, a // 8 * LANES : (a // 8 + 1) * LANES]
                    moved = jnp.where(valid, jnp.take_along_axis(source, index, axis=1), 0.0)
                    first = du * PAIR_ROWS + a * tiles
                    placed[c, first : first + tiles, e * LANES : (e + 1) * LANES] = moved.astype(
                        bf16
                    )

    def alone_placed(c):
        rr, cc = iota((32, n_stn * 16), 0), iota((32, n_stn * 16), 1)
        b = rr % tiles
        take = ones_where(cc == (b % n_stn) * 16 + (b // n_stn) * 8 + c * 2 + rr // tiles)
        alone = dot(take, drecv_ref[...].reshape(n_stn * 16, LANES)).astype(bf16)
        alone = dot(alone, oweights[c, 0]) + dot(alone, oweights[c, 1])
        valid, index = moves(c, tiles - 1)
        for du in range(SEPS):
            for e in range(2):
                source = alone[e * tiles : (e + 1) * tiles, du // 8 * LANES : (du // 8 + 1) * LANES]
                moved = jnp.take_along_axis(source, index + (du % 8) * PATCH, axis=1)
                first = du * PAIR_ROWS + (tiles - 1) * tiles
                placed[c, first : first + tiles, e * LANES : (e + 1) * LANES] = jnp.where(
                    valid, moved, 0.0
                ).astype(bf16)

    def gridded(c):
        plane = dot(bands[c], placed[c])
        plane = (plane[:UV] + plane[UV:]) * norm
        rs_send[c] = plane.astype(bf16).reshape(n_grid, UV // n_grid, 2 * UV)
        for k in range(1, n_grid):
            to = lax.rem(here + k, n_grid)
            copy = pltpu.make_async_remote_copy(
                src_ref=rs_send.at[c, to],
                dst_ref=rs_recv.at[c, k],
                send_sem=rs_send_sem.at[c, k],
                recv_sem=rs_recv_sem.at[c, k],
                device_id=(me, to),
                device_id_type=MESH,
            )
            copy.start()
            reduced.append(copy)

    for c in range(chans):
        correlated(c)
        if c == 0:
            for copy in own_arrivals:
                copy.wait_recv()
            for other in range(chans):
                alone_placed(other)
        gridded(c)

    for c in range(chans):
        total = rs_send[c, here].astype(f32)
        for k in range(1, n_grid):
            reduced[c * (n_grid - 1) + k - 1].wait_recv()
            total = total + rs_recv[c, k].astype(f32)
        out_ref[:, c, :] = total
    for copy in copies + reduced:
        copy.wait_send()

    @pl.when(here < n_grid - 1)
    def _():
        halo_copy.wait_send()


def kernel_body(voltages, pfb_coeffs, station_offsets, tile_cells, kernel_table):
    st, pols, samples = voltages.shape
    taps, frame_len = pfb_coeffs.shape
    n_stn, n_grid = lax.axis_size("stn"), lax.axis_size("grid")
    chans = tile_cells.shape[0]
    dims = (n_stn, n_grid, chans, taps, frame_len, st)
    reach = (STEP + taps) * frame_len
    whole, first = chans * SUMS, padded(SUMS)
    second = first + padded(2 * SUMS - first)
    third = SUMS // 16 * 16
    groups = (
        (1, 0, third), (1, third, whole), (0, 0, first), (0, first, second), (0, second, whole),
    )

    line = np.arange(frame_len)[:, None] * np.arange(frame_len // 2)[None, :] % frame_len
    angles = line.astype(np.float32) * np.float32(2.0 * math.pi / frame_len)
    scale = np.float32(1.0 / math.sqrt(frame_len))
    table = np.stack([np.cos(angles) * scale, -np.sin(angles) * scale], axis=2)
    table = table.astype(jnp.bfloat16).astype(np.float32)
    table = table.transpose(1, 2, 0).reshape(n_stn, chans, 2, frame_len).transpose(1, 0, 2, 3)
    table = jnp.asarray(np.tile(table.reshape(-1, frame_len), (1, STEP + taps)))
    vmem = pl.BlockSpec(memory_space=pltpu.VMEM)
    smem = pl.BlockSpec(memory_space=pltpu.SMEM)
    flat = jnp.transpose(voltages, (1, 0, 2)).reshape(pols * st, samples)
    tiles = 2 * n_stn
    full = SPREAD * SPREAD * tiles
    strip = UV // n_grid
    heights = [padded(stop - start) for _, start, stop in groups]
    summed = pl.pallas_call(
        functools.partial(whole_kernel, dims, groups),
        out_shape=jax.ShapeDtypeStruct((strip, chans, 2 * UV), f32),
        in_specs=[vmem, vmem, vmem, vmem, vmem, smem],
        out_specs=vmem,
        scratch_shapes=[
            pltpu.VMEM((LANES, reach), bf16),
            pltpu.VMEM((2 * n_stn * chans * STEP, reach), bf16),
            pltpu.VMEM((2, n_stn, 2, 2, 2, STEP, chans * LANES), bf16),
            pltpu.VMEM((chans, n_stn, st, 2 * LANES), bf16),
            pltpu.VMEM((n_stn * 8, st, LANES), f32),
            pltpu.VMEM((n_stn * 8, TILE * st), bf16),
            pltpu.VMEM((TILE * st, 2 * LANES), bf16),
            pltpu.VMEM((n_stn, 16, LANES), bf16),
            pltpu.VMEM((n_stn, 16, LANES), bf16),
            pltpu.VMEM((chans, 2 * UV, SEPS * PAIR_ROWS), bf16),
            pltpu.VMEM((chans, 2, 2 * LANES, tiles * PATCH), bf16),
            pltpu.VMEM((chans, 2, LANES, tiles * PATCH), bf16),
            pltpu.VMEM((chans, PAIR_ROWS, LANES), f32),
            pltpu.VMEM((full + 48, 2 * LANES), bf16),
            pltpu.VMEM((4 * SEPS * tiles, 2 * LANES), bf16),
            pltpu.VMEM((chans, SEPS * PAIR_ROWS, 2 * UV), bf16),
            pltpu.VMEM((chans, n_grid, strip, 2 * UV), bf16),
            pltpu.VMEM((chans, n_grid, strip, 2 * UV), bf16),
            *[pltpu.VMEM((n_stn, h, LANES), bf16) for h in heights],
            *[pltpu.VMEM((n_stn, h, LANES), bf16) for h in heights],
            *[pltpu.VMEM((n_stn, h, LANES), f32) for h in heights],
            pltpu.SemaphoreType.DMA,
            pltpu.SemaphoreType.DMA,
            pltpu.SemaphoreType.DMA((len(groups), n_stn)),
            pltpu.SemaphoreType.DMA((len(groups), n_stn)),
            pltpu.SemaphoreType.DMA((n_stn,)),
            pltpu.SemaphoreType.DMA((n_stn,)),
            pltpu.SemaphoreType.DMA((chans, n_grid)),
            pltpu.SemaphoreType.DMA((chans, n_grid)),
        ],
        compiler_params=pltpu.CompilerParams(
            collective_id=0, has_side_effects=True, vmem_limit_bytes=48 << 20
        ),
    )(flat, pfb_coeffs, table, station_offsets, tile_cells, kernel_table)
    return summed


def kernels_fit(mesh, args):
    voltages, pfb_coeffs, offsets, cells, _ = args
    n_stn, n_grid = mesh.shape["stn"], mesh.shape["grid"]
    stations, pols, samples = voltages.shape
    taps, frame_len = pfb_coeffs.shape
    spectra = samples // frame_len // n_grid
    return (
        stations == 2 * TILE * n_stn
        and n_stn == 8
        and pols == 2
        and spectra == 64
        and taps == 16
        and frame_len // 2 == cells.shape[0] == 3 * n_stn
    )


def solution(mesh):
    placed = (P("stn", None, "grid"), P(), P(), P("stn", None, None), P())

    def run(*args):
        inner = kernel_body if kernels_fit(mesh, args) else body
        return jax.shard_map(
            inner, mesh=mesh, in_specs=placed, out_specs=P("grid", "stn", None), check_vma=False
        )(*args)

    return run
```
